256 devices in a mesh: ty: 16 (over y, z_hi), tx: 16 (over z_lo, x, core).
Axes of the slice: x: 4, y: 4, z: 8 (z_hi: 4, z_lo: 2; z = z_hi * 2 + z_lo), core: 2. Of those that a mesh axis runs over, the one named last changes fastest.
Arguments:
- specimen: float32 [2, 8192, 8192], P(None, 'ty', 'tx'), may hold values from -5 to 5
- illumination: float32 [2, 256, 256], replicated, may hold values from -6 to 6
- scan_offsets: int32 [16, 16, 2, 16], P('ty', 'tx'), may hold values from 0 to 7936, as said below
- slot_counts: int32 [16, 16], P('ty', 'tx'), may hold values from 1 to 16, as said below
- measured: float32 [16, 16, 16, 256, 256], P('ty', 'tx'), may hold values from 0.2 to 3
Outputs:
- new_specimen: float32 [2, 8192, 8192], P(None, 'ty', 'tx')
- new_illumination: float32 [2, 256, 256], replicated
The draws below stay inside these ranges and needn't reach their ends.
Inputs may be any that keep to these rules, and one draw needn't show every extreme that they name: `scan_offsets`: the row of slot s of tile (a, b) lies in [a * 512 - 256 / 2, a * 512 + 512 - 256 / 2) and in [0, 7936]; the column lies in [b * 512 - 256 / 2, b * 512 + 512 - 256 / 2) and in [0, 7936]. Dead slots hold valid offsets too. Only the first slot_counts[a, b] slots of tile (a, b) are live. Some tile has all 16 slots live in every draw.
All inputs are finite; a program needn't handle non-finite values.
Results may differ from the reference program's by a relative error of at most 0.00016.
Values sent between devices are 32-bit elements; how exact they have to be, the bound alone decides.
A program may use at most 128 MiB of HBM per device.

```python
import math
import jax
import jax.numpy as jnp
from jax import lax

P_SIZE = 256
TH = 512
TW = 512
CAP = 16
NY = 8192
NX = 8192
N_TY = 16
N_TX = 16


def draw_scan_offsets(key, part):
    key = jax.random.fold_in(key, 11)
    row_key, col_key = jax.random.split(key)
    tile_row = jnp.arange(N_TY, dtype=jnp.int32)[:, None, None] * TH - P_SIZE // 2
    tile_col = jnp.arange(N_TX, dtype=jnp.int32)[None, :, None] * TW - P_SIZE // 2
    row_draw = jax.random.randint(row_key, (N_TY, N_TX, CAP), 0, TH, dtype=jnp.int32)
    col_draw = jax.random.randint(col_key, (N_TY, N_TX, CAP), 0, TW, dtype=jnp.int32)
    row_values = jnp.clip(tile_row + row_draw, 0, N_TY * TH - P_SIZE)
    col_values = jnp.clip(tile_col + col_draw, 0, N_TX * TW - P_SIZE)
    return jnp.stack([row_values, col_values], axis=2).astype(jnp.int32)


def draw_slot_counts(key, part):
    key = jax.random.fold_in(key, 23)
    first_key, second_key, chosen_key = jax.random.split(key, 3)
    first_factor = jax.random.randint(first_key, (N_TY, N_TX), 0, CAP, dtype=jnp.int32)
    second_factor = jax.random.randint(second_key, (N_TY, N_TX), 0, CAP, dtype=jnp.int32)
    base_counts = 1 + first_factor * second_factor // CAP
    chosen_tile = jax.random.randint(chosen_key, (), 0, N_TY * N_TX, dtype=jnp.int32)
    tile_numbers = jnp.arange(N_TY * N_TX, dtype=jnp.int32).reshape(N_TY, N_TX)
    return jnp.where(tile_numbers == chosen_tile, CAP, base_counts).astype(jnp.int32)


def block_scale(stream_key, extent, shards, smallest, top_value):
    gain, own = 1.0, jax.random.fold_in(stream_key, 6)
    for axis_at, shards_of in shards:
        draws = jnp.exp(jax.random.uniform(jax.random.fold_in(own, axis_at), (shards_of,), jnp.float32, smallest / len(shards), top_value / len(shards)))
        gain = gain * jnp.repeat(draws, extent[axis_at] // shards_of).reshape([-1 if axis == axis_at else 1 for axis in range(len(extent))])
    return gain


def scatter_about(own_key, extent, width, bound, cuts=(), held_as=jnp.bfloat16):
    values = width * jax.random.normal(own_key, extent, jnp.float32)
    if cuts:
        values = values * block_scale(own_key, extent, cuts, -0.22, 0.18)
    return jnp.clip(values, -bound, bound).astype(held_as)


def setup_inputs(seed: int = 0) -> dict:
    streams_of = jax.random.split(jax.random.key(seed), 6)
    return {
        "specimen": scatter_about(streams_of[0], (2, NY, NX), 0.7, 5.0, ((1, 16), (2, 16)), jnp.float32),
        "illumination": scatter_about(streams_of[1], (2, P_SIZE, P_SIZE), 1.0, 6.0, (), jnp.float32),
        "scan_offsets": draw_scan_offsets(jax.random.fold_in(streams_of[5], 71), 0),
        "slot_counts": draw_slot_counts(jax.random.fold_in(streams_of[5], 71), 0),
        "measured": jnp.clip(0.2 + 2.8 * jax.random.uniform(streams_of[4], (N_TY, N_TX, CAP, P_SIZE, P_SIZE), jnp.float32) ** block_scale(streams_of[4], (N_TY, N_TX, CAP, P_SIZE, P_SIZE), ((0, 16), (1, 16)), -0.2, 0.2), 0.2, 3.0),
    }


FLOOR = 0.5

def reference(specimen, illumination, scan_offsets, slot_counts, measured):
    total_slots = CAP * N_TY * N_TX
    row_starts = scan_offsets[:, :, 0, :].reshape(-1).astype(jnp.int32)
    col_starts = scan_offsets[:, :, 1, :].reshape(-1).astype(jnp.int32)
    slot_numbers = jnp.arange(CAP, dtype=jnp.int32)
    alive = (slot_numbers[None, None, :] < slot_counts[:, :, None]).reshape(-1)
    flags = alive.astype(specimen.dtype)
    moduli = measured.reshape(total_slots, P_SIZE, P_SIZE)
    probe_field = illumination[0] + 1j * illumination[1]
    object_field = specimen[0] + 1j * specimen[1]

    def visit_slot(carry, item):
        gradient, probe_term = carry
        row_start, col_start, modulus, flag = item
        patch = lax.dynamic_slice(object_field, (row_start, col_start), (P_SIZE, P_SIZE))
        wave = probe_field * patch
        far = jnp.fft.fft2(wave, norm='ortho')
        projected = modulus * far / jnp.maximum(jnp.abs(far), FLOOR)
        correction = (jnp.fft.ifft2(projected, norm='ortho') - wave) * flag
        existing = lax.dynamic_slice(gradient, (row_start, col_start), (P_SIZE, P_SIZE))
        gradient = lax.dynamic_update_slice(gradient, existing + jnp.conj(probe_field) * correction, (row_start, col_start))
        probe_term = probe_term + jnp.conj(patch) * correction
        return ((gradient, probe_term), None)
    start_carry = (jnp.zeros_like(object_field), jnp.zeros_like(probe_field))
    (gradient, probe_term), unused = lax.scan(visit_slot, start_carry, (row_starts, col_starts, moduli, flags))
    probe_power = jnp.mean(illumination[0] * illumination[0] + illumination[1] * illumination[1]) + 1e-05
    new_object = object_field + gradient / probe_power
    new_probe = probe_field + probe_term / math.sqrt(total_slots)
    new_specimen = jnp.stack([jnp.real(new_object), jnp.imag(new_object)])
    new_illumination = jnp.stack([jnp.real(new_probe), jnp.imag(new_probe)])
    return (new_specimen, new_illumination)
```

```python
import math

import numpy as np
import jax, jax.numpy as jnp
from jax import lax
from jax.experimental import pallas as pl
from jax.experimental.pallas import tpu as pltpu
import ml_dtypes
from jax.sharding import PartitionSpec as P

F32=jnp.float32; BF=jnp.bfloat16

def consts():
    k=np.arange(128)
    ang=2*np.pi*np.outer(k,k)%(2*np.pi*128)/128
    ang=2*np.pi*((np.outer(k,k))%128)/128
    C=np.cos(ang)/16; S=np.sin(ang)/16
    A=np.block([[C,-S],[S,C]]); B=A.T.copy()
    def split(x):
        x=x.astype(np.float32)
        h=x.astype(ml_dtypes.bfloat16); l=(x-h.astype(np.float32)).astype(ml_dtypes.bfloat16)
        return h,l
    ah,al=split(A); bh,bl=split(B)
    mats=np.stack([ah,al,bh,bl])
    t=2*np.pi*np.arange(128)/256
    c=np.cos(t).astype(np.float32); s=np.sin(t).astype(np.float32)
    twr=np.stack([np.broadcast_to(c[:,None],(128,128)),np.broadcast_to(s[:,None],(128,128))])
    twl=np.stack([np.broadcast_to(c[None],(16,128)),np.broadcast_to(s[None],(16,128))])
    k=np.arange(256)
    perm=np.zeros((256,256));
    perm[k, (k%2)*128+k//2]=1
    return mats, twr.astype(np.float32).copy(), twl.astype(np.float32).copy(), perm.astype(ml_dtypes.bfloat16)

def split(x):
    h=x.astype(BF)
    return h,(x-h.astype(F32)).astype(BF)

def dot(a,b): return jnp.dot(a,b,preferred_element_type=F32)

RC=16
def wkernel(offs, cnt, ext, ill, mats, twr, twl, perm, meas, grad, pterm,
            mbuf, patch, wave, hi, lo, mid, msem):
    n=cnt[0]
    def cp(s,t): return pltpu.make_async_copy(meas.at[s,:,pl.ds(128*t,128)], mbuf.at[s,t], msem.at[s,t])
    @pl.loop(0,n)
    def _(s):
        cp(s,0).start(); cp(s,1).start()
    @pl.loop(0,96)
    def _(i):
        for p in range(2):
            for t in range(6):
                grad[p,t,pl.ds(pl.multiple_of(8*i,8),8),:]=jnp.zeros((8,128),F32)
    pterm[...]=jnp.zeros_like(pterm)
    lane=lax.broadcasted_iota(jnp.int32,(RC,128),1)
    @pl.loop(0,n)
    def _(s):
        r=offs[0,s]; c=offs[1,s]
        ct=c//128; sh=c%128
        ush=(128-sh)%128
        lmask=lane<128-sh
        for j in range(128//RC):
            half=[]
            for h in range(2):
                row=h*128+j*RC
                rr=pl.ds(row,RC)
                x=[[pltpu.roll(ext[p,ct+t,pl.ds(r+row,RC),:],ush,1) for t in range(3)] for p in range(2)]
                pt=[[jnp.where(lmask,x[p][t],x[p][t+1]) for t in range(2)] for p in range(2)]
                ws=[]
                for t in range(2):
                    ls=pl.ds(128*t,128)
                    pr,pi=ill[0,rr,ls],ill[1,rr,ls]
                    a,b=pt[0][t],pt[1][t]
                    patch[0,rr,ls]=a; patch[1,rr,ls]=b
                    wr=pr*a-pi*b; wi=pr*b+pi*a
                    wave[0,rr,ls]=wr; wave[1,rr,ls]=wi
                    ws.append((wr,wi))
                half.append(ws)
            tc=twr[0,pl.ds(j*RC,RC),:]; ts=twr[1,pl.ds(j*RC,RC),:]
            for t in range(2):
                ls=pl.ds(128*t,128)
                (ar,ai),(br,bi)=half[0][t],half[1][t]
                er,ei=ar+br,ai+bi
                dr,di=ar-br,ai-bi
                vr=dr*tc+di*ts; vi=di*tc-dr*ts
                for q,(xr,xi) in enumerate(((er,ei),(vr,vi))):
                    for z,val in enumerate((xr,xi)):
                        hh,ll=split(val)
                        rs=pl.ds(z*128+j*RC,RC)
                        hi[q,rs,ls]=hh; lo[q,rs,ls]=ll
        bh=mats[2]; bl=mats[3]
        for q in range(2):
            mid[q]=dot(bh,hi[q])+dot(bh,lo[q])+dot(bl,hi[q])
        lc=twl[0]; lsn=twl[1]
        for q in range(2):
            for j in range(128//RC):
                ar=mid[q,pl.ds(j*RC,RC),pl.ds(0,128)]; br=mid[q,pl.ds(j*RC,RC),pl.ds(128,128)]
                ai=mid[q,pl.ds(128+j*RC,RC),pl.ds(0,128)]; bi=mid[q,pl.ds(128+j*RC,RC),pl.ds(128,128)]
                er,ei=ar+br,ai+bi
                dr,di=ar-br,ai-bi
                vr=dr*lc+di*lsn; vi=di*lc-dr*lsn
                rs=pl.ds(q*128+j*RC,RC)
                for e,(xr,xi) in enumerate(((er,ei),(vr,vi))):
                    for z,val in enumerate((xr,xi)):
                        hh,ll=split(val)
                        hi[e,rs,pl.ds(128*z,128)]=hh; lo[e,rs,pl.ds(128*z,128)]=ll
        ah=mats[0]; al=mats[1]
        for e in range(2):
            mid[e]=dot(hi[e],ah)+dot(lo[e],ah)+dot(hi[e],al)
        cp(s,0).wait(); cp(s,1).wait()
        pm=perm[...]
        for q in range(2):
            mv=jnp.concatenate([mbuf[s,t,pl.ds(q,128,stride=2),:] for t in range(2)],axis=1)
            mh,ml=split(mv)
            mp=dot(mh,pm)+dot(ml,pm)
            for e in range(2):
                for j in range(128//RC):
                    rs=pl.ds(q*128+j*RC,RC)
                    fr=mid[e,rs,pl.ds(0,128)]; fi=mid[e,rs,pl.ds(128,128)]
                    m=mp[j*RC:(j+1)*RC,e*128:(e+1)*128]
                    f=m*lax.rsqrt(jnp.maximum(fr*fr+fi*fi,0.25))
                    for z,val in enumerate((fr*f,fi*f)):
                        hh,ll=split(val)
                        hi[e,rs,pl.ds(128*z,128)]=hh; lo[e,rs,pl.ds(128*z,128)]=ll
        for e in range(2):
            mid[e]=dot(hi[e],bh)+dot(lo[e],bh)+dot(hi[e],bl)
        for q in range(2):
            for j in range(128//RC):
                rs=pl.ds(q*128+j*RC,RC)
                er=mid[0,rs,pl.ds(0,128)]; ei=mid[0,rs,pl.ds(128,128)]
                orr=mid[1,rs,pl.ds(0,128)]; oi=mid[1,rs,pl.ds(128,128)]
                vr=orr*lc-oi*lsn; vi=oi*lc+orr*lsn
                for t,(xr,xi) in enumerate(((er+vr,ei+vi),(er-vr,ei-vi))):
                    for z,val in enumerate((xr,xi)):
                        hh,ll=split(val)
                        hi[q,pl.ds(z*128+j*RC,RC),pl.ds(128*t,128)]=hh
                        lo[q,pl.ds(z*128+j*RC,RC),pl.ds(128*t,128)]=ll
        for q in range(2):
            mid[q]=dot(ah,hi[q])+dot(ah,lo[q])+dot(al,hi[q])
        for j in range(128//RC):
            tc=twr[0,pl.ds(j*RC,RC),:]; ts=twr[1,pl.ds(j*RC,RC),:]
            g=[[[None]*2 for _ in range(2)] for _ in range(2)]
            for t in range(2):
                ls=pl.ds(128*t,128)
                er=mid[0,pl.ds(j*RC,RC),ls]; ei=mid[0,pl.ds(128+j*RC,RC),ls]
                orr=mid[1,pl.ds(j*RC,RC),ls]; oi=mid[1,pl.ds(128+j*RC,RC),ls]
                vr=orr*tc-oi*ts; vi=oi*tc+orr*ts
                for h,(xr,xi) in enumerate(((er+vr,ei+vi),(er-vr,ei-vi))):
                    rr=pl.ds(h*128+j*RC,RC)
                    cr=xr-wave[0,rr,ls]; ci=xi-wave[1,rr,ls]
                    a,b=patch[0,rr,ls],patch[1,rr,ls]
                    pterm[0,rr,ls]+=a*cr+b*ci
                    pterm[1,rr,ls]+=a*ci-b*cr
                    pr,pi=ill[0,rr,ls],ill[1,rr,ls]
                    g[h][0][t]=pr*cr+pi*ci
                    g[h][1][t]=pr*ci-pi*cr
            for h in range(2):
                for z in range(2):
                    rg=[pltpu.roll(g[h][z][t],sh,1) for t in range(2)]
                    low=lane<sh
                    rows=pl.ds(r+h*128+j*RC,RC)
                    grad[z,ct,rows,:]+=jnp.where(low,0.0,rg[0])
                    grad[z,ct+1,rows,:]+=jnp.where(low,rg[0],rg[1])
                    grad[z,ct+2,rows,:]+=jnp.where(low,rg[1],0.0)

def windows(offs,cnt,ext,ill,meas):
    mats,twr,twl,perm=consts()
    V=pl.BlockSpec(memory_space=pltpu.VMEM); Sm=pl.BlockSpec(memory_space=pltpu.SMEM)
    return pl.pallas_call(wkernel,
        out_shape=(jax.ShapeDtypeStruct((2,6,768,128),F32),jax.ShapeDtypeStruct((2,256,256),F32)),
        in_specs=[Sm,Sm,V,V,V,V,V,V,pl.BlockSpec(memory_space=pl.ANY)],
        out_specs=(V,V),
        scratch_shapes=[pltpu.VMEM((16,2,256,128),F32),pltpu.VMEM((2,256,256),F32),pltpu.VMEM((2,256,256),F32),
            pltpu.VMEM((2,256,256),BF),pltpu.VMEM((2,256,256),BF),pltpu.VMEM((2,256,256),F32),pltpu.SemaphoreType.DMA((16,2))],
        compiler_params=pltpu.CompilerParams(vmem_limit_bytes=48*2**20),
    )(offs,cnt,ext,ill,jnp.asarray(mats),jnp.asarray(twr),jnp.asarray(twl),jnp.asarray(perm),meas)


def padded(cells, sides, width):
    for axis, dim in sides:
        count = lax.axis_size(axis)
        ends = count - 1
        head = lax.slice_in_dim(cells, 0, width, axis=dim)
        tail = lax.slice_in_dim(cells, cells.shape[dim] - width, cells.shape[dim], axis=dim)
        cells = jnp.concatenate(
            [
                lax.ppermute(tail, axis, [(i, (i + 1) % count) for i in range(ends)]),
                cells,
                lax.ppermute(head, axis, [((i + 1) % count, i) for i in range(ends)]),
            ],
            axis=dim,
        )
    return cells


def shards(specimen, illumination, scan_offsets, slot_counts, measured):
    tile_rows = specimen.shape[1]
    tile_cols = specimen.shape[2]
    margin = 128
    slot_count = measured.shape[2]
    anchor = jnp.stack([lax.axis_index("ty") * tile_rows, lax.axis_index("tx") * tile_cols]) - margin
    local = scan_offsets[0, 0] - anchor[:, None]
    extended = padded(specimen, (("ty", 1), ("tx", 2)), margin)
    ext = extended.reshape(2, 768, 6, 128).transpose(0, 2, 1, 3)
    grad, probe_term = windows(local, slot_counts[0], ext, illumination, measured[0, 0])
    gradient = grad.transpose(0, 2, 1, 3).reshape(2, 768, 768)
    folded = padded(gradient, (("ty", 1), ("tx", 2)), margin)
    row_folded = folded[:, 2 * margin : 2 * margin + tile_rows, :]
    row_folded = row_folded.at[:, :margin, :].add(folded[:, :margin, :])
    row_folded = row_folded.at[:, tile_rows - margin :, :].add(
        folded[:, tile_rows + 3 * margin :, :]
    )
    update_field = row_folded[:, :, 2 * margin : 2 * margin + tile_cols]
    update_field = update_field.at[:, :, :margin].add(row_folded[:, :, :margin])
    update_field = update_field.at[:, :, tile_cols - margin :].add(
        row_folded[:, :, tile_cols + 3 * margin :]
    )
    probe_power = (
        jnp.mean(illumination[0] * illumination[0] + illumination[1] * illumination[1]) + 1e-05
    )
    new_specimen = specimen + update_field / probe_power
    summed_term = lax.psum(probe_term, ("ty", "tx"))
    total_slots = slot_count * lax.axis_size("ty") * lax.axis_size("tx")
    new_illumination = illumination + summed_term / math.sqrt(total_slots)
    return (new_specimen, new_illumination)

def solution(mesh):
    in_specs = (
        P(None, "ty", "tx"),
        P(),
        P("ty", "tx", None, None),
        P("ty", "tx"),
        P("ty", "tx", None, None, None),
    )
    out_specs = (P(None, "ty", "tx"), P())
    return jax.shard_map(shards, mesh=mesh, in_specs=in_specs, out_specs=out_specs, check_vma=False)
```

```python
import math

import numpy as np
import jax, jax.numpy as jnp
from jax import lax
from jax.experimental import pallas as pl
from jax.experimental.pallas import tpu as pltpu
import ml_dtypes
from jax.sharding import PartitionSpec as P

F32=jnp.float32; BF=jnp.bfloat16

def consts():
    k=np.arange(128)
    ang=2*np.pi*np.outer(k,k)%(2*np.pi*128)/128
    ang=2*np.pi*((np.outer(k,k))%128)/128
    C=np.cos(ang)/16; S=np.sin(ang)/16
    A=np.block([[C,-S],[S,C]]); B=A.T.copy()
    def split(x):
        x=x.astype(np.float32)
        h=x.astype(ml_dtypes.bfloat16); l=(x-h.astype(np.float32)).astype(ml_dtypes.bfloat16)
        return h,l
    ah,al=split(A); bh,bl=split(B)
    mats=np.stack([ah,al,bh,bl])
    t=2*np.pi*np.arange(128)/256
    c=np.cos(t).astype(np.float32); s=np.sin(t).astype(np.float32)
    twr=np.stack([np.broadcast_to(c[:,None],(128,128)),np.broadcast_to(s[:,None],(128,128))])
    twl=np.stack([np.broadcast_to(c[None],(16,128)),np.broadcast_to(s[None],(16,128))])
    k=np.arange(256)
    perm=np.zeros((256,256));
    perm[k, (k%2)*128+k//2]=1
    return mats, twr.astype(np.float32).copy(), twl.astype(np.float32).copy(), perm.astype(ml_dtypes.bfloat16)

def split(x):
    h=x.astype(BF)
    return h,(x-h.astype(F32)).astype(BF)

def dot(a,b): return jnp.dot(a,b,preferred_element_type=F32)

RC=16
def wkernel(offs, cnt, ext, ill, mats, twr, twl, perm, meas, grad, pterm,
            mbuf, patch, wave, hi, lo, mid, msem):
    n=cnt[0]
    def cp(s,t): return pltpu.make_async_copy(meas.at[s,:,pl.ds(128*t,128)], mbuf.at[s,t], msem.at[s,t])
    @pl.loop(0,n)
    def _(s):
        cp(s,0).start(); cp(s,1).start()
    @pl.loop(0,96)
    def _(i):
        for p in range(2):
            for t in range(6):
                grad[p,t,pl.ds(pl.multiple_of(8*i,8),8),:]=jnp.zeros((8,128),F32)
    pterm[...]=jnp.zeros_like(pterm)
    lane=lax.broadcasted_iota(jnp.int32,(RC,128),1)
    @pl.loop(0,n)
    def _(s):
        r=offs[0,s]; c=offs[1,s]
        ct=c//128; sh=c%128
        ush=(128-sh)%128
        lmask=lane<128-sh
        for j in range(128//RC):
            half=[]
            for h in range(2):
                row=h*128+j*RC
                rr=pl.ds(row,RC)
                x=[[pltpu.roll(ext[p,ct+t,pl.ds(r+row,RC),:],ush,1) for t in range(3)] for p in range(2)]
                pt=[[jnp.where(lmask,x[p][t],x[p][t+1]) for t in range(2)] for p in range(2)]
                ws=[]
                for t in range(2):
                    ls=pl.ds(128*t,128)
                    pr,pi=ill[0,rr,ls],ill[1,rr,ls]
                    a,b=pt[0][t],pt[1][t]
                    patch[0,rr,ls]=a; patch[1,rr,ls]=b
                    wr=pr*a-pi*b; wi=pr*b+pi*a
                    wave[0,rr,ls]=wr; wave[1,rr,ls]=wi
                    ws.append((wr,wi))
                half.append(ws)
            tc=twr[0,pl.ds(j*RC,RC),:]; ts=twr[1,pl.ds(j*RC,RC),:]
            for t in range(2):
                ls=pl.ds(128*t,128)
                (ar,ai),(br,bi)=half[0][t],half[1][t]
                er,ei=ar+br,ai+bi
                dr,di=ar-br,ai-bi
                vr=dr*tc+di*ts; vi=di*tc-dr*ts
                for q,(xr,xi) in enumerate(((er,ei),(vr,vi))):
                    for z,val in enumerate((xr,xi)):
                        hh,ll=split(val)
                        rs=pl.ds(z*128+j*RC,RC)
                        hi[q,rs,ls]=hh; lo[q,rs,ls]=ll
        bh=mats[2]; bl=mats[3]
        for q in range(2):
            mid[q]=dot(bh,hi[q])+dot(bh,lo[q])+dot(bl,hi[q])
        lc=twl[0]; lsn=twl[1]
        for q in range(2):
            for j in range(128//RC):
                ar=mid[q,pl.ds(j*RC,RC),pl.ds(0,128)]; br=mid[q,pl.ds(j*RC,RC),pl.ds(128,128)]
                ai=mid[q,pl.ds(128+j*RC,RC),pl.ds(0,128)]; bi=mid[q,pl.ds(128+j*RC,RC),pl.ds(128,128)]
                er,ei=ar+br,ai+bi
                dr,di=ar-br,ai-bi
                vr=dr*lc+di*lsn; vi=di*lc-dr*lsn
                rs=pl.ds(q*128+j*RC,RC)
                for e,(xr,xi) in enumerate(((er,ei),(vr,vi))):
                    for z,val in enumerate((xr,xi)):
                        hh,ll=split(val)
                        hi[e,rs,pl.ds(128*z,128)]=hh; lo[e,rs,pl.ds(128*z,128)]=ll
        ah=mats[0]; al=mats[1]
        for e in range(2):
            mid[e]=dot(hi[e],ah)+dot(lo[e],ah)+dot(hi[e],al)
        cp(s,0).wait(); cp(s,1).wait()
        pm=perm[...]
        for q in range(2):
            mv=jnp.concatenate([mbuf[s,t,pl.ds(q,128,stride=2),:] for t in range(2)],axis=1)
            mh,ml=split(mv)
            mp=dot(mh,pm)+dot(ml,pm)
            for e in range(2):
                for j in range(128//RC):
                    rs=pl.ds(q*128+j*RC,RC)
                    fr=mid[e,rs,pl.ds(0,128)]; fi=mid[e,rs,pl.ds(128,128)]
                    m=mp[j*RC:(j+1)*RC,e*128:(e+1)*128]
                    f=m*lax.rsqrt(jnp.maximum(fr*fr+fi*fi,0.25))
                    for z,val in enumerate((fr*f,fi*f)):
                        hh,ll=split(val)
                        hi[e,rs,pl.ds(128*z,128)]=hh; lo[e,rs,pl.ds(128*z,128)]=ll
        for e in range(2):
            mid[e]=dot(hi[e],bh)+dot(lo[e],bh)+dot(hi[e],bl)
        for q in range(2):
            for j in range(128//RC):
                rs=pl.ds(q*128+j*RC,RC)
                er=mid[0,rs,pl.ds(0,128)]; ei=mid[0,rs,pl.ds(128,128)]
                orr=mid[1,rs,pl.ds(0,128)]; oi=mid[1,rs,pl.ds(128,128)]
                vr=orr*lc-oi*lsn; vi=oi*lc+orr*lsn
                for t,(xr,xi) in enumerate(((er+vr,ei+vi),(er-vr,ei-vi))):
                    for z,val in enumerate((xr,xi)):
                        hh,ll=split(val)
                        hi[q,pl.ds(z*128+j*RC,RC),pl.ds(128*t,128)]=hh
                        lo[q,pl.ds(z*128+j*RC,RC),pl.ds(128*t,128)]=ll
        for q in range(2):
            mid[q]=dot(ah,hi[q])+dot(ah,lo[q])+dot(al,hi[q])
        for j in range(128//RC):
            tc=twr[0,pl.ds(j*RC,RC),:]; ts=twr[1,pl.ds(j*RC,RC),:]
            g=[[[None]*2 for _ in range(2)] for _ in range(2)]
            for t in range(2):
                ls=pl.ds(128*t,128)
                er=mid[0,pl.ds(j*RC,RC),ls]; ei=mid[0,pl.ds(128+j*RC,RC),ls]
                orr=mid[1,pl.ds(j*RC,RC),ls]; oi=mid[1,pl.ds(128+j*RC,RC),ls]
                vr=orr*tc-oi*ts; vi=oi*tc+orr*ts
                for h,(xr,xi) in enumerate(((er+vr,ei+vi),(er-vr,ei-vi))):
                    rr=pl.ds(h*128+j*RC,RC)
                    cr=xr-wave[0,rr,ls]; ci=xi-wave[1,rr,ls]
                    a,b=patch[0,rr,ls],patch[1,rr,ls]
                    pterm[0,t,rr,:]+=a*cr+b*ci
                    pterm[1,t,rr,:]+=a*ci-b*cr
                    pr,pi=ill[0,rr,ls],ill[1,rr,ls]
                    g[h][0][t]=pr*cr+pi*ci
                    g[h][1][t]=pr*ci-pi*cr
            for h in range(2):
                for z in range(2):
                    rg=[pltpu.roll(g[h][z][t],sh,1) for t in range(2)]
                    low=lane<sh
                    rows=pl.ds(r+h*128+j*RC,RC)
                    grad[z,ct,rows,:]+=jnp.where(low,0.0,rg[0])
                    grad[z,ct+1,rows,:]+=jnp.where(low,rg[0],rg[1])
                    grad[z,ct+2,rows,:]+=jnp.where(low,rg[1],0.0)

def windows(offs,cnt,ext,ill,meas):
    mats,twr,twl,perm=consts()
    V=pl.BlockSpec(memory_space=pltpu.VMEM); Sm=pl.BlockSpec(memory_space=pltpu.SMEM)
    return pl.pallas_call(wkernel,
        out_shape=(jax.ShapeDtypeStruct((2,6,768,128),F32),jax.ShapeDtypeStruct((2,2,256,128),F32)),
        in_specs=[Sm,Sm,V,V,V,V,V,V,pl.BlockSpec(memory_space=pl.ANY)],
        out_specs=(V,V),
        scratch_shapes=[pltpu.VMEM((16,2,256,128),F32),pltpu.VMEM((2,256,256),F32),pltpu.VMEM((2,256,256),F32),
            pltpu.VMEM((2,256,256),BF),pltpu.VMEM((2,256,256),BF),pltpu.VMEM((2,256,256),F32),pltpu.SemaphoreType.DMA((16,2))],
        compiler_params=pltpu.CompilerParams(vmem_limit_bytes=48*2**20),
    )(offs,cnt,ext,ill,jnp.asarray(mats),jnp.asarray(twr),jnp.asarray(twl),jnp.asarray(perm),meas)


MESH = pl.DeviceIdType.MESH


def remote(src, dst, send_sem, recv_sem, device):
    return pltpu.make_async_remote_copy(
        src_ref=src, dst_ref=dst, send_sem=send_sem, recv_sem=recv_sem,
        device_id=device, device_id_type=MESH,
    )


def greet(devices):
    barrier = pltpu.get_barrier_semaphore()
    expected = 0
    for condition, device in devices:
        if condition is None:
            pl.semaphore_signal(barrier, inc=1, device_id=device, device_id_type=MESH)
            expected = expected + 1
        else:
            @pl.when(condition)
            def _(device=device):
                pl.semaphore_signal(barrier, inc=1, device_id=device, device_id_type=MESH)
            expected = expected + condition.astype(jnp.int32)
    return barrier, expected


def neighbours():
    a = lax.axis_index("ty")
    b = lax.axis_index("tx")
    has = {"up": a > 0, "down": a < 15, "left": b > 0, "right": b < 15}
    ids = {"up": (jnp.maximum(a - 1, 0), b), "down": (jnp.minimum(a + 1, 15), b),
           "left": (a, jnp.maximum(b - 1, 0)), "right": (a, jnp.minimum(b + 1, 15))}
    return a, b, has, ids


OPPOSITE = {"up": "down", "down": "up", "left": "right", "right": "left"}


def halo_kernel(tile, ext, own_sem, row_send, row_recv, col_send, col_recv, cor_send, cor_recv):
    a, b, has, ids = neighbours()
    barrier, expected = greet([(has[k], ids[k]) for k in ids])
    own = [pltpu.make_async_copy(tile.at[:, :, pl.ds(128 * t, 128)], ext.at[:, 1 + t, pl.ds(128, 512), :], own_sem.at[t]) for t in range(4)]
    for copy in own:
        copy.start()
    pl.semaphore_wait(barrier, expected)
    rows, cols, corners = {}, {}, {}
    for i, way in enumerate(("down", "up")):
        src_row, dst_row = (384, 0) if way == "down" else (0, 640)
        for t in (0, 3, 1, 2):
            rows[way, t] = remote(
                tile.at[:, pl.ds(src_row, 128), pl.ds(128 * t, 128)],
                ext.at[:, 1 + t, pl.ds(dst_row, 128), :],
                row_send.at[i, t], row_recv.at[i, t], ids[way])
    for i, way in enumerate(("right", "left")):
        src_t, dst_t = (3, 0) if way == "right" else (0, 5)
        cols[way] = remote(
            tile.at[:, :, pl.ds(128 * src_t, 128)], ext.at[:, dst_t, pl.ds(128, 512), :],
            col_send.at[i], col_recv.at[i], ids[way])
        for j, row in enumerate((0, 640)):
            corners[way, j] = remote(
                ext.at[:, 1 + src_t, pl.ds(row, 128), :], ext.at[:, dst_t, pl.ds(row, 128), :],
                cor_send.at[i, j], cor_recv.at[i, j], ids[way])
    for t in (0, 3, 1, 2):
        for way in ("down", "up"):
            pl.when(has[way])(rows[way, t].start)
    for way in ("right", "left"):
        pl.when(has[way])(cols[way].start)
    for j, way in enumerate(("down", "up")):
        @pl.when(has[OPPOSITE[way]])
        def _(way=way):
            rows[way, 0].wait_recv()
            rows[way, 3].wait_recv()
        for side in ("right", "left"):
            pl.when(jnp.logical_and(has[side], has[OPPOSITE[way]]))(corners[side, j].start)
    for copy in own:
        copy.wait()
    for way in ("down", "up"):
        for t in (1, 2):
            pl.when(has[OPPOSITE[way]])(rows[way, t].wait_recv)
        for t in range(4):
            pl.when(has[way])(rows[way, t].wait_send)
    for side in ("right", "left"):
        pl.when(has[OPPOSITE[side]])(cols[side].wait_recv)
        pl.when(has[side])(cols[side].wait_send)
        for j, way in enumerate(("down", "up")):
            pl.when(jnp.logical_and(has[OPPOSITE[side]], has[OPPOSITE[way]]))(corners[side, j].wait_recv)
            pl.when(jnp.logical_and(has[side], has[OPPOSITE[way]]))(corners[side, j].wait_send)


def halo(tile):
    D = pltpu.SemaphoreType.DMA
    A = pl.BlockSpec(memory_space=pl.ANY)
    return pl.pallas_call(
        halo_kernel,
        out_shape=jax.ShapeDtypeStruct((2, 6, 768, 128), F32),
        in_specs=[A], out_specs=A,
        scratch_shapes=[D((4,)), D((2, 4)), D((2, 4)), D((2,)), D((2,)), D((2, 2)), D((2, 2))],
        compiler_params=pltpu.CompilerParams(collective_id=1, has_side_effects=True, vmem_limit_bytes=60 * 2**20),
    )(tile)


def partners(b):
    core = b % 2
    x = (b // 2) % 4
    zlo = b // 8
    return core, x, zlo


def fold_kernel(grad, pterm, upd, part, rxc, rxm, rz, edge, rcore, rx, sumc,
                core_s, core_r, xs, xr, cs, cr, ms, mr, zs, zr):
    a, b, has, ids = neighbours()
    core, x, zlo = partners(b)
    mates = [(a, zlo * 8 + ((x + d) % 4) * 2 + core) for d in (1, 2, 3)]
    other = (a, zlo * 8 + x * 2 + (1 - core))
    barrier, expected = greet([(has[k], ids[k]) for k in ids] + [(None, m) for m in mates])
    pl.semaphore_wait(barrier, expected)
    first = remote(pterm.at[1 - core], rcore, core_s, core_r, other)
    first.start()
    corner, middle, zmid, zedge = {}, {}, {}, {}
    for i, side in enumerate(("right", "left")):
        src_t = 5 if side == "right" else 0
        for j, row in enumerate((0, 640)):
            corner[side, j] = remote(grad.at[:, src_t, pl.ds(row, 128), :], rxc.at[i, j],
                                     cs.at[i, j], cr.at[i, j], ids[side])
        middle[side] = remote(grad.at[:, src_t, pl.ds(128, 512), :], rxm.at[i], ms.at[i], mr.at[i], ids[side])
    for j, way in enumerate(("up", "down")):
        row = 0 if way == "up" else 640
        zmid[way] = remote(grad.at[:, pl.ds(2, 2), pl.ds(row, 128), :], rz.at[j, :, pl.ds(1, 2)],
                           zs.at[j, 1], zr.at[j, 1], ids[way])
        for k, t in ((0, 0), (2, 3)):
            zedge[way, k] = remote(edge.at[j, k // 2], rz.at[j, :, t], zs.at[j, k], zr.at[j, k], ids[way])
    for side in ("right", "left"):
        for j in range(2):
            pl.when(has[side])(corner[side, j].start)
    for way in ("up", "down"):
        pl.when(has[way])(zmid[way].start)
    for side in ("right", "left"):
        pl.when(has[side])(middle[side].start)
    for j, row in enumerate((0, 640)):
        for k, (t, side) in enumerate(((1, "right"), (4, "left"))):
            i = k
            edge[j, k] = grad[:, t, row:row + 128, :]
            @pl.when(has[OPPOSITE[side]])
            def _(i=i, j=j, k=k, side=side):
                corner[side, j].wait_recv()
                edge[j, k] += rxc[i, j]
            way = "up" if j == 0 else "down"
            pl.when(has[way])(zedge[way, 2 * k].start)
    first.wait_recv()
    sumc[...] = pterm[core] + rcore[...]
    xsend = [remote(sumc.at[(x + d) % 4], rx.at[d - 1], xs.at[d - 1], xr.at[d - 1], mates[d - 1]) for d in (1, 2, 3)]
    for copy in xsend:
        copy.start()
    for t in range(4):
        upd[:, t] = grad[:, 1 + t, 128:640, :]
    for copy in xsend:
        copy.wait_recv()
    part[...] = sumc[x] + rx[0] + rx[1] + rx[2]
    for i, (side, t) in enumerate((("right", 0), ("left", 3))):
        @pl.when(has[OPPOSITE[side]])
        def _(i=i, side=side, t=t):
            middle[side].wait_recv()
            upd[:, t] += rxm[i]
    for j, (way, row) in enumerate((("up", 384), ("down", 0))):
        @pl.when(has[OPPOSITE[way]])
        def _(j=j, way=way, row=row):
            zmid[way].wait_recv()
            zedge[way, 0].wait_recv()
            zedge[way, 2].wait_recv()
            upd[:, :, row:row + 128, :] += rz[j]
    first.wait_send()
    for copy in xsend:
        copy.wait_send()
    for side in ("right", "left"):
        for j in range(2):
            pl.when(has[side])(corner[side, j].wait_send)
        pl.when(has[side])(middle[side].wait_send)
    for way in ("up", "down"):
        pl.when(has[way])(zmid[way].wait_send)
        for k in (0, 2):
            pl.when(has[way])(zedge[way, k].wait_send)


def fold(grad, pterm):
    D = pltpu.SemaphoreType.DMA
    V = pl.BlockSpec(memory_space=pltpu.VMEM)
    return pl.pallas_call(
        fold_kernel,
        out_shape=(jax.ShapeDtypeStruct((2, 4, 512, 128), F32), jax.ShapeDtypeStruct((16, 8, 128), F32)),
        in_specs=[V, V], out_specs=(V, V),
        scratch_shapes=[
            pltpu.VMEM((2, 2, 2, 128, 128), F32), pltpu.VMEM((2, 2, 512, 128), F32),
            pltpu.VMEM((2, 2, 4, 128, 128), F32), pltpu.VMEM((2, 2, 2, 128, 128), F32),
            pltpu.VMEM((4, 16, 8, 128), F32), pltpu.VMEM((3, 16, 8, 128), F32), pltpu.VMEM((4, 16, 8, 128), F32),
            D, D, D((3,)), D((3,)), D((2, 2)), D((2, 2)), D((2,)), D((2,)), D((2, 3)), D((2, 3)),
        ],
        compiler_params=pltpu.CompilerParams(collective_id=2, has_side_effects=True, vmem_limit_bytes=60 * 2**20),
    )(grad, pterm)


def spread_kernel(part, total, rc, cs, cr, ds, dr, es, er, fs, fr):
    a = lax.axis_index("ty")
    b = lax.axis_index("tx")
    core, x, zlo = partners(b)
    low = x * 2 + core
    unit = zlo * 16 + a

    def member(d):
        u = (unit + d) % 32
        return (u % 16, (u // 16) * 8 + low)

    mates = [(a, zlo * 8 + ((x + d) % 4) * 2 + core) for d in (1, 2, 3)]
    other = (a, zlo * 8 + x * 2 + (1 - core))
    barrier, expected = greet([(None, m) for m in mates] + [(None, other)])

    @pl.loop(1, 32)
    def _(d):
        pl.semaphore_signal(barrier, inc=1, device_id=member(d), device_id_type=MESH)

    pl.semaphore_wait(barrier, expected + 31)

    @pl.loop(1, 32)
    def _(d):
        device = member(d)
        remote(part.at[device[0]], rc.at[d - 1], cs, cr, device).start()

    whole = remote(rc, rc, cs, cr, other)
    whole.wait_recv()
    acc = part[a]
    for i in range(31):
        acc = acc + rc[i]
    total[core, x, a] = acc

    @pl.loop(1, 16)
    def _(d):
        remote(total.at[core, x, a], total.at[core, x, a], ds, dr, ((a + d) % 16, b)).start()

    some = remote(rc.at[pl.ds(0, 15)], rc.at[pl.ds(0, 15)], ds, dr, other)
    some.wait_recv()
    gather = [remote(total.at[core, x], total.at[core, x], es.at[d - 1], er.at[d - 1], mates[d - 1]) for d in (1, 2, 3)]
    for copy in gather:
        copy.start()
    for copy in gather:
        copy.wait_recv()
    last = remote(total.at[core], total.at[core], fs, fr, other)
    last.start()
    whole.wait_send()
    some.wait_send()
    for copy in gather:
        copy.wait_send()
    last.wait()


def spread(part):
    D = pltpu.SemaphoreType.DMA
    V = pl.BlockSpec(memory_space=pltpu.VMEM)
    return pl.pallas_call(
        spread_kernel,
        out_shape=jax.ShapeDtypeStruct((2, 4, 16, 8, 128), F32),
        in_specs=[V], out_specs=V,
        scratch_shapes=[pltpu.VMEM((31, 8, 128), F32), D, D, D, D, D((3,)), D((3,)), D, D],
        compiler_params=pltpu.CompilerParams(collective_id=3, has_side_effects=True, vmem_limit_bytes=60 * 2**20),
    )(part)


def shards(specimen, illumination, scan_offsets, slot_counts, measured):
    anchor = jnp.stack([lax.axis_index("ty") * 512, lax.axis_index("tx") * 512]) - 128
    local = scan_offsets[0, 0] - anchor[:, None]
    ext = halo(specimen)
    grad, probe_term = windows(local, slot_counts[0], ext, illumination, measured[0, 0])
    update, part = fold(grad, probe_term.reshape(2, 4, 16, 8, 128))
    total = spread(part)
    probe_power = (
        jnp.mean(illumination[0] * illumination[0] + illumination[1] * illumination[1]) + 1e-05
    )
    field = update.transpose(0, 2, 1, 3).reshape(2, 512, 512)
    new_specimen = specimen + field / probe_power
    summed = total.reshape(2, 2, 256, 128).transpose(0, 2, 1, 3).reshape(2, 256, 256)
    total_slots = measured.shape[2] * lax.axis_size("ty") * lax.axis_size("tx")
    new_illumination = illumination + summed / math.sqrt(total_slots)
    return (new_specimen, new_illumination)

def solution(mesh):
    in_specs = (
        P(None, "ty", "tx"),
        P(),
        P("ty", "tx", None, None),
        P("ty", "tx"),
        P("ty", "tx", None, None, None),
    )
    out_specs = (P(None, "ty", "tx"), P())
    return jax.shard_map(shards, mesh=mesh, in_specs=in_specs, out_specs=out_specs, check_vma=False)
```

```python
import math

import numpy as np
import jax, jax.numpy as jnp
from jax import lax
from jax.experimental import pallas as pl
from jax.experimental.pallas import tpu as pltpu
import ml_dtypes
from jax.sharding import PartitionSpec as P

F32=jnp.float32; BF=jnp.bfloat16

def consts():
    k=np.arange(128)
    ang=2*np.pi*np.outer(k,k)%(2*np.pi*128)/128
    ang=2*np.pi*((np.outer(k,k))%128)/128
    C=np.cos(ang)/16; S=np.sin(ang)/16
    A=np.block([[C,-S],[S,C]]); B=A.T.copy()
    def split(x):
        x=x.astype(np.float32)
        h=x.astype(ml_dtypes.bfloat16); l=(x-h.astype(np.float32)).astype(ml_dtypes.bfloat16)
        return h,l
    ah,al=split(A); bh,bl=split(B)
    mats=np.stack([ah,al,bh,bl])
    t=2*np.pi*np.arange(128)/256
    c=np.cos(t).astype(np.float32); s=np.sin(t).astype(np.float32)
    twr=np.stack([np.broadcast_to(c[:,None],(128,128)),np.broadcast_to(s[:,None],(128,128))])
    twl=np.stack([np.broadcast_to(c[None],(16,128)),np.broadcast_to(s[None],(16,128))])
    k=np.arange(256)
    perm=np.zeros((256,256));
    perm[k, (k%2)*128+k//2]=1
    return mats, twr.astype(np.float32).copy(), twl.astype(np.float32).copy(), perm.astype(ml_dtypes.bfloat16)

def split(x):
    h=x.astype(BF)
    return h,(x-h.astype(F32)).astype(BF)

def dot(a,b): return jnp.dot(a,b,preferred_element_type=F32)

RC=16
def wkernel(offs, cnt, ext, ill, mats, twr, twl, perm, meas, grad, pterm,
            mbuf, patch, wave, hi, lo, mid, msem):
    n=cnt[0]
    def cp(s,t): return pltpu.make_async_copy(meas.at[s,:,pl.ds(128*t,128)], mbuf.at[s,t], msem.at[s,t])
    @pl.loop(0,n)
    def _(s):
        cp(s,0).start(); cp(s,1).start()
    @pl.loop(0,96)
    def _(i):
        for p in range(2):
            for t in range(6):
                grad[p,t,pl.ds(pl.multiple_of(8*i,8),8),:]=jnp.zeros((8,128),F32)
    pterm[...]=jnp.zeros_like(pterm)
    lane=lax.broadcasted_iota(jnp.int32,(RC,128),1)
    @pl.loop(0,n)
    def _(s):
        r=offs[0,s]; c=offs[1,s]
        ct=c//128; sh=c%128
        ush=(128-sh)%128
        lmask=lane<128-sh
        for j in range(128//RC):
            half=[]
            for h in range(2):
                row=h*128+j*RC
                rr=pl.ds(row,RC)
                x=[[pltpu.roll(ext[p,ct+t,pl.ds(r+row,RC),:],ush,1) for t in range(3)] for p in range(2)]
                pt=[[jnp.where(lmask,x[p][t],x[p][t+1]) for t in range(2)] for p in range(2)]
                ws=[]
                for t in range(2):
                    ls=pl.ds(128*t,128)
                    pr,pi=ill[0,rr,ls],ill[1,rr,ls]
                    a,b=pt[0][t],pt[1][t]
                    patch[0,rr,ls]=a; patch[1,rr,ls]=b
                    wr=pr*a-pi*b; wi=pr*b+pi*a
                    wave[0,rr,ls]=wr; wave[1,rr,ls]=wi
                    ws.append((wr,wi))
                half.append(ws)
            tc=twr[0,pl.ds(j*RC,RC),:]; ts=twr[1,pl.ds(j*RC,RC),:]
            for t in range(2):
                ls=pl.ds(128*t,128)
                (ar,ai),(br,bi)=half[0][t],half[1][t]
                er,ei=ar+br,ai+bi
                dr,di=ar-br,ai-bi
                vr=dr*tc+di*ts; vi=di*tc-dr*ts
                for q,(xr,xi) in enumerate(((er,ei),(vr,vi))):
                    for z,val in enumerate((xr,xi)):
                        hh,ll=split(val)
                        rs=pl.ds(z*128+j*RC,RC)
                        hi[q,rs,ls]=hh; lo[q,rs,ls]=ll
        bh=mats[2]; bl=mats[3]
        for q in range(2):
            mid[q]=dot(bh,hi[q])+dot(bh,lo[q])+dot(bl,hi[q])
        lc=twl[0]; lsn=twl[1]
        for q in range(2):
            for j in range(128//RC):
                ar=mid[q,pl.ds(j*RC,RC),pl.ds(0,128)]; br=mid[q,pl.ds(j*RC,RC),pl.ds(128,128)]
                ai=mid[q,pl.ds(128+j*RC,RC),pl.ds(0,128)]; bi=mid[q,pl.ds(128+j*RC,RC),pl.ds(128,128)]
                er,ei=ar+br,ai+bi
                dr,di=ar-br,ai-bi
                vr=dr*lc+di*lsn; vi=di*lc-dr*lsn
                rs=pl.ds(q*128+j*RC,RC)
                for e,(xr,xi) in enumerate(((er,ei),(vr,vi))):
                    for z,val in enumerate((xr,xi)):
                        hh,ll=split(val)
                        hi[e,rs,pl.ds(128*z,128)]=hh; lo[e,rs,pl.ds(128*z,128)]=ll
        ah=mats[0]; al=mats[1]
        for e in range(2):
            mid[e]=dot(hi[e],ah)+dot(lo[e],ah)+dot(hi[e],al)
        cp(s,0).wait(); cp(s,1).wait()
        pm=perm[...]
        for q in range(2):
            mv=jnp.concatenate([mbuf[s,t,pl.ds(q,128,stride=2),:] for t in range(2)],axis=1)
            mh,ml=split(mv)
            mp=dot(mh,pm)+dot(ml,pm)
            for e in range(2):
                for j in range(128//RC):
                    rs=pl.ds(q*128+j*RC,RC)
                    fr=mid[e,rs,pl.ds(0,128)]; fi=mid[e,rs,pl.ds(128,128)]
                    m=mp[j*RC:(j+1)*RC,e*128:(e+1)*128]
                    f=m*lax.rsqrt(jnp.maximum(fr*fr+fi*fi,0.25))
                    for z,val in enumerate((fr*f,fi*f)):
                        hh,ll=split(val)
                        hi[e,rs,pl.ds(128*z,128)]=hh; lo[e,rs,pl.ds(128*z,128)]=ll
        for e in range(2):
            mid[e]=dot(hi[e],bh)+dot(lo[e],bh)+dot(hi[e],bl)
        for q in range(2):
            for j in range(128//RC):
                rs=pl.ds(q*128+j*RC,RC)
                er=mid[0,rs,pl.ds(0,128)]; ei=mid[0,rs,pl.ds(128,128)]
                orr=mid[1,rs,pl.ds(0,128)]; oi=mid[1,rs,pl.ds(128,128)]
                vr=orr*lc-oi*lsn; vi=oi*lc+orr*lsn
                for t,(xr,xi) in enumerate(((er+vr,ei+vi),(er-vr,ei-vi))):
                    for z,val in enumerate((xr,xi)):
                        hh,ll=split(val)
                        hi[q,pl.ds(z*128+j*RC,RC),pl.ds(128*t,128)]=hh
                        lo[q,pl.ds(z*128+j*RC,RC),pl.ds(128*t,128)]=ll
        for q in range(2):
            mid[q]=dot(ah,hi[q])+dot(ah,lo[q])+dot(al,hi[q])
        for j in range(128//RC):
            tc=twr[0,pl.ds(j*RC,RC),:]; ts=twr[1,pl.ds(j*RC,RC),:]
            g=[[[None]*2 for _ in range(2)] for _ in range(2)]
            for t in range(2):
                ls=pl.ds(128*t,128)
                er=mid[0,pl.ds(j*RC,RC),ls]; ei=mid[0,pl.ds(128+j*RC,RC),ls]
                orr=mid[1,pl.ds(j*RC,RC),ls]; oi=mid[1,pl.ds(128+j*RC,RC),ls]
                vr=orr*tc-oi*ts; vi=oi*tc+orr*ts
                for h,(xr,xi) in enumerate(((er+vr,ei+vi),(er-vr,ei-vi))):
                    rr=pl.ds(h*128+j*RC,RC)
                    cr=xr-wave[0,rr,ls]; ci=xi-wave[1,rr,ls]
                    a,b=patch[0,rr,ls],patch[1,rr,ls]
                    pterm[0,t,rr,:]+=a*cr+b*ci
                    pterm[1,t,rr,:]+=a*ci-b*cr
                    pr,pi=ill[0,rr,ls],ill[1,rr,ls]
                    g[h][0][t]=pr*cr+pi*ci
                    g[h][1][t]=pr*ci-pi*cr
            for h in range(2):
                for z in range(2):
                    rg=[pltpu.roll(g[h][z][t],sh,1) for t in range(2)]
                    low=lane<sh
                    rows=pl.ds(r+h*128+j*RC,RC)
                    grad[z,ct,rows,:]+=jnp.where(low,0.0,rg[0])
                    grad[z,ct+1,rows,:]+=jnp.where(low,rg[0],rg[1])
                    grad[z,ct+2,rows,:]+=jnp.where(low,rg[1],0.0)

def windows(offs,cnt,ext,ill,meas):
    mats,twr,twl,perm=consts()
    V=pl.BlockSpec(memory_space=pltpu.VMEM); Sm=pl.BlockSpec(memory_space=pltpu.SMEM)
    return pl.pallas_call(wkernel,
        out_shape=(jax.ShapeDtypeStruct((2,6,768,128),F32),jax.ShapeDtypeStruct((2,2,256,128),F32)),
        in_specs=[Sm,Sm,V,V,V,V,V,V,pl.BlockSpec(memory_space=pl.ANY)],
        out_specs=(V,V),
        scratch_shapes=[pltpu.VMEM((16,2,256,128),F32),pltpu.VMEM((2,256,256),F32),pltpu.VMEM((2,256,256),F32),
            pltpu.VMEM((2,256,256),BF),pltpu.VMEM((2,256,256),BF),pltpu.VMEM((2,256,256),F32),pltpu.SemaphoreType.DMA((16,2))],
        compiler_params=pltpu.CompilerParams(vmem_limit_bytes=28*2**20),
    )(offs,cnt,ext,ill,jnp.asarray(mats),jnp.asarray(twr),jnp.asarray(twl),jnp.asarray(perm),meas)


MESH = pl.DeviceIdType.MESH


def remote(src, dst, send_sem, recv_sem, device):
    return pltpu.make_async_remote_copy(
        src_ref=src, dst_ref=dst, send_sem=send_sem, recv_sem=recv_sem,
        device_id=device, device_id_type=MESH,
    )


def greet(devices):
    barrier = pltpu.get_barrier_semaphore()
    expected = 0
    for condition, device in devices:
        if condition is None:
            pl.semaphore_signal(barrier, inc=1, device_id=device, device_id_type=MESH)
            expected = expected + 1
        else:
            @pl.when(condition)
            def _(device=device):
                pl.semaphore_signal(barrier, inc=1, device_id=device, device_id_type=MESH)
            expected = expected + condition.astype(jnp.int32)
    return barrier, expected


def neighbours():
    a = lax.axis_index("ty")
    b = lax.axis_index("tx")
    has = {"up": a > 0, "down": a < 15, "left": b > 0, "right": b < 15}
    ids = {"up": (jnp.maximum(a - 1, 0), b), "down": (jnp.minimum(a + 1, 15), b),
           "left": (a, jnp.maximum(b - 1, 0)), "right": (a, jnp.minimum(b + 1, 15))}
    return a, b, has, ids


OPPOSITE = {"up": "down", "down": "up", "left": "right", "right": "left"}


def halo_kernel(tile, ext, own_sem, row_send, row_recv, col_send, col_recv, cor_send, cor_recv):
    a, b, has, ids = neighbours()
    barrier, expected = greet([(has[k], ids[k]) for k in ids])
    own = [pltpu.make_async_copy(tile.at[:, :, pl.ds(128 * t, 128)], ext.at[:, 1 + t, pl.ds(128, 512), :], own_sem.at[t]) for t in range(4)]
    for copy in own:
        copy.start()
    pl.semaphore_wait(barrier, expected)
    rows, cols, corners = {}, {}, {}
    for i, way in enumerate(("down", "up")):
        src_row, dst_row = (384, 0) if way == "down" else (0, 640)
        for t in (0, 3, 1, 2):
            rows[way, t] = remote(
                tile.at[:, pl.ds(src_row, 128), pl.ds(128 * t, 128)],
                ext.at[:, 1 + t, pl.ds(dst_row, 128), :],
                row_send.at[i, t], row_recv.at[i, t], ids[way])
    for i, way in enumerate(("right", "left")):
        src_t, dst_t = (3, 0) if way == "right" else (0, 5)
        cols[way] = remote(
            tile.at[:, :, pl.ds(128 * src_t, 128)], ext.at[:, dst_t, pl.ds(128, 512), :],
            col_send.at[i], col_recv.at[i], ids[way])
        for j, row in enumerate((0, 640)):
            corners[way, j] = remote(
                ext.at[:, 1 + src_t, pl.ds(row, 128), :], ext.at[:, dst_t, pl.ds(row, 128), :],
                cor_send.at[i, j], cor_recv.at[i, j], ids[way])
    for t in (0, 3, 1, 2):
        for way in ("down", "up"):
            pl.when(has[way])(rows[way, t].start)
    for way in ("right", "left"):
        pl.when(has[way])(cols[way].start)
    for j, way in enumerate(("down", "up")):
        @pl.when(has[OPPOSITE[way]])
        def _(way=way):
            rows[way, 0].wait_recv()
            rows[way, 3].wait_recv()
        for side in ("right", "left"):
            pl.when(jnp.logical_and(has[side], has[OPPOSITE[way]]))(corners[side, j].start)
    for copy in own:
        copy.wait()
    for way in ("down", "up"):
        for t in (1, 2):
            pl.when(has[OPPOSITE[way]])(rows[way, t].wait_recv)
        for t in range(4):
            pl.when(has[way])(rows[way, t].wait_send)
    for side in ("right", "left"):
        pl.when(has[OPPOSITE[side]])(cols[side].wait_recv)
        pl.when(has[side])(cols[side].wait_send)
        for j, way in enumerate(("down", "up")):
            pl.when(jnp.logical_and(has[OPPOSITE[side]], has[OPPOSITE[way]]))(corners[side, j].wait_recv)
            pl.when(jnp.logical_and(has[side], has[OPPOSITE[way]]))(corners[side, j].wait_send)


def halo(tile):
    D = pltpu.SemaphoreType.DMA
    A = pl.BlockSpec(memory_space=pl.ANY)
    return pl.pallas_call(
        halo_kernel,
        out_shape=jax.ShapeDtypeStruct((2, 6, 768, 128), F32),
        in_specs=[A], out_specs=pl.BlockSpec(memory_space=pltpu.VMEM),
        scratch_shapes=[D((4,)), D((2, 4)), D((2, 4)), D((2,)), D((2,)), D((2, 2)), D((2, 2))],
        compiler_params=pltpu.CompilerParams(collective_id=1, has_side_effects=True, vmem_limit_bytes=24 * 2**20),
    )(tile)


def partners(b):
    core = b % 2
    x = (b // 2) % 4
    zlo = b // 8
    return core, x, zlo


def finish_kernel(spec, ill, grad, pterm, newspec, newill,
                  rxc, rxm, rz, edge, rcore, rx, sumc, part, rc, total,
                  core_s, core_r, xs, xr, cs, cr, ms, mr, zs, zr,
                  us, ur, ds, dr, es, er, fs, fr):
    a, b, has, ids = neighbours()
    core, x, zlo = partners(b)
    low = x * 2 + core
    unit = zlo * 16 + a

    def member(d):
        u = (unit + d) % 32
        return (u % 16, (u // 16) * 8 + low)

    mates = [(a, zlo * 8 + ((x + d) % 4) * 2 + core) for d in (1, 2, 3)]
    other = (a, zlo * 8 + x * 2 + (1 - core))
    barrier, expected = greet([(None, m) for m in mates] + [(None, other)]
                              + [(jnp.logical_and(core == 0, has["left"]), ids["left"]),
                                 (jnp.logical_and(core == 1, has["right"]), ids["right"])])

    @pl.loop(1, 32)
    def _(d):
        pl.semaphore_signal(barrier, inc=1, device_id=member(d), device_id_type=MESH)

    power = jnp.sum(ill[0] * ill[0] + ill[1] * ill[1]) * (1.0 / 65536) + 1e-05
    inv = 1.0 / power
    pl.semaphore_wait(barrier, expected + 31)
    first = remote(pterm.at[1 - core], rcore, core_s, core_r, other)
    first.start()
    corner, middle, zmid, zedge = {}, {}, {}, {}
    for i, side in enumerate(("right", "left")):
        src_t = 5 if side == "right" else 0
        for j, row in enumerate((0, 640)):
            corner[side, j] = remote(grad.at[:, src_t, pl.ds(row, 128), :], rxc.at[i, j],
                                     cs.at[i, j], cr.at[i, j], ids[side])
        middle[side] = remote(grad.at[:, src_t, pl.ds(128, 512), :], rxm.at[i], ms.at[i], mr.at[i], ids[side])
    for j, way in enumerate(("up", "down")):
        row = 0 if way == "up" else 640
        zmid[way] = remote(grad.at[:, pl.ds(2, 2), pl.ds(row, 128), :], rz.at[j, :, pl.ds(1, 2)],
                           zs.at[j, 1], zr.at[j, 1], ids[way])
        for k, t in ((0, 0), (2, 3)):
            zedge[way, k] = remote(edge.at[j, k // 2], rz.at[j, :, t], zs.at[j, k], zr.at[j, k], ids[way])
    for side in ("right", "left"):
        for j in range(2):
            pl.when(has[side])(corner[side, j].start)
    for way in ("up", "down"):
        pl.when(has[way])(zmid[way].start)
    first.wait_recv()
    sumc[...] = pterm[core] + rcore[...]
    xsend = [remote(sumc.at[(x + d) % 4], rx.at[d - 1], xs.at[d - 1], xr.at[d - 1], mates[d - 1]) for d in (1, 2, 3)]
    for copy in xsend:
        copy.start()
    for side in ("right", "left"):
        pl.when(has[side])(middle[side].start)
    for j, row in enumerate((0, 640)):
        for k, (t, side) in enumerate(((1, "right"), (4, "left"))):
            edge[j, k] = grad[:, t, row:row + 128, :]
            @pl.when(has[OPPOSITE[side]])
            def _(j=j, k=k, side=side):
                corner[side, j].wait_recv()
                edge[j, k] += rxc[k, j]
            way = "up" if j == 0 else "down"
            pl.when(has[way])(zedge[way, 2 * k].start)
    for copy in xsend:
        copy.wait_recv()
    part[...] = sumc[x] + rx[0] + rx[1] + rx[2]

    @pl.loop(1, 32)
    def _(d):
        device = member(d)
        remote(part.at[device[0]], rc.at[d - 1], us, ur, device).start()

    @pl.loop(0, 16)
    def _(i):
        rows = pl.ds(pl.multiple_of(32 * i, 32), 32)
        more = pl.ds(pl.multiple_of(32 * i + 128, 32), 32)
        for p in range(2):
            for t in range(4):
                lanes = pl.ds(128 * t, 128)
                newspec[p, rows, lanes] = spec[p, rows, lanes] + inv * grad[p, 1 + t, more, :]

    whole = remote(rc, rc, us, ur, other)
    whole.wait_recv()
    acc = part[a]
    for i in range(31):
        acc = acc + rc[i]
    total[core, x, a] = acc

    @pl.loop(1, 16)
    def _(d):
        remote(total.at[core, x, a], total.at[core, x, a], ds, dr, ((a + d) % 16, b)).start()

    for k, (side, t) in enumerate((("right", 0), ("left", 3))):
        @pl.when(has[OPPOSITE[side]])
        def _(k=k, side=side, t=t):
            middle[side].wait_recv()
            newspec[:, :, 128 * t:128 * t + 128] += inv * rxm[k]
    some = remote(rc.at[pl.ds(0, 15)], rc.at[pl.ds(0, 15)], ds, dr, other)
    some.wait_recv()
    gather = [remote(total.at[core, x], total.at[core, x], es.at[d - 1], er.at[d - 1], mates[d - 1]) for d in (1, 2, 3)]
    for copy in gather:
        copy.start()
    for copy in gather:
        copy.wait_recv()
    last = remote(total.at[core], total.at[core], fs, fr, other)
    last.start()
    for j, (way, row) in enumerate((("up", 384), ("down", 0))):
        @pl.when(has[OPPOSITE[way]])
        def _(j=j, way=way, row=row):
            zmid[way].wait_recv()
            zedge[way, 0].wait_recv()
            zedge[way, 2].wait_recv()
            for t in range(4):
                newspec[:, row:row + 128, 128 * t:128 * t + 128] += inv * rz[j, :, t]
    last.wait()
    for p in range(2):
        for s in range(4):
            rows, lanes = pl.ds((s % 2) * 128, 128), pl.ds((s // 2) * 128, 128)
            newill[p, rows, lanes] = ill[p, rows, lanes] + total[p, s].reshape(128, 128) * (1.0 / 64)
    first.wait_send()
    for copy in xsend + gather:
        copy.wait_send()
    whole.wait_send()
    some.wait_send()
    for side in ("right", "left"):
        for j in range(2):
            pl.when(has[side])(corner[side, j].wait_send)
        pl.when(has[side])(middle[side].wait_send)
    for way in ("up", "down"):
        pl.when(has[way])(zmid[way].wait_send)
        for k in (0, 2):
            pl.when(has[way])(zedge[way, k].wait_send)


def finish(spec, ill, grad, pterm):
    D = pltpu.SemaphoreType.DMA
    V = pl.BlockSpec(memory_space=pltpu.VMEM)
    return pl.pallas_call(
        finish_kernel,
        out_shape=(jax.ShapeDtypeStruct((2, 512, 512), F32), jax.ShapeDtypeStruct((2, 256, 256), F32)),
        in_specs=[V, V, V, V], out_specs=(V, V),
        scratch_shapes=[
            pltpu.VMEM((2, 2, 2, 128, 128), F32), pltpu.VMEM((2, 2, 512, 128), F32),
            pltpu.VMEM((2, 2, 4, 128, 128), F32), pltpu.VMEM((2, 2, 2, 128, 128), F32),
            pltpu.VMEM((4, 16, 8, 128), F32), pltpu.VMEM((3, 16, 8, 128), F32), pltpu.VMEM((4, 16, 8, 128), F32),
            pltpu.VMEM((16, 8, 128), F32), pltpu.VMEM((31, 8, 128), F32), pltpu.VMEM((2, 4, 16, 8, 128), F32),
            D, D, D((3,)), D((3,)), D((2, 2)), D((2, 2)), D((2,)), D((2,)), D((2, 3)), D((2, 3)),
            D, D, D, D, D((3,)), D((3,)), D, D,
        ],
        compiler_params=pltpu.CompilerParams(collective_id=2, has_side_effects=True, vmem_limit_bytes=32 * 2**20),
    )(spec, ill, grad, pterm)


def shards(specimen, illumination, scan_offsets, slot_counts, measured):
    anchor = jnp.stack([lax.axis_index("ty") * 512, lax.axis_index("tx") * 512]) - 128
    local = scan_offsets[0, 0] - anchor[:, None]
    ext = halo(specimen)
    grad, probe_term = windows(local, slot_counts[0], ext, illumination, measured[0, 0])
    return finish(specimen, illumination, grad, probe_term.reshape(2, 4, 16, 8, 128))


def solution(mesh):
    in_specs = (
        P(None, "ty", "tx"),
        P(),
        P("ty", "tx", None, None),
        P("ty", "tx"),
        P("ty", "tx", None, None, None),
    )
    out_specs = (P(None, "ty", "tx"), P())
    return jax.shard_map(shards, mesh=mesh, in_specs=in_specs, out_specs=out_specs, check_vma=False)
```

```python
import math
import numpy as np
import jax, jax.numpy as jnp
from jax import lax
from jax.experimental import pallas as pl
from jax.experimental.pallas import tpu as pltpu
import ml_dtypes
from jax.sharding import PartitionSpec as P

F32=jnp.float32; BF=jnp.bfloat16

def consts():
    n=np.arange(128)
    out=[]
    for odd in (0,1):
        phase=np.outer(n,2*n+odd)%256
        ang=2*np.pi*phase/256
        tr,ti=np.cos(ang)/16,-np.sin(ang)/16
        r=np.block([[tr,ti],[-ti,tr]])
        for m in (r,r.T):
            m=m.astype(np.float32)
            h=m.astype(ml_dtypes.bfloat16); l=(m-h.astype(np.float32)).astype(ml_dtypes.bfloat16)
            out.append(np.stack([h,l]))
    mats=np.stack(out).reshape(2,2,2,256,256)
    k=np.arange(256)
    perm=np.zeros((256,256)); perm[k, (k%2)*128+k//2]=1
    return mats, perm.astype(ml_dtypes.bfloat16)

def split(x):
    h=x.astype(BF)
    return h,(x-h.astype(F32)).astype(BF)

def dot(a,b): return jnp.dot(a,b,preferred_element_type=F32)


RC=16
def left(mh,ml,h,l):
    return dot(mh,h)+dot(mh,l)+dot(ml,h)
def right(h,l,mh,ml):
    return dot(h,mh)+dot(l,mh)+dot(h,ml)

def wkernel(offs, cnt, ext, ill, mats, meas, grad, pterm, *bufs):
    n=cnt[0]
    @pl.loop(0,96)
    def _(i):
        for p in range(2):
            for t in range(6):
                grad[p,t,pl.ds(pl.multiple_of(8*i,8),8),:]=jnp.zeros((8,128),F32)
    pterm[...]=jnp.zeros_like(pterm)
    lane=lax.broadcasted_iota(jnp.int32,(RC,128),1)

    def phases(s, live, bset):
        patch, wave, h1, l1, m1, h2, l2, m2, h3, l3, m3, h4, l4, m4 = bset
        r=offs[0,s]; c=offs[1,s]
        ct=c//128; sh=c%128
        ush=(128-sh)%128
        lmask=lane<128-sh
        low=lane<sh
        def P1():
            for j in range(128//RC):
                half=[]
                for h in range(2):
                    row=h*128+j*RC
                    rr=pl.ds(row,RC)
                    x=[[pltpu.roll(ext[p,ct+t,pl.ds(r+row,RC),:],ush,1) for t in range(3)] for p in range(2)]
                    pt=[[jnp.where(lmask,x[p][t],x[p][t+1]) for t in range(2)] for p in range(2)]
                    ws=[]
                    for t in range(2):
                        ls=pl.ds(128*t,128)
                        pr,pi=ill[0,rr,ls],ill[1,rr,ls]
                        a,b=pt[0][t],pt[1][t]
                        patch[0,rr,ls]=a; patch[1,rr,ls]=b
                        wr=pr*a-pi*b; wi=pr*b+pi*a
                        wave[0,rr,ls]=wr; wave[1,rr,ls]=wi
                        ws.append((wr,wi))
                    half.append(ws)
                for t in range(2):
                    ls=pl.ds(128*t,128)
                    (ar,ai),(br,bi)=half[0][t],half[1][t]
                    for q,(xr,xi) in enumerate(((ar+br,ai+bi),(ar-br,ai-bi))):
                        for z,val in enumerate((xr,xi)):
                            hh,ll=split(val)
                            rs=pl.ds(z*128+j*RC,RC)
                            h1[q,rs,ls]=hh; l1[q,rs,ls]=ll
                yield
        def M1():
            for q in range(2):
                m1[q]=left(mats[q,1,0],mats[q,1,1],h1[q],l1[q]); yield
        def P2():
            for q in range(2):
                for j in range(128//RC):
                    ar=m1[q,pl.ds(j*RC,RC),pl.ds(0,128)]; br=m1[q,pl.ds(j*RC,RC),pl.ds(128,128)]
                    ai=m1[q,pl.ds(128+j*RC,RC),pl.ds(0,128)]; bi=m1[q,pl.ds(128+j*RC,RC),pl.ds(128,128)]
                    rs=pl.ds(q*128+j*RC,RC)
                    for e,(xr,xi) in enumerate(((ar+br,ai+bi),(ar-br,ai-bi))):
                        for z,val in enumerate((xr,xi)):
                            hh,ll=split(val)
                            h2[e,rs,pl.ds(128*z,128)]=hh; l2[e,rs,pl.ds(128*z,128)]=ll
                    yield
        def M2():
            for e in range(2):
                m2[e]=right(h2[e],l2[e],mats[e,0,0],mats[e,0,1]); yield
        def P3():
            for q in range(2):
                for e in range(2):
                    for j in range(128//RC):
                        rs=pl.ds(q*128+j*RC,RC)
                        fr=m2[e,rs,pl.ds(0,128)]; fi=m2[e,rs,pl.ds(128,128)]
                        f=meas[s,rs,pl.ds(e*128,128)]*lax.rsqrt(jnp.maximum(fr*fr+fi*fi,0.25))
                        for z,val in enumerate((fr*f,fi*f)):
                            hh,ll=split(val)
                            h3[e,rs,pl.ds(128*z,128)]=hh; l3[e,rs,pl.ds(128*z,128)]=ll
                        yield
        def M3():
            for e in range(2):
                m3[e]=right(h3[e],l3[e],mats[e,1,0],mats[e,1,1]); yield
        def P4():
            for q in range(2):
                for j in range(128//RC):
                    rs=pl.ds(q*128+j*RC,RC)
                    er=m3[0,rs,pl.ds(0,128)]; ei=m3[0,rs,pl.ds(128,128)]
                    vr=m3[1,rs,pl.ds(0,128)]; vi=m3[1,rs,pl.ds(128,128)]
                    for t,(xr,xi) in enumerate(((er+vr,ei+vi),(er-vr,ei-vi))):
                        for z,val in enumerate((xr,xi)):
                            hh,ll=split(val)
                            h4[q,pl.ds(z*128+j*RC,RC),pl.ds(128*t,128)]=hh
                            l4[q,pl.ds(z*128+j*RC,RC),pl.ds(128*t,128)]=ll
                    yield
        def M4():
            for q in range(2):
                m4[q]=left(mats[q,0,0],mats[q,0,1],h4[q],l4[q]); yield
        def P5():
            for j in range(128//RC):
                g=[[[None]*2 for _ in range(2)] for _ in range(2)]
                for t in range(2):
                    ls=pl.ds(128*t,128)
                    er=m4[0,pl.ds(j*RC,RC),ls]; ei=m4[0,pl.ds(128+j*RC,RC),ls]
                    vr=m4[1,pl.ds(j*RC,RC),ls]; vi=m4[1,pl.ds(128+j*RC,RC),ls]
                    for h,(xr,xi) in enumerate(((er+vr,ei+vi),(er-vr,ei-vi))):
                        rr=pl.ds(h*128+j*RC,RC)
                        cr=xr-wave[0,rr,ls]; ci=xi-wave[1,rr,ls]
                        if live is not None:
                            cr=cr*live; ci=ci*live
                        a,b=patch[0,rr,ls],patch[1,rr,ls]
                        pterm[0,t,rr,:]+=a*cr+b*ci
                        pterm[1,t,rr,:]+=a*ci-b*cr
                        pr,pi=ill[0,rr,ls],ill[1,rr,ls]
                        g[h][0][t]=pr*cr+pi*ci
                        g[h][1][t]=pr*ci-pi*cr
                for h in range(2):
                    for z in range(2):
                        rg=[pltpu.roll(g[h][z][t],sh,1) for t in range(2)]
                        rows=pl.ds(r+h*128+j*RC,RC)
                        grad[z,ct,rows,:]+=jnp.where(low,0.0,rg[0])
                        grad[z,ct+1,rows,:]+=jnp.where(low,rg[0],rg[1])
                        grad[z,ct+2,rows,:]+=jnp.where(low,rg[1],0.0)
                yield
        return P1,M1,P2,M2,P3,M3,P4,M4,P5

    def together(m, p):
        m, p = list_len(m), list_len(p)
        mi, pi_ = iter(m[0]()), iter(p[0]())
        for k in range(m[1]):
            next(mi, None)
            for _ in range(-(-p[1]//m[1])):
                next(pi_, None)
        for _ in mi: pass
        for _ in pi_: pass
    COUNT={"P1":128//RC,"P2":256//RC,"P3":512//RC,"P4":256//RC,"P5":128//RC,"M1":2,"M2":2,"M3":2,"M4":2}
    def list_len(f): return f, COUNT[f.__name__]
    def alone(f):
        for _ in f(): pass
    half=len(bufs)//2

    @pl.loop(0,(n+1)//2)
    def _(k):
        S=[]
        for i in range(2):
            s=jnp.minimum(2*k+i,15)
            live=None if i==0 else jnp.where(2*k+i<n,1.0,0.0).astype(F32)
            S.append(phases(s,live,bufs[half*i:half*(i+1)]))
        A,Bp=S
        alone(A[0])
        for i in range(4):
            together(A[2*i+1],Bp[2*i])
            together(Bp[2*i+1],A[2*i+2])
        alone(Bp[8])

def windows(offs,cnt,ext,ill,mats,meas):
    V=pl.BlockSpec(memory_space=pltpu.VMEM); Sm=pl.BlockSpec(memory_space=pltpu.SMEM)
    W=pltpu.VMEM((2,256,256),F32); Bq=pltpu.VMEM((2,256,256),BF)
    return pl.pallas_call(wkernel,
        out_shape=(jax.ShapeDtypeStruct((2,6,768,128),F32),jax.ShapeDtypeStruct((2,2,256,128),F32)),
        in_specs=[Sm,Sm,V,V,V,V],
        out_specs=(V,V),
        scratch_shapes=([W,W]+[Bq,Bq,W]*4)*2,
        compiler_params=pltpu.CompilerParams(vmem_limit_bytes=36*2**20),
    )(offs,cnt,ext,ill,mats,meas)


MESH = pl.DeviceIdType.MESH


def remote(src, dst, send_sem, recv_sem, device):
    return pltpu.make_async_remote_copy(
        src_ref=src, dst_ref=dst, send_sem=send_sem, recv_sem=recv_sem,
        device_id=device, device_id_type=MESH,
    )


def greet(devices):
    barrier = pltpu.get_barrier_semaphore()
    expected = 0
    for condition, device in devices:
        if condition is None:
            pl.semaphore_signal(barrier, inc=1, device_id=device, device_id_type=MESH)
            expected = expected + 1
        else:
            @pl.when(condition)
            def _(device=device):
                pl.semaphore_signal(barrier, inc=1, device_id=device, device_id_type=MESH)
            expected = expected + condition.astype(jnp.int32)
    return barrier, expected


def neighbours():
    a = lax.axis_index("ty")
    b = lax.axis_index("tx")
    has = {"up": a > 0, "down": a < 15, "left": b > 0, "right": b < 15}
    ids = {"up": (jnp.maximum(a - 1, 0), b), "down": (jnp.minimum(a + 1, 15), b),
           "left": (a, jnp.maximum(b - 1, 0)), "right": (a, jnp.minimum(b + 1, 15))}
    return a, b, has, ids


OPPOSITE = {"up": "down", "down": "up", "left": "right", "right": "left"}


def halo_kernel(tile, meas, perm, ext, sorted_meas, mbuf, meas_sem, own_sem, row_send, row_recv, col_send, col_recv, cor_send, cor_recv):
    a, b, has, ids = neighbours()
    barrier, expected = greet([(has[k], ids[k]) for k in ids])
    own = [pltpu.make_async_copy(tile.at[:, :, pl.ds(128 * t, 128)], ext.at[:, 1 + t, pl.ds(128, 512), :], own_sem.at[t]) for t in range(4)]
    for copy in own:
        copy.start()

    def fetch(s, t):
        return pltpu.make_async_copy(meas.at[s, :, pl.ds(128 * t, 128)], mbuf.at[s, t], meas_sem.at[s, t])

    @pl.loop(0, 16)
    def _(s):
        for t in range(2):
            fetch(s, t).start()

    pl.semaphore_wait(barrier, expected)
    rows, cols, corners = {}, {}, {}
    for i, way in enumerate(("down", "up")):
        src_row, dst_row = (384, 0) if way == "down" else (0, 640)
        for t in (0, 3, 1, 2):
            rows[way, t] = remote(
                tile.at[:, pl.ds(src_row, 128), pl.ds(128 * t, 128)],
                ext.at[:, 1 + t, pl.ds(dst_row, 128), :],
                row_send.at[i, t], row_recv.at[i, t], ids[way])
    for i, way in enumerate(("right", "left")):
        src_t, dst_t = (3, 0) if way == "right" else (0, 5)
        cols[way] = remote(
            tile.at[:, :, pl.ds(128 * src_t, 128)], ext.at[:, dst_t, pl.ds(128, 512), :],
            col_send.at[i], col_recv.at[i], ids[way])
        for j, row in enumerate((0, 640)):
            corners[way, j] = remote(
                ext.at[:, 1 + src_t, pl.ds(row, 128), :], ext.at[:, dst_t, pl.ds(row, 128), :],
                cor_send.at[i, j], cor_recv.at[i, j], ids[way])
    for t in (0, 3, 1, 2):
        for way in ("down", "up"):
            pl.when(has[way])(rows[way, t].start)
    for way in ("right", "left"):
        pl.when(has[way])(cols[way].start)

    @pl.loop(0, 16)
    def _(s):
        for t in range(2):
            fetch(s, t).wait()
        for q in range(2):
            picked = jnp.concatenate([mbuf[s, t, pl.ds(q, 128, stride=2), :] for t in range(2)], axis=1)
            high, low = split(picked)
            sorted_meas[s, pl.ds(128 * q, 128), :] = dot(high, perm[...]) + dot(low, perm[...])

    for j, way in enumerate(("down", "up")):
        @pl.when(has[OPPOSITE[way]])
        def _(way=way):
            rows[way, 0].wait_recv()
            rows[way, 3].wait_recv()
        for side in ("right", "left"):
            pl.when(jnp.logical_and(has[side], has[OPPOSITE[way]]))(corners[side, j].start)
    for copy in own:
        copy.wait()
    for way in ("down", "up"):
        for t in (1, 2):
            pl.when(has[OPPOSITE[way]])(rows[way, t].wait_recv)
        for t in range(4):
            pl.when(has[way])(rows[way, t].wait_send)
    for side in ("right", "left"):
        pl.when(has[OPPOSITE[side]])(cols[side].wait_recv)
        pl.when(has[side])(cols[side].wait_send)
        for j, way in enumerate(("down", "up")):
            pl.when(jnp.logical_and(has[OPPOSITE[side]], has[OPPOSITE[way]]))(corners[side, j].wait_recv)
            pl.when(jnp.logical_and(has[side], has[OPPOSITE[way]]))(corners[side, j].wait_send)


def halo(tile, meas, perm):
    D = pltpu.SemaphoreType.DMA
    H = pl.BlockSpec(memory_space=pltpu.HBM)
    V = pl.BlockSpec(memory_space=pltpu.VMEM)
    return pl.pallas_call(
        halo_kernel,
        out_shape=(jax.ShapeDtypeStruct((2, 6, 768, 128), F32), jax.ShapeDtypeStruct((16, 256, 256), F32)),
        in_specs=[H, H, V], out_specs=(V, V),
        scratch_shapes=[pltpu.VMEM((16, 2, 256, 128), F32), D((16, 2)),
                        D((4,)), D((2, 4)), D((2, 4)), D((2,)), D((2,)), D((2, 2)), D((2, 2))],
        compiler_params=pltpu.CompilerParams(collective_id=1, has_side_effects=True, vmem_limit_bytes=24 * 2**20),
    )(tile, meas, perm)


def partners(b):
    core = b % 2
    x = (b // 2) % 4
    zlo = b // 8
    return core, x, zlo


def finish_kernel(spec, ill, grad, pterm, newspec, newill,
                  rxc, rxm, rz, edge, rcore, rx, sumc, part, rc, total,
                  core_s, core_r, xs, xr, cs, cr, ms, mr, zs, zr,
                  us, ur, ds, dr, es, er, fs, fr):
    a, b, has, ids = neighbours()
    core, x, zlo = partners(b)
    low = x * 2 + core
    unit = zlo * 16 + a

    def member(d):
        u = (unit + d) % 32
        return (u % 16, (u // 16) * 8 + low)

    mates = [(a, zlo * 8 + ((x + d) % 4) * 2 + core) for d in (1, 2, 3)]
    other = (a, zlo * 8 + x * 2 + (1 - core))
    barrier, expected = greet([(None, m) for m in mates] + [(None, other)]
                              + [(jnp.logical_and(core == 0, has["left"]), ids["left"]),
                                 (jnp.logical_and(core == 1, has["right"]), ids["right"])])

    @pl.loop(1, 32)
    def _(d):
        pl.semaphore_signal(barrier, inc=1, device_id=member(d), device_id_type=MESH)

    power = jnp.sum(ill[0] * ill[0] + ill[1] * ill[1]) * (1.0 / 65536) + 1e-05
    inv = 1.0 / power
    pl.semaphore_wait(barrier, expected + 31)
    first = remote(pterm.at[1 - core], rcore, core_s, core_r, other)
    first.start()
    corner, middle, zmid, zedge = {}, {}, {}, {}
    for i, side in enumerate(("right", "left")):
        src_t = 5 if side == "right" else 0
        for j, row in enumerate((0, 640)):
            corner[side, j] = remote(grad.at[:, src_t, pl.ds(row, 128), :], rxc.at[i, j],
                                     cs.at[i, j], cr.at[i, j], ids[side])
        middle[side] = remote(grad.at[:, src_t, pl.ds(128, 512), :], rxm.at[i], ms.at[i], mr.at[i], ids[side])
    for j, way in enumerate(("up", "down")):
        row = 0 if way == "up" else 640
        zmid[way] = remote(grad.at[:, pl.ds(2, 2), pl.ds(row, 128), :], rz.at[j, :, pl.ds(1, 2)],
                           zs.at[j, 1], zr.at[j, 1], ids[way])
        for k, t in ((0, 0), (2, 3)):
            zedge[way, k] = remote(edge.at[j, k // 2], rz.at[j, :, t], zs.at[j, k], zr.at[j, k], ids[way])
    for side in ("right", "left"):
        for j in range(2):
            pl.when(has[side])(corner[side, j].start)
    for way in ("up", "down"):
        pl.when(has[way])(zmid[way].start)
    first.wait_recv()
    sumc[...] = pterm[core] + rcore[...]
    xsend = [remote(sumc.at[(x + d) % 4], rx.at[d - 1], xs.at[d - 1], xr.at[d - 1], mates[d - 1]) for d in (1, 2, 3)]
    for copy in xsend:
        copy.start()
    for side in ("right", "left"):
        pl.when(has[side])(middle[side].start)
    for j, row in enumerate((0, 640)):
        for k, (t, side) in enumerate(((1, "right"), (4, "left"))):
            edge[j, k] = grad[:, t, row:row + 128, :]
            @pl.when(has[OPPOSITE[side]])
            def _(j=j, k=k, side=side):
                corner[side, j].wait_recv()
                edge[j, k] += rxc[k, j]
            way = "up" if j == 0 else "down"
            pl.when(has[way])(zedge[way, 2 * k].start)
    for copy in xsend:
        copy.wait_recv()
    part[...] = sumc[x] + rx[0] + rx[1] + rx[2]

    @pl.loop(1, 32)
    def _(d):
        device = member(d)
        remote(part.at[device[0]], rc.at[d - 1], us, ur, device).start()

    @pl.loop(0, 16)
    def _(i):
        rows = pl.ds(pl.multiple_of(32 * i, 32), 32)
        more = pl.ds(pl.multiple_of(32 * i + 128, 32), 32)
        for p in range(2):
            for t in range(4):
                lanes = pl.ds(128 * t, 128)
                newspec[p, rows, lanes] = spec[p, rows, lanes] + inv * grad[p, 1 + t, more, :]

    whole = remote(rc, rc, us, ur, other)
    whole.wait_recv()
    acc = part[a]
    for i in range(31):
        acc = acc + rc[i]
    total[core, x, a] = acc

    @pl.loop(1, 16)
    def _(d):
        remote(total.at[core, x, a], total.at[core, x, a], ds, dr, ((a + d) % 16, b)).start()

    for k, (side, t) in enumerate((("right", 0), ("left", 3))):
        @pl.when(has[OPPOSITE[side]])
        def _(k=k, side=side, t=t):
            middle[side].wait_recv()
            newspec[:, :, 128 * t:128 * t + 128] += inv * rxm[k]
    some = remote(rc.at[pl.ds(0, 15)], rc.at[pl.ds(0, 15)], ds, dr, other)
    some.wait_recv()
    gather = [remote(total.at[core, x], total.at[core, x], es.at[d - 1], er.at[d - 1], mates[d - 1]) for d in (1, 2, 3)]
    for copy in gather:
        copy.start()
    for copy in gather:
        copy.wait_recv()
    last = remote(total.at[core], total.at[core], fs, fr, other)
    last.start()
    for j, (way, row) in enumerate((("up", 384), ("down", 0))):
        @pl.when(has[OPPOSITE[way]])
        def _(j=j, way=way, row=row):
            zmid[way].wait_recv()
            zedge[way, 0].wait_recv()
            zedge[way, 2].wait_recv()
            for t in range(4):
                newspec[:, row:row + 128, 128 * t:128 * t + 128] += inv * rz[j, :, t]
    last.wait()
    for p in range(2):
        for s in range(4):
            rows, lanes = pl.ds((s % 2) * 128, 128), pl.ds((s // 2) * 128, 128)
            newill[p, rows, lanes] = ill[p, rows, lanes] + total[p, s].reshape(128, 128) * (1.0 / 64)
    first.wait_send()
    for copy in xsend + gather:
        copy.wait_send()
    whole.wait_send()
    some.wait_send()
    for side in ("right", "left"):
        for j in range(2):
            pl.when(has[side])(corner[side, j].wait_send)
        pl.when(has[side])(middle[side].wait_send)
    for way in ("up", "down"):
        pl.when(has[way])(zmid[way].wait_send)
        for k in (0, 2):
            pl.when(has[way])(zedge[way, k].wait_send)


def finish(spec, ill, grad, pterm):
    D = pltpu.SemaphoreType.DMA
    V = pl.BlockSpec(memory_space=pltpu.VMEM)
    return pl.pallas_call(
        finish_kernel,
        out_shape=(jax.ShapeDtypeStruct((2, 512, 512), F32), jax.ShapeDtypeStruct((2, 256, 256), F32)),
        in_specs=[V, V, V, V], out_specs=(V, V),
        scratch_shapes=[
            pltpu.VMEM((2, 2, 2, 128, 128), F32), pltpu.VMEM((2, 2, 512, 128), F32),
            pltpu.VMEM((2, 2, 4, 128, 128), F32), pltpu.VMEM((2, 2, 2, 128, 128), F32),
            pltpu.VMEM((4, 16, 8, 128), F32), pltpu.VMEM((3, 16, 8, 128), F32), pltpu.VMEM((4, 16, 8, 128), F32),
            pltpu.VMEM((16, 8, 128), F32), pltpu.VMEM((31, 8, 128), F32), pltpu.VMEM((2, 4, 16, 8, 128), F32),
            D, D, D((3,)), D((3,)), D((2, 2)), D((2, 2)), D((2,)), D((2,)), D((2, 3)), D((2, 3)),
            D, D, D, D, D((3,)), D((3,)), D, D,
        ],
        compiler_params=pltpu.CompilerParams(collective_id=2, has_side_effects=True, vmem_limit_bytes=32 * 2**20),
    )(spec, ill, grad, pterm)


def shards(specimen, illumination, scan_offsets, slot_counts, measured):
    anchor = jnp.stack([lax.axis_index("ty") * 512, lax.axis_index("tx") * 512]) - 128
    local = scan_offsets[0, 0] - anchor[:, None]
    mats, perm = consts()
    ext, moduli = halo(specimen, measured[0, 0], jnp.asarray(perm))
    grad, probe_term = windows(local, slot_counts[0], ext, illumination, jnp.asarray(mats), moduli)
    return finish(specimen, illumination, grad, probe_term.reshape(2, 4, 16, 8, 128))


def solution(mesh):
    in_specs = (
        P(None, "ty", "tx"),
        P(),
        P("ty", "tx", None, None),
        P("ty", "tx"),
        P("ty", "tx", None, None, None),
    )
    out_specs = (P(None, "ty", "tx"), P())
    return jax.shard_map(shards, mesh=mesh, in_specs=in_specs, out_specs=out_specs, check_vma=False)
```

```python
import math
import numpy as np
import jax, jax.numpy as jnp
from jax import lax
from jax.experimental import pallas as pl
from jax.experimental.pallas import tpu as pltpu
import ml_dtypes
from jax.sharding import PartitionSpec as P

F32=jnp.float32; BF=jnp.bfloat16

def consts():
    n=np.arange(128)
    out=[]
    for odd in (0,1):
        phase=np.outer(n,2*n+odd)%256
        ang=2*np.pi*phase/256
        tr,ti=np.cos(ang)/16,-np.sin(ang)/16
        r=np.block([[tr,ti],[-ti,tr]])
        for m in (r,r.T):
            m=m.astype(np.float32)
            h=m.astype(ml_dtypes.bfloat16); l=(m-h.astype(np.float32)).astype(ml_dtypes.bfloat16)
            out.append(np.stack([h,l]))
    mats=np.stack(out).reshape(2,2,2,256,256)
    k=np.arange(256)
    perm=np.zeros((256,256)); perm[k, (k%2)*128+k//2]=1
    return mats, perm.astype(ml_dtypes.bfloat16)

def split(x):
    h=x.astype(BF)
    return h,(x-h.astype(F32)).astype(BF)

def dot(a,b): return jnp.dot(a,b,preferred_element_type=F32)


RC=16
def left(mh,ml,h,l):
    return dot(mh,h)+dot(mh,l)+dot(ml,h)
def right(h,l,mh,ml):
    return dot(h,mh)+dot(l,mh)+dot(h,ml)

def wkernel(offs, cnt, ext, ill, mats, meas, grad, pterm, *bufs):
    n=cnt[0]
    @pl.loop(0,96)
    def _(i):
        for p in range(2):
            for t in range(6):
                grad[p,t,pl.ds(pl.multiple_of(8*i,8),8),:]=jnp.zeros((8,128),F32)
    pterm[...]=jnp.zeros_like(pterm)
    lane=lax.broadcasted_iota(jnp.int32,(RC,128),1)

    def phases(s, live, bset):
        patch, wave, h1, l1, m1, h2, l2, m2, h3, l3, m3, h4, l4, m4 = bset
        r=offs[0,s]; c=offs[1,s]
        ct=c//128; sh=c%128
        ush=(128-sh)%128
        lmask=lane<128-sh
        low=lane<sh
        def P1():
            for j in range(128//RC):
                half=[]
                for h in range(2):
                    row=h*128+j*RC
                    rr=pl.ds(row,RC)
                    x=[[pltpu.roll(ext[p,ct+t,pl.ds(r+row,RC),:],ush,1) for t in range(3)] for p in range(2)]
                    pt=[[jnp.where(lmask,x[p][t],x[p][t+1]) for t in range(2)] for p in range(2)]
                    ws=[]
                    for t in range(2):
                        ls=pl.ds(128*t,128)
                        pr,pi=ill[0,rr,ls],ill[1,rr,ls]
                        a,b=pt[0][t],pt[1][t]
                        patch[0,rr,ls]=a; patch[1,rr,ls]=b
                        wr=pr*a-pi*b; wi=pr*b+pi*a
                        wave[0,rr,ls]=wr; wave[1,rr,ls]=wi
                        ws.append((wr,wi))
                    half.append(ws)
                for t in range(2):
                    ls=pl.ds(128*t,128)
                    (ar,ai),(br,bi)=half[0][t],half[1][t]
                    for q,(xr,xi) in enumerate(((ar+br,ai+bi),(ar-br,ai-bi))):
                        for z,val in enumerate((xr,xi)):
                            hh,ll=split(val)
                            rs=pl.ds(z*128+j*RC,RC)
                            h1[q,rs,ls]=hh; l1[q,rs,ls]=ll
                yield
        def M1():
            for q in range(2):
                m1[q]=left(mats[q,1,0],mats[q,1,1],h1[q],l1[q]); yield
        def P2():
            for q in range(2):
                for j in range(128//RC):
                    ar=m1[q,pl.ds(j*RC,RC),pl.ds(0,128)]; br=m1[q,pl.ds(j*RC,RC),pl.ds(128,128)]
                    ai=m1[q,pl.ds(128+j*RC,RC),pl.ds(0,128)]; bi=m1[q,pl.ds(128+j*RC,RC),pl.ds(128,128)]
                    rs=pl.ds(q*128+j*RC,RC)
                    for e,(xr,xi) in enumerate(((ar+br,ai+bi),(ar-br,ai-bi))):
                        for z,val in enumerate((xr,xi)):
                            hh,ll=split(val)
                            h2[e,rs,pl.ds(128*z,128)]=hh; l2[e,rs,pl.ds(128*z,128)]=ll
                    yield
        def M2():
            for e in range(2):
                m2[e]=right(h2[e],l2[e],mats[e,0,0],mats[e,0,1]); yield
        def P3():
            for q in range(2):
                for e in range(2):
                    for j in range(128//RC):
                        rs=pl.ds(q*128+j*RC,RC)
                        fr=m2[e,rs,pl.ds(0,128)]; fi=m2[e,rs,pl.ds(128,128)]
                        f=meas[s,rs,pl.ds(e*128,128)]*lax.rsqrt(jnp.maximum(fr*fr+fi*fi,0.25))
                        for z,val in enumerate((fr*f,fi*f)):
                            hh,ll=split(val)
                            h3[e,rs,pl.ds(128*z,128)]=hh; l3[e,rs,pl.ds(128*z,128)]=ll
                        yield
        def M3():
            for e in range(2):
                m3[e]=right(h3[e],l3[e],mats[e,1,0],mats[e,1,1]); yield
        def P4():
            for q in range(2):
                for j in range(128//RC):
                    rs=pl.ds(q*128+j*RC,RC)
                    er=m3[0,rs,pl.ds(0,128)]; ei=m3[0,rs,pl.ds(128,128)]
                    vr=m3[1,rs,pl.ds(0,128)]; vi=m3[1,rs,pl.ds(128,128)]
                    for t,(xr,xi) in enumerate(((er+vr,ei+vi),(er-vr,ei-vi))):
                        for z,val in enumerate((xr,xi)):
                            hh,ll=split(val)
                            h4[q,pl.ds(z*128+j*RC,RC),pl.ds(128*t,128)]=hh
                            l4[q,pl.ds(z*128+j*RC,RC),pl.ds(128*t,128)]=ll
                    yield
        def M4():
            for q in range(2):
                m4[q]=left(mats[q,0,0],mats[q,0,1],h4[q],l4[q]); yield
        def P5():
            for j in range(128//RC):
                g=[[[None]*2 for _ in range(2)] for _ in range(2)]
                for t in range(2):
                    ls=pl.ds(128*t,128)
                    er=m4[0,pl.ds(j*RC,RC),ls]; ei=m4[0,pl.ds(128+j*RC,RC),ls]
                    vr=m4[1,pl.ds(j*RC,RC),ls]; vi=m4[1,pl.ds(128+j*RC,RC),ls]
                    for h,(xr,xi) in enumerate(((er+vr,ei+vi),(er-vr,ei-vi))):
                        rr=pl.ds(h*128+j*RC,RC)
                        cr=xr-wave[0,rr,ls]; ci=xi-wave[1,rr,ls]
                        if live is not None:
                            cr=cr*live; ci=ci*live
                        a,b=patch[0,rr,ls],patch[1,rr,ls]
                        pterm[0,t,rr,:]+=a*cr+b*ci
                        pterm[1,t,rr,:]+=a*ci-b*cr
                        pr,pi=ill[0,rr,ls],ill[1,rr,ls]
                        g[h][0][t]=pr*cr+pi*ci
                        g[h][1][t]=pr*ci-pi*cr
                for h in range(2):
                    for z in range(2):
                        rg=[pltpu.roll(g[h][z][t],sh,1) for t in range(2)]
                        rows=pl.ds(r+h*128+j*RC,RC)
                        grad[z,ct,rows,:]+=jnp.where(low,0.0,rg[0])
                        grad[z,ct+1,rows,:]+=jnp.where(low,rg[0],rg[1])
                        grad[z,ct+2,rows,:]+=jnp.where(low,rg[1],0.0)
                yield
        return P1,M1,P2,M2,P3,M3,P4,M4,P5

    def together(m, p):
        m, p = list_len(m), list_len(p)
        mi, pi_ = iter(m[0]()), iter(p[0]())
        for k in range(m[1]):
            next(mi, None)
            for _ in range(-(-p[1]//m[1])):
                next(pi_, None)
        for _ in mi: pass
        for _ in pi_: pass
    COUNT={"P1":128//RC,"P2":256//RC,"P3":512//RC,"P4":256//RC,"P5":128//RC,"M1":2,"M2":2,"M3":2,"M4":2}
    def list_len(f): return f, COUNT[f.__name__]
    def alone(f):
        for _ in f(): pass
    half=len(bufs)//2

    @pl.loop(0,(n+1)//2)
    def _(k):
        S=[]
        for i in range(2):
            s=jnp.minimum(2*k+i,15)
            live=None if i==0 else jnp.where(2*k+i<n,1.0,0.0).astype(F32)
            S.append(phases(s,live,bufs[half*i:half*(i+1)]))
        A,Bp=S
        alone(A[0])
        for i in range(4):
            together(A[2*i+1],Bp[2*i])
            together(Bp[2*i+1],A[2*i+2])
        alone(Bp[8])

def windows(offs,cnt,ext,ill,mats,meas):
    V=pl.BlockSpec(memory_space=pltpu.VMEM); Sm=pl.BlockSpec(memory_space=pltpu.SMEM)
    W=pltpu.VMEM((2,256,256),F32); Bq=pltpu.VMEM((2,256,256),BF)
    return pl.pallas_call(wkernel,
        out_shape=(jax.ShapeDtypeStruct((2,6,768,128),F32),jax.ShapeDtypeStruct((2,2,256,128),F32)),
        in_specs=[Sm,Sm,V,V,V,V],
        out_specs=(V,V),
        scratch_shapes=([W,W]+[Bq,Bq,W]*4)*2,
        compiler_params=pltpu.CompilerParams(vmem_limit_bytes=36*2**20),
    )(offs,cnt,ext,ill,mats,meas)


MESH = pl.DeviceIdType.MESH


def remote(src, dst, send_sem, recv_sem, device):
    return pltpu.make_async_remote_copy(
        src_ref=src, dst_ref=dst, send_sem=send_sem, recv_sem=recv_sem,
        device_id=device, device_id_type=MESH,
    )


def greet(devices):
    barrier = pltpu.get_barrier_semaphore()
    expected = 0
    for condition, device in devices:
        if condition is None:
            pl.semaphore_signal(barrier, inc=1, device_id=device, device_id_type=MESH)
            expected = expected + 1
        else:
            @pl.when(condition)
            def _(device=device):
                pl.semaphore_signal(barrier, inc=1, device_id=device, device_id_type=MESH)
            expected = expected + condition.astype(jnp.int32)
    return barrier, expected


def neighbours():
    a = lax.axis_index("ty")
    b = lax.axis_index("tx")
    has = {"up": a > 0, "down": a < 15, "left": b > 0, "right": b < 15}
    ids = {"up": (jnp.maximum(a - 1, 0), b), "down": (jnp.minimum(a + 1, 15), b),
           "left": (a, jnp.maximum(b - 1, 0)), "right": (a, jnp.minimum(b + 1, 15))}
    return a, b, has, ids


OPPOSITE = {"up": "down", "down": "up", "left": "right", "right": "left"}


def halo_kernel(tile, meas, perm, ext, sorted_meas, mbuf, meas_sem, own_sem, row_send, row_recv, col_send, col_recv, cor_send, cor_recv):
    a, b, has, ids = neighbours()
    barrier, expected = greet([(has[k], ids[k]) for k in ids])
    own = [pltpu.make_async_copy(tile.at[:, :, pl.ds(128 * t, 128)], ext.at[:, 1 + t, pl.ds(128, 512), :], own_sem.at[t]) for t in range(4)]
    for copy in own:
        copy.start()

    def fetch(s, t):
        return pltpu.make_async_copy(meas.at[s, :, pl.ds(128 * t, 128)], mbuf.at[s, t], meas_sem.at[s, t])

    @pl.loop(0, 16)
    def _(s):
        for t in range(2):
            fetch(s, t).start()

    pl.semaphore_wait(barrier, expected)
    rows, cols, corners = {}, {}, {}
    for i, way in enumerate(("down", "up")):
        src_row, dst_row = (384, 0) if way == "down" else (0, 640)
        for t in (0, 3, 1, 2):
            rows[way, t] = remote(
                tile.at[:, pl.ds(src_row, 128), pl.ds(128 * t, 128)],
                ext.at[:, 1 + t, pl.ds(dst_row, 128), :],
                row_send.at[i, t], row_recv.at[i, t], ids[way])
    for i, way in enumerate(("right", "left")):
        src_t, dst_t = (3, 0) if way == "right" else (0, 5)
        cols[way] = remote(
            tile.at[:, :, pl.ds(128 * src_t, 128)], ext.at[:, dst_t, pl.ds(128, 512), :],
            col_send.at[i], col_recv.at[i], ids[way])
        for j, row in enumerate((0, 640)):
            corners[way, j] = remote(
                ext.at[:, 1 + src_t, pl.ds(row, 128), :], ext.at[:, dst_t, pl.ds(row, 128), :],
                cor_send.at[i, j], cor_recv.at[i, j], ids[way])
    for t in (0, 3, 1, 2):
        for way in ("down", "up"):
            pl.when(has[way])(rows[way, t].start)
    for way in ("right", "left"):
        pl.when(has[way])(cols[way].start)

    @pl.loop(0, 16)
    def _(s):
        for t in range(2):
            fetch(s, t).wait()
        for q in range(2):
            picked = jnp.concatenate([mbuf[s, t, pl.ds(q, 128, stride=2), :] for t in range(2)], axis=1)
            high, low = split(picked)
            sorted_meas[s, pl.ds(128 * q, 128), :] = dot(high, perm[...]) + dot(low, perm[...])

    for j, way in enumerate(("down", "up")):
        @pl.when(has[OPPOSITE[way]])
        def _(way=way):
            rows[way, 0].wait_recv()
            rows[way, 3].wait_recv()
        for side in ("right", "left"):
            pl.when(jnp.logical_and(has[side], has[OPPOSITE[way]]))(corners[side, j].start)
    for copy in own:
        copy.wait()
    for way in ("down", "up"):
        for t in (1, 2):
            pl.when(has[OPPOSITE[way]])(rows[way, t].wait_recv)
        for t in range(4):
            pl.when(has[way])(rows[way, t].wait_send)
    for side in ("right", "left"):
        pl.when(has[OPPOSITE[side]])(cols[side].wait_recv)
        pl.when(has[side])(cols[side].wait_send)
        for j, way in enumerate(("down", "up")):
            pl.when(jnp.logical_and(has[OPPOSITE[side]], has[OPPOSITE[way]]))(corners[side, j].wait_recv)
            pl.when(jnp.logical_and(has[side], has[OPPOSITE[way]]))(corners[side, j].wait_send)


def halo(tile, meas, perm):
    D = pltpu.SemaphoreType.DMA
    H = pl.BlockSpec(memory_space=pltpu.HBM)
    V = pl.BlockSpec(memory_space=pltpu.VMEM)
    return pl.pallas_call(
        halo_kernel,
        out_shape=(jax.ShapeDtypeStruct((2, 6, 768, 128), F32), jax.ShapeDtypeStruct((16, 256, 256), F32)),
        in_specs=[H, H, V], out_specs=(V, V),
        scratch_shapes=[pltpu.VMEM((16, 2, 256, 128), F32), D((16, 2)),
                        D((4,)), D((2, 4)), D((2, 4)), D((2,)), D((2,)), D((2, 2)), D((2, 2))],
        compiler_params=pltpu.CompilerParams(collective_id=1, has_side_effects=True, vmem_limit_bytes=24 * 2**20),
    )(tile, meas, perm)


def partners(b):
    core = b % 2
    x = (b // 2) % 4
    zlo = b // 8
    return core, x, zlo


def finish_kernel(spec, ill, grad, pterm, newspec, newill,
                  rxc, rxm, rz, edge, rcore, rx, sumc, part, rc, total,
                  core_s, core_r, xs, xr, cs, cr, ms, mr, zs, zr,
                  us, ur, ds, dr, es, er, fs, fr):
    a, b, has, ids = neighbours()
    core, x, zlo = partners(b)
    low = x * 2 + core
    unit = zlo * 16 + a

    def member(d):
        u = (unit + d) % 32
        return (u % 16, (u // 16) * 8 + low)

    mates = [(a, zlo * 8 + ((x + d) % 4) * 2 + core) for d in (1, 2, 3)]
    other = (a, zlo * 8 + x * 2 + (1 - core))
    barrier, expected = greet([(None, m) for m in mates] + [(None, other)]
                              + [(jnp.logical_and(core == 0, has["left"]), ids["left"]),
                                 (jnp.logical_and(core == 1, has["right"]), ids["right"])])

    @pl.loop(1, 32)
    def _(d):
        pl.semaphore_signal(barrier, inc=1, device_id=member(d), device_id_type=MESH)

    power = jnp.sum(ill[0] * ill[0] + ill[1] * ill[1]) * (1.0 / 65536) + 1e-05
    inv = 1.0 / power
    pl.semaphore_wait(barrier, expected + 31)
    first = remote(pterm.at[1 - core], rcore, core_s, core_r, other)
    corner, middle, vert = {}, {}, {}
    for i, side in enumerate(("right", "left")):
        src_t = 5 if side == "right" else 0
        for j, row in enumerate((0, 640)):
            corner[side, j] = remote(grad.at[:, src_t, pl.ds(row, 128), :], rxc.at[i, j],
                                     cs.at[i, j], cr.at[i, j], ids[side])
        middle[side] = remote(grad.at[:, src_t, pl.ds(128, 512), :], rxm.at[i], ms.at[i], mr.at[i], ids[side])
    for j, way in enumerate(("up", "down")):
        row = 0 if way == "up" else 640
        for t in range(4):
            src = edge.at[j, t // 3] if t in (0, 3) else grad.at[:, 1 + t, pl.ds(row, 128), :]
            vert[way, t] = remote(src, rz.at[j, :, t], zs.at[j, t], zr.at[j, t], ids[way])

    def send_vert(t):
        for way in ("up", "down"):
            pl.when(has[way])(vert[way, t].start)

    def add_vert(t):
        for j, (way, row) in enumerate((("up", 384), ("down", 0))):
            @pl.when(has[OPPOSITE[way]])
            def _(j=j, way=way, row=row):
                vert[way, t].wait_recv()
                newspec[:, row:row + 128, 128 * t:128 * t + 128] += inv * rz[j, :, t]

    first.start()
    send_vert(1)
    first.wait_recv()
    sumc[...] = pterm[core] + rcore[...]
    xsend = [remote(sumc.at[(x + d) % 4], rx.at[d - 1], xs.at[d - 1], xr.at[d - 1], mates[d - 1]) for d in (1, 2, 3)]
    for copy in xsend:
        copy.start()
    for side in ("right", "left"):
        for j in range(2):
            pl.when(has[side])(corner[side, j].start)
    for copy in xsend:
        copy.wait_recv()
    part[...] = sumc[x] + rx[0] + rx[1] + rx[2]

    @pl.loop(1, 32)
    def _(d):
        device = member(d)
        remote(part.at[device[0]], rc.at[d - 1], us, ur, device).start()

    send_vert(2)
    for side in ("right", "left"):
        pl.when(has[side])(middle[side].start)

    @pl.loop(0, 16)
    def _(i):
        rows = pl.ds(pl.multiple_of(32 * i, 32), 32)
        more = pl.ds(pl.multiple_of(32 * i + 128, 32), 32)
        for p in range(2):
            for t in range(4):
                lanes = pl.ds(128 * t, 128)
                newspec[p, rows, lanes] = spec[p, rows, lanes] + inv * grad[p, 1 + t, more, :]

    for j, row in enumerate((0, 640)):
        for k, (t, side) in enumerate(((1, "right"), (4, "left"))):
            edge[j, k] = grad[:, t, row:row + 128, :]
            @pl.when(has[OPPOSITE[side]])
            def _(j=j, k=k, side=side):
                corner[side, j].wait_recv()
                edge[j, k] += rxc[k, j]
    whole = remote(rc, rc, us, ur, other)
    whole.wait_recv()
    acc = part[a]
    for i in range(31):
        acc = acc + rc[i]
    total[core, x, a] = acc

    @pl.loop(1, 16)
    def _(d):
        remote(total.at[core, x, a], total.at[core, x, a], ds, dr, ((a + d) % 16, b)).start()

    send_vert(0)
    send_vert(3)
    for k, (side, t) in enumerate((("right", 0), ("left", 3))):
        @pl.when(has[OPPOSITE[side]])
        def _(k=k, side=side, t=t):
            middle[side].wait_recv()
            newspec[:, :, 128 * t:128 * t + 128] += inv * rxm[k]
    some = remote(rc.at[pl.ds(0, 15)], rc.at[pl.ds(0, 15)], ds, dr, other)
    some.wait_recv()
    gather = [remote(total.at[core, x], total.at[core, x], es.at[d - 1], er.at[d - 1], mates[d - 1]) for d in (1, 2, 3)]
    for copy in gather:
        copy.start()
    add_vert(1)
    add_vert(2)
    for copy in gather:
        copy.wait_recv()
    last = remote(total.at[core], total.at[core], fs, fr, other)
    last.start()
    last.wait()
    for p in range(2):
        for s in range(4):
            rows, lanes = pl.ds((s % 2) * 128, 128), pl.ds((s // 2) * 128, 128)
            newill[p, rows, lanes] = ill[p, rows, lanes] + total[p, s].reshape(128, 128) * (1.0 / 64)
    add_vert(0)
    add_vert(3)
    first.wait_send()
    for copy in xsend + gather:
        copy.wait_send()
    whole.wait_send()
    some.wait_send()
    for side in ("right", "left"):
        for j in range(2):
            pl.when(has[side])(corner[side, j].wait_send)
        pl.when(has[side])(middle[side].wait_send)
    for way in ("up", "down"):
        for t in range(4):
            pl.when(has[way])(vert[way, t].wait_send)


def finish(spec, ill, grad, pterm):
    D = pltpu.SemaphoreType.DMA
    V = pl.BlockSpec(memory_space=pltpu.VMEM)
    return pl.pallas_call(
        finish_kernel,
        out_shape=(jax.ShapeDtypeStruct((2, 512, 512), F32), jax.ShapeDtypeStruct((2, 256, 256), F32)),
        in_specs=[V, V, V, V], out_specs=(V, V),
        scratch_shapes=[
            pltpu.VMEM((2, 2, 2, 128, 128), F32), pltpu.VMEM((2, 2, 512, 128), F32),
            pltpu.VMEM((2, 2, 4, 128, 128), F32), pltpu.VMEM((2, 2, 2, 128, 128), F32),
            pltpu.VMEM((4, 16, 8, 128), F32), pltpu.VMEM((3, 16, 8, 128), F32), pltpu.VMEM((4, 16, 8, 128), F32),
            pltpu.VMEM((16, 8, 128), F32), pltpu.VMEM((31, 8, 128), F32), pltpu.VMEM((2, 4, 16, 8, 128), F32),
            D, D, D((3,)), D((3,)), D((2, 2)), D((2, 2)), D((2,)), D((2,)), D((2, 4)), D((2, 4)),
            D, D, D, D, D((3,)), D((3,)), D, D,
        ],
        compiler_params=pltpu.CompilerParams(collective_id=2, has_side_effects=True, vmem_limit_bytes=32 * 2**20),
    )(spec, ill, grad, pterm)


def shards(specimen, illumination, scan_offsets, slot_counts, measured):
    anchor = jnp.stack([lax.axis_index("ty") * 512, lax.axis_index("tx") * 512]) - 128
    local = scan_offsets[0, 0] - anchor[:, None]
    mats, perm = consts()
    ext, moduli = halo(specimen, measured[0, 0], jnp.asarray(perm))
    grad, probe_term = windows(local, slot_counts[0], ext, illumination, jnp.asarray(mats), moduli)
    return finish(specimen, illumination, grad, probe_term.reshape(2, 4, 16, 8, 128))


def solution(mesh):
    in_specs = (
        P(None, "ty", "tx"),
        P(),
        P("ty", "tx", None, None),
        P("ty", "tx"),
        P("ty", "tx", None, None, None),
    )
    out_specs = (P(None, "ty", "tx"), P())
    return jax.shard_map(shards, mesh=mesh, in_specs=in_specs, out_specs=out_specs, check_vma=False)
```

```python
import math
import numpy as np
import jax, jax.numpy as jnp
from jax import lax
from jax.experimental import pallas as pl
from jax.experimental.pallas import tpu as pltpu
from jax.sharding import PartitionSpec as P
import ml_dtypes

F32 = jnp.float32
BF = jnp.bfloat16
MESH = pl.DeviceIdType.MESH
NEAR = 10


def consts():
    n = np.arange(128)
    out = []
    for odd in (0, 1):
        angle = 2 * np.pi * (np.outer(n, 2 * n + odd) % 256) / 256
        real, imag = np.cos(angle) / 16, -np.sin(angle) / 16
        block = np.block([[real, imag], [-imag, real]])
        for m in (block, block.T):
            m = m.astype(np.float32)
            high = m.astype(ml_dtypes.bfloat16)
            low = (m - high.astype(np.float32)).astype(ml_dtypes.bfloat16)
            out.append(np.stack([high, low]))
    mats = np.stack(out).reshape(2, 2, 2, 256, 256)
    k = np.arange(256)
    perm = np.zeros((256, 256))
    perm[k, (k % 2) * 128 + k // 2] = 1
    return mats, perm.astype(ml_dtypes.bfloat16)


def split(x):
    high = x.astype(BF)
    return high, (x - high.astype(F32)).astype(BF)


def dot(a, b):
    return jnp.dot(a, b, preferred_element_type=F32)


def left(mats, high, low):
    x = dot(jnp.concatenate([mats[0], mats[1]], axis=0), high)
    return x[:256] + x[256:] + dot(mats[0], low)


def right(high, low, mats):
    x = dot(jnp.concatenate([high, low], axis=0), mats[0])
    return x[:256] + x[256:] + dot(high, mats[1])


BUFFERS = 14


def buffers():
    whole = pltpu.VMEM((2, 256, 256), F32)
    half = pltpu.VMEM((2, 256, 256), BF)
    return [whole, whole] + [half, half, whole] * 4


def stages(slot, row, col, live, source, ill, mats, moduli, pterm, place, bufs):
    patch, wave, h1, l1, m1, h2, l2, m2, h3, l3, m3, h4, l4, m4 = bufs
    tile = col // 128
    shift = col % 128
    back = (128 - shift) % 128
    lane = lax.broadcasted_iota(jnp.int32, (128, 128), 1)

    def cut():
        halves = []
        for h in range(2):
            rows = pl.ds(h * 128, 128)
            x = [[pltpu.roll(source[p, tile + t, pl.ds(row + h * 128, 128), :], back, 1) for t in range(3)]
                 for p in range(2)]
            picked = [[jnp.where(lane < 128 - shift, x[p][t], x[p][t + 1]) for t in range(2)] for p in range(2)]
            waves = []
            for t in range(2):
                lanes = pl.ds(128 * t, 128)
                pr, pi = ill[0, rows, lanes], ill[1, rows, lanes]
                a, b = picked[0][t], picked[1][t]
                patch[0, rows, lanes] = a
                patch[1, rows, lanes] = b
                wr, wi = pr * a - pi * b, pr * b + pi * a
                wave[0, rows, lanes] = wr
                wave[1, rows, lanes] = wi
                waves.append((wr, wi))
            halves.append(waves)
        for t in range(2):
            lanes = pl.ds(128 * t, 128)
            (ar, ai), (br, bi) = halves[0][t], halves[1][t]
            for q, pair in enumerate(((ar + br, ai + bi), (ar - br, ai - bi))):
                for z, value in enumerate(pair):
                    rows = pl.ds(z * 128, 128)
                    h1[q, rows, lanes], l1[q, rows, lanes] = split(value)

    def rows_forward():
        for q in range(2):
            m1[q] = left(mats.at[q, 1], h1[q], l1[q])

    def between_forward():
        for q in range(2):
            ar, br = m1[q, pl.ds(0, 128), pl.ds(0, 128)], m1[q, pl.ds(0, 128), pl.ds(128, 128)]
            ai, bi = m1[q, pl.ds(128, 128), pl.ds(0, 128)], m1[q, pl.ds(128, 128), pl.ds(128, 128)]
            rows = pl.ds(q * 128, 128)
            for e, pair in enumerate(((ar + br, ai + bi), (ar - br, ai - bi))):
                for z, value in enumerate(pair):
                    lanes = pl.ds(z * 128, 128)
                    h2[e, rows, lanes], l2[e, rows, lanes] = split(value)

    def columns_forward():
        for e in range(2):
            m2[e] = right(h2[e], l2[e], mats.at[e, 0])

    def project():
        for q in range(2):
            for e in range(2):
                rows = pl.ds(q * 128, 128)
                fr, fi = m2[e, rows, pl.ds(0, 128)], m2[e, rows, pl.ds(128, 128)]
                f = moduli[slot, rows, pl.ds(e * 128, 128)] * lax.rsqrt(jnp.maximum(fr * fr + fi * fi, 0.25))
                for z, value in enumerate((fr * f, fi * f)):
                    lanes = pl.ds(z * 128, 128)
                    h3[e, rows, lanes], l3[e, rows, lanes] = split(value)

    def columns_back():
        for e in range(2):
            m3[e] = right(h3[e], l3[e], mats.at[e, 1])

    def between_back():
        for q in range(2):
            rows = pl.ds(q * 128, 128)
            er, ei = m3[0, rows, pl.ds(0, 128)], m3[0, rows, pl.ds(128, 128)]
            vr, vi = m3[1, rows, pl.ds(0, 128)], m3[1, rows, pl.ds(128, 128)]
            for t, pair in enumerate(((er + vr, ei + vi), (er - vr, ei - vi))):
                for z, value in enumerate(pair):
                    at, lanes = pl.ds(z * 128, 128), pl.ds(t * 128, 128)
                    h4[q, at, lanes], l4[q, at, lanes] = split(value)

    def rows_back():
        for q in range(2):
            m4[q] = left(mats.at[q, 0], h4[q], l4[q])

    def update():
        out = [[[None] * 2 for _ in range(2)] for _ in range(2)]
        for t in range(2):
            lanes = pl.ds(128 * t, 128)
            er, ei = m4[0, pl.ds(0, 128), lanes], m4[0, pl.ds(128, 128), lanes]
            vr, vi = m4[1, pl.ds(0, 128), lanes], m4[1, pl.ds(128, 128), lanes]
            for h, (xr, xi) in enumerate(((er + vr, ei + vi), (er - vr, ei - vi))):
                rows = pl.ds(h * 128, 128)
                cr, ci = xr - wave[0, rows, lanes], xi - wave[1, rows, lanes]
                if live is not None:
                    cr, ci = cr * live, ci * live
                a, b = patch[0, rows, lanes], patch[1, rows, lanes]
                pterm[0, t, rows, :] += a * cr + b * ci
                pterm[1, t, rows, :] += a * ci - b * cr
                pr, pi = ill[0, rows, lanes], ill[1, rows, lanes]
                out[h][0][t] = pr * cr + pi * ci
                out[h][1][t] = pr * ci - pi * cr
        for h in range(2):
            for z in range(2):
                place(z, h, out[h][z])

    return (cut, rows_forward, between_forward, columns_forward, project,
            columns_back, between_back, rows_back, update)


def together(*windows):
    for steps in zip(*windows):
        for step in steps:
            step()


def deposit(grad, row, col, z, h, values):
    tile = col // 128
    shift = col % 128
    low = lax.broadcasted_iota(jnp.int32, (128, 128), 1) < shift
    first, second = (pltpu.roll(v, shift, 1) for v in values)
    rows = pl.ds(row + h * 128, 128)
    grad[z, tile, rows, :] += jnp.where(low, 0.0, first)
    grad[z, tile + 1, rows, :] += jnp.where(low, first, second)
    grad[z, tile + 2, rows, :] += jnp.where(low, second, 0.0)


def window_kernel(offs, count, ext, ill, mats, moduli, near, near_term, grad, pterm, todo, done, *bufs):
    n = count[0]

    @pl.loop(0, 96)
    def _(i):
        rows = pl.ds(pl.multiple_of(8 * i, 8), 8)
        for p in range(2):
            for t in range(6):
                grad[p, t, rows, :] = jnp.zeros((8, 128), F32)

    pterm[...] = near_term[...]

    def sort(s, counts):
        left_over, taken = counts
        r = offs[0, s]
        inside = jnp.logical_and(jnp.logical_and(r >= 128, r <= 384), s < n)
        inside = jnp.logical_and(inside, taken < NEAR)
        todo[left_over] = s
        done[taken] = s
        return (left_over + jnp.logical_and(s < n, jnp.logical_not(inside)).astype(jnp.int32),
                taken + inside.astype(jnp.int32))

    left_over, taken = lax.fori_loop(0, 16, sort, (jnp.int32(0), jnp.int32(0)))

    @pl.loop(0, taken)
    def _(i):
        s = done[i]
        for h in range(2):
            for z in range(2):
                deposit(grad, offs[0, s], offs[1, s], z, h, [near[i, z, t, pl.ds(h * 128, 128), :] for t in range(2)])

    @pl.loop(0, (left_over + 1) // 2)
    def _(k):
        windows = []
        for i in range(2):
            s = todo[jnp.minimum(2 * k + i, left_over - 1)]
            row, col = offs[0, s], offs[1, s]
            live = None if i == 0 else jnp.where(2 * k + i < left_over, 1.0, 0.0).astype(F32)

            def place(z, h, values, row=row, col=col):
                deposit(grad, row, col, z, h, values)

            windows.append(stages(s, row, col, live, ext, ill, mats, moduli, pterm, place,
                                  bufs[BUFFERS * i:BUFFERS * (i + 1)]))
        together(*windows)


def windows(offs, count, ext, ill, mats, moduli, near, near_term):
    V = pl.BlockSpec(memory_space=pltpu.VMEM)
    S = pl.BlockSpec(memory_space=pltpu.SMEM)
    return pl.pallas_call(
        window_kernel,
        out_shape=(jax.ShapeDtypeStruct((2, 6, 768, 128), F32), jax.ShapeDtypeStruct((2, 2, 256, 128), F32)),
        in_specs=[S, S, V, V, V, V, V, V], out_specs=(V, V),
        scratch_shapes=[pltpu.SMEM((16,), jnp.int32), pltpu.SMEM((16,), jnp.int32)] + buffers() * 2,
        compiler_params=pltpu.CompilerParams(vmem_limit_bytes=28 * 2**20),
    )(offs, count, ext, ill, mats, moduli, near, near_term)


def remote(src, dst, send_sem, recv_sem, device):
    return pltpu.make_async_remote_copy(
        src_ref=src, dst_ref=dst, send_sem=send_sem, recv_sem=recv_sem,
        device_id=device, device_id_type=MESH,
    )


def greet(devices):
    barrier = pltpu.get_barrier_semaphore()
    expected = 0
    for condition, device in devices:
        if condition is None:
            pl.semaphore_signal(barrier, inc=1, device_id=device, device_id_type=MESH)
            expected = expected + 1
        else:
            @pl.when(condition)
            def _(device=device):
                pl.semaphore_signal(barrier, inc=1, device_id=device, device_id_type=MESH)
            expected = expected + condition.astype(jnp.int32)
    return barrier, expected


def neighbours():
    a = lax.axis_index("ty")
    b = lax.axis_index("tx")
    has = {"up": a > 0, "down": a < 15, "left": b > 0, "right": b < 15}
    ids = {"up": (jnp.maximum(a - 1, 0), b), "down": (jnp.minimum(a + 1, 15), b),
           "left": (a, jnp.maximum(b - 1, 0)), "right": (a, jnp.minimum(b + 1, 15))}
    return a, b, has, ids


OPPOSITE = {"up": "down", "down": "up", "left": "right", "right": "left"}


def halo_kernel(offs, count, tile, meas, perm, ill, mats, ext, moduli, near, near_term,
                mid, mbuf, meas_sem, own_sem, mid_sem, row_send, row_recv, col_send, col_recv, cor_send, cor_recv, *bufs):
    a, b, has, ids = neighbours()
    barrier, expected = greet([(has[k], ids[k]) for k in ids])
    own = [pltpu.make_async_copy(tile.at[:, :, pl.ds(128 * t, 128)], mid.at[:, 1 + t], own_sem.at[t]) for t in range(4)]
    for copy in own:
        copy.start()

    def fetch(s, t):
        return pltpu.make_async_copy(meas.at[s, :, pl.ds(128 * t, 128)], mbuf.at[s, t], meas_sem.at[s, t])

    @pl.loop(0, 16)
    def _(s):
        for t in range(2):
            fetch(s, t).start()

    pl.semaphore_wait(barrier, expected)
    rows, cols, corners = {}, {}, {}
    for i, way in enumerate(("down", "up")):
        src_row, dst_row = (384, 0) if way == "down" else (0, 640)
        for t in (0, 3, 1, 2):
            rows[way, t] = remote(
                tile.at[:, pl.ds(src_row, 128), pl.ds(128 * t, 128)],
                ext.at[:, 1 + t, pl.ds(dst_row, 128), :],
                row_send.at[i, t], row_recv.at[i, t], ids[way])
    for i, way in enumerate(("right", "left")):
        src_t, dst_t = (3, 0) if way == "right" else (0, 5)
        cols[way] = remote(
            tile.at[:, :, pl.ds(128 * src_t, 128)], mid.at[:, dst_t],
            col_send.at[i], col_recv.at[i], ids[way])
        for j, row in enumerate((0, 640)):
            corners[way, j] = remote(
                ext.at[:, 1 + src_t, pl.ds(row, 128), :], ext.at[:, dst_t, pl.ds(row, 128), :],
                cor_send.at[i, j], cor_recv.at[i, j], ids[way])
    for t in (0, 3):
        for way in ("down", "up"):
            pl.when(has[way])(rows[way, t].start)
    for way in ("right", "left"):
        pl.when(has[way])(cols[way].start)
    for t in (1, 2):
        for way in ("down", "up"):
            pl.when(has[way])(rows[way, t].start)

    @pl.loop(0, 16)
    def _(s):
        for t in range(2):
            fetch(s, t).wait()
        for q in range(2):
            picked = jnp.concatenate([mbuf[s, t, pl.ds(q, 128, stride=2), :] for t in range(2)], axis=1)
            high, low = split(picked)
            moduli[s, pl.ds(128 * q, 128), :] = dot(high, perm[...]) + dot(low, perm[...])

    near_term[...] = jnp.zeros_like(near_term)
    n = count[0]
    inside, rank, total = [], [], jnp.int32(0)
    for s in range(16):
        r = offs[0, s]
        ok = jnp.logical_and(jnp.logical_and(r >= 128, r <= 384), s < n).astype(jnp.int32)
        inside.append(ok)
        rank.append(total)
        total = total + ok
    for copy in own:
        copy.wait()
    for side in ("right", "left"):
        pl.when(has[OPPOSITE[side]])(cols[side].wait_recv)
    centre = pltpu.make_async_copy(mid, ext.at[:, :, pl.ds(128, 512), :], mid_sem)
    centre.start()

    @pl.loop(0, NEAR // 2)
    def _(k):
        @pl.when(k == 2)
        def _():
            for j, way in enumerate(("down", "up")):
                @pl.when(has[OPPOSITE[way]])
                def _(way=way):
                    rows[way, 0].wait_recv()
                    rows[way, 3].wait_recv()
                for side in ("right", "left"):
                    pl.when(jnp.logical_and(has[side], has[OPPOSITE[way]]))(corners[side, j].start)

        taken = []
        for i in range(2):
            at = 2 * k + i
            slot = jnp.int32(0)
            for s in range(1, 16):
                slot = slot + s * inside[s] * (rank[s] == at).astype(jnp.int32)
            row = jnp.clip(offs[0, slot] - 128, 0, 256)
            live = (at < total).astype(F32)

            def place(z, h, values, at=at):
                for t in range(2):
                    near[at, z, t, pl.ds(h * 128, 128), :] = values[t]

            taken.append(stages(slot, row, offs[1, slot], live, mid, ill, mats, moduli, near_term, place,
                                bufs[BUFFERS * i:BUFFERS * (i + 1)]))
        together(*taken)

    for way in ("down", "up"):
        for t in (1, 2):
            pl.when(has[OPPOSITE[way]])(rows[way, t].wait_recv)
        for t in range(4):
            pl.when(has[way])(rows[way, t].wait_send)
    for side in ("right", "left"):
        pl.when(has[side])(cols[side].wait_send)
        for j, way in enumerate(("down", "up")):
            pl.when(jnp.logical_and(has[OPPOSITE[side]], has[OPPOSITE[way]]))(corners[side, j].wait_recv)
            pl.when(jnp.logical_and(has[side], has[OPPOSITE[way]]))(corners[side, j].wait_send)
    centre.wait()


def halo(offs, count, tile, meas, perm, ill, mats):
    D = pltpu.SemaphoreType.DMA
    A = pl.BlockSpec(memory_space=pl.ANY)
    V = pl.BlockSpec(memory_space=pltpu.VMEM)
    S = pl.BlockSpec(memory_space=pltpu.SMEM)
    return pl.pallas_call(
        halo_kernel,
        out_shape=(jax.ShapeDtypeStruct((2, 6, 768, 128), F32), jax.ShapeDtypeStruct((16, 256, 256), F32),
                   jax.ShapeDtypeStruct((NEAR, 2, 2, 256, 128), F32), jax.ShapeDtypeStruct((2, 2, 256, 128), F32)),
        in_specs=[S, S, A, A, V, V, V], out_specs=(V, V, V, V),
        scratch_shapes=[pltpu.VMEM((2, 6, 512, 128), F32), pltpu.VMEM((16, 2, 256, 128), F32), D((16, 2)),
                        D((4,)), D, D((2, 4)), D((2, 4)), D((2,)), D((2,)), D((2, 2)), D((2, 2))] + buffers() * 2,
        compiler_params=pltpu.CompilerParams(collective_id=1, has_side_effects=True, vmem_limit_bytes=26 * 2**20),
    )(offs, count, tile, meas, perm, ill, mats)


def partners(b):
    core = b % 2
    x = (b // 2) % 4
    zlo = b // 8
    return core, x, zlo


def finish_kernel(spec, ill, grad, pterm, newspec, newill,
                  rxc, rxm, rz, edge, rcore, rx, sumc, part, rc, total,
                  core_s, core_r, xs, xr, cs, cr, ms, mr, zs, zr,
                  us, ur, ds, dr, es, er, fs, fr):
    a, b, has, ids = neighbours()
    core, x, zlo = partners(b)
    low = x * 2 + core
    unit = zlo * 16 + a

    def member(d):
        u = (unit + d) % 32
        return (u % 16, (u // 16) * 8 + low)

    mates = [(a, zlo * 8 + ((x + d) % 4) * 2 + core) for d in (1, 2, 3)]
    other = (a, zlo * 8 + x * 2 + (1 - core))
    barrier, expected = greet([(None, m) for m in mates] + [(None, other)]
                              + [(jnp.logical_and(core == 0, has["left"]), ids["left"]),
                                 (jnp.logical_and(core == 1, has["right"]), ids["right"])])

    @pl.loop(1, 32)
    def _(d):
        pl.semaphore_signal(barrier, inc=1, device_id=member(d), device_id_type=MESH)

    power = jnp.sum(ill[0] * ill[0] + ill[1] * ill[1]) * (1.0 / 65536) + 1e-05
    inv = 1.0 / power
    pl.semaphore_wait(barrier, expected + 31)
    first = remote(pterm.at[1 - core], rcore, core_s, core_r, other)
    corner, middle, vert = {}, {}, {}
    for i, side in enumerate(("right", "left")):
        src_t = 5 if side == "right" else 0
        for j, row in enumerate((0, 640)):
            corner[side, j] = remote(grad.at[:, src_t, pl.ds(row, 128), :], rxc.at[i, j],
                                     cs.at[i, j], cr.at[i, j], ids[side])
        middle[side] = remote(grad.at[:, src_t, pl.ds(128, 512), :], rxm.at[i], ms.at[i], mr.at[i], ids[side])
    for j, way in enumerate(("up", "down")):
        row = 0 if way == "up" else 640
        for t in range(4):
            src = edge.at[j, t // 3] if t in (0, 3) else grad.at[:, 1 + t, pl.ds(row, 128), :]
            vert[way, t] = remote(src, rz.at[j, :, t], zs.at[j, t], zr.at[j, t], ids[way])

    def send_vert(t):
        for way in ("up", "down"):
            pl.when(has[way])(vert[way, t].start)

    def add_vert(t):
        for j, (way, row) in enumerate((("up", 384), ("down", 0))):
            @pl.when(has[OPPOSITE[way]])
            def _(j=j, way=way, row=row):
                vert[way, t].wait_recv()
                newspec[:, row:row + 128, 128 * t:128 * t + 128] += inv * rz[j, :, t]

    first.start()
    send_vert(1)
    first.wait_recv()
    sumc[...] = pterm[core] + rcore[...]
    xsend = [remote(sumc.at[(x + d) % 4], rx.at[d - 1], xs.at[d - 1], xr.at[d - 1], mates[d - 1]) for d in (1, 2, 3)]
    for copy in xsend:
        copy.start()
    for side in ("right", "left"):
        for j in range(2):
            pl.when(has[side])(corner[side, j].start)
    for copy in xsend:
        copy.wait_recv()
    part[...] = sumc[x] + rx[0] + rx[1] + rx[2]

    @pl.loop(1, 32)
    def _(d):
        device = member(d)
        remote(part.at[device[0]], rc.at[d - 1], us, ur, device).start()

    send_vert(2)
    for side in ("right", "left"):
        pl.when(has[side])(middle[side].start)

    @pl.loop(0, 16)
    def _(i):
        rows = pl.ds(pl.multiple_of(32 * i, 32), 32)
        more = pl.ds(pl.multiple_of(32 * i + 128, 32), 32)
        for p in range(2):
            for t in range(4):
                lanes = pl.ds(128 * t, 128)
                newspec[p, rows, lanes] = spec[p, rows, lanes] + inv * grad[p, 1 + t, more, :]

    for j, row in enumerate((0, 640)):
        for k, (t, side) in enumerate(((1, "right"), (4, "left"))):
            edge[j, k] = grad[:, t, row:row + 128, :]
            @pl.when(has[OPPOSITE[side]])
            def _(j=j, k=k, side=side):
                corner[side, j].wait_recv()
                edge[j, k] += rxc[k, j]
    whole = remote(rc, rc, us, ur, other)
    whole.wait_recv()
    acc = part[a]
    for i in range(31):
        acc = acc + rc[i]
    total[core, x, a] = acc

    @pl.loop(1, 16)
    def _(d):
        remote(total.at[core, x, a], total.at[core, x, a], ds, dr, ((a + d) % 16, b)).start()

    send_vert(0)
    send_vert(3)
    for k, (side, t) in enumerate((("right", 0), ("left", 3))):
        @pl.when(has[OPPOSITE[side]])
        def _(k=k, side=side, t=t):
            middle[side].wait_recv()
            newspec[:, :, 128 * t:128 * t + 128] += inv * rxm[k]
    some = remote(rc.at[pl.ds(0, 15)], rc.at[pl.ds(0, 15)], ds, dr, other)
    some.wait_recv()
    gather = [remote(total.at[core, x], total.at[core, x], es.at[d - 1], er.at[d - 1], mates[d - 1]) for d in (1, 2, 3)]
    for copy in gather:
        copy.start()
    add_vert(1)
    add_vert(2)
    for copy in gather:
        copy.wait_recv()
    last = remote(total.at[core], total.at[core], fs, fr, other)
    last.start()
    last.wait()
    for p in range(2):
        for s in range(4):
            rows, lanes = pl.ds((s % 2) * 128, 128), pl.ds((s // 2) * 128, 128)
            newill[p, rows, lanes] = ill[p, rows, lanes] + total[p, s].reshape(128, 128) * (1.0 / 64)
    add_vert(0)
    add_vert(3)
    first.wait_send()
    for copy in xsend + gather:
        copy.wait_send()
    whole.wait_send()
    some.wait_send()
    for side in ("right", "left"):
        for j in range(2):
            pl.when(has[side])(corner[side, j].wait_send)
        pl.when(has[side])(middle[side].wait_send)
    for way in ("up", "down"):
        for t in range(4):
            pl.when(has[way])(vert[way, t].wait_send)


def finish(spec, ill, grad, pterm):
    D = pltpu.SemaphoreType.DMA
    V = pl.BlockSpec(memory_space=pltpu.VMEM)
    return pl.pallas_call(
        finish_kernel,
        out_shape=(jax.ShapeDtypeStruct((2, 512, 512), F32), jax.ShapeDtypeStruct((2, 256, 256), F32)),
        in_specs=[V, V, V, V], out_specs=(V, V),
        scratch_shapes=[
            pltpu.VMEM((2, 2, 2, 128, 128), F32), pltpu.VMEM((2, 2, 512, 128), F32),
            pltpu.VMEM((2, 2, 4, 128, 128), F32), pltpu.VMEM((2, 2, 2, 128, 128), F32),
            pltpu.VMEM((4, 16, 8, 128), F32), pltpu.VMEM((3, 16, 8, 128), F32), pltpu.VMEM((4, 16, 8, 128), F32),
            pltpu.VMEM((16, 8, 128), F32), pltpu.VMEM((31, 8, 128), F32), pltpu.VMEM((2, 4, 16, 8, 128), F32),
            D, D, D((3,)), D((3,)), D((2, 2)), D((2, 2)), D((2,)), D((2,)), D((2, 4)), D((2, 4)),
            D, D, D, D, D((3,)), D((3,)), D, D,
        ],
        compiler_params=pltpu.CompilerParams(collective_id=2, has_side_effects=True, vmem_limit_bytes=32 * 2**20),
    )(spec, ill, grad, pterm)


def shards(specimen, illumination, scan_offsets, slot_counts, measured):
    anchor = jnp.stack([lax.axis_index("ty") * 512, lax.axis_index("tx") * 512]) - 128
    local = scan_offsets[0, 0] - anchor[:, None]
    count = slot_counts[0]
    mats, perm = (jnp.asarray(m) for m in consts())
    ext, moduli, near, near_term = halo(local, count, specimen, measured[0, 0], perm, illumination, mats)
    grad, probe_term = windows(local, count, ext, illumination, mats, moduli, near, near_term)
    return finish(specimen, illumination, grad, probe_term.reshape(2, 4, 16, 8, 128))


def solution(mesh):
    in_specs = (
        P(None, "ty", "tx"),
        P(),
        P("ty", "tx", None, None),
        P("ty", "tx"),
        P("ty", "tx", None, None, None),
    )
    out_specs = (P(None, "ty", "tx"), P())
    return jax.shard_map(shards, mesh=mesh, in_specs=in_specs, out_specs=out_specs, check_vma=False)
```

```python
import math
import numpy as np
import jax, jax.numpy as jnp
from jax import lax
from jax.experimental import pallas as pl
from jax.experimental.pallas import tpu as pltpu
from jax.sharding import PartitionSpec as P
import ml_dtypes

F32 = jnp.float32
BF = jnp.bfloat16
MESH = pl.DeviceIdType.MESH
NEAR = 10


def consts():
    n = np.arange(128)
    out = []
    for odd in (0, 1):
        angle = 2 * np.pi * (np.outer(n, 2 * n + odd) % 256) / 256
        real, imag = np.cos(angle) / 16, -np.sin(angle) / 16
        block = np.block([[real, imag], [-imag, real]])
        for m in (block, block.T):
            m = m.astype(np.float32)
            high = m.astype(ml_dtypes.bfloat16)
            low = (m - high.astype(np.float32)).astype(ml_dtypes.bfloat16)
            out.append(np.stack([high, low]))
    mats = np.stack(out).reshape(2, 2, 2, 256, 256)
    return mats


def split(x):
    high = x.astype(BF)
    return high, (x - high.astype(F32)).astype(BF)


def dot(a, b):
    return jnp.dot(a, b, preferred_element_type=F32)


def left(mats, high, low):
    x = dot(jnp.concatenate([mats[0], mats[1]], axis=0), high)
    return x[:256] + x[256:] + dot(mats[0], low)


def right(high, low, mats):
    x = dot(jnp.concatenate([high, low], axis=0), mats[0])
    return x[:256] + x[256:] + dot(high, mats[1])


BUFFERS = 14


def buffers():
    whole = pltpu.VMEM((2, 256, 256), F32)
    half = pltpu.VMEM((2, 256, 256), BF)
    return [whole, whole] + [half, half, whole] * 4


def stages(slot, row, col, live, source, ill, mats, moduli, pterm, place, bufs):
    patch, wave, h1, l1, m1, h2, l2, m2, h3, l3, m3, h4, l4, m4 = bufs
    tile = col // 128
    shift = col % 128
    back = (128 - shift) % 128
    lane = lax.broadcasted_iota(jnp.int32, (128, 128), 1)

    def cut():
        halves = []
        for h in range(2):
            rows = pl.ds(h * 128, 128)
            x = [[pltpu.roll(source[p, tile + t, pl.ds(row + h * 128, 128), :], back, 1) for t in range(3)]
                 for p in range(2)]
            picked = [[jnp.where(lane < 128 - shift, x[p][t], x[p][t + 1]) for t in range(2)] for p in range(2)]
            waves = []
            for t in range(2):
                lanes = pl.ds(128 * t, 128)
                pr, pi = ill[0, rows, lanes], ill[1, rows, lanes]
                a, b = picked[0][t], picked[1][t]
                patch[0, rows, lanes] = a
                patch[1, rows, lanes] = b
                wr, wi = pr * a - pi * b, pr * b + pi * a
                wave[0, rows, lanes] = wr
                wave[1, rows, lanes] = wi
                waves.append((wr, wi))
            halves.append(waves)
        for t in range(2):
            lanes = pl.ds(128 * t, 128)
            (ar, ai), (br, bi) = halves[0][t], halves[1][t]
            for q, pair in enumerate(((ar + br, ai + bi), (ar - br, ai - bi))):
                for z, value in enumerate(pair):
                    rows = pl.ds(z * 128, 128)
                    h1[q, rows, lanes], l1[q, rows, lanes] = split(value)

    def rows_forward():
        for q in range(2):
            m1[q] = left(mats.at[q, 1], h1[q], l1[q])

    def between_forward():
        for q in range(2):
            ar, br = m1[q, pl.ds(0, 128), pl.ds(0, 128)], m1[q, pl.ds(0, 128), pl.ds(128, 128)]
            ai, bi = m1[q, pl.ds(128, 128), pl.ds(0, 128)], m1[q, pl.ds(128, 128), pl.ds(128, 128)]
            rows = pl.ds(q * 128, 128)
            for e, pair in enumerate(((ar + br, ai + bi), (ar - br, ai - bi))):
                for z, value in enumerate(pair):
                    lanes = pl.ds(z * 128, 128)
                    h2[e, rows, lanes], l2[e, rows, lanes] = split(value)

    def columns_forward():
        for e in range(2):
            m2[e] = right(h2[e], l2[e], mats.at[e, 0])

    def project():
        for q in range(2):
            for e in range(2):
                rows = pl.ds(q * 128, 128)
                fr, fi = m2[e, rows, pl.ds(0, 128)], m2[e, rows, pl.ds(128, 128)]
                f = moduli[slot, rows, pl.ds(e * 128, 128)] * lax.rsqrt(jnp.maximum(fr * fr + fi * fi, 0.25))
                for z, value in enumerate((fr * f, fi * f)):
                    lanes = pl.ds(z * 128, 128)
                    h3[e, rows, lanes], l3[e, rows, lanes] = split(value)

    def columns_back():
        for e in range(2):
            m3[e] = right(h3[e], l3[e], mats.at[e, 1])

    def between_back():
        for q in range(2):
            rows = pl.ds(q * 128, 128)
            er, ei = m3[0, rows, pl.ds(0, 128)], m3[0, rows, pl.ds(128, 128)]
            vr, vi = m3[1, rows, pl.ds(0, 128)], m3[1, rows, pl.ds(128, 128)]
            for t, pair in enumerate(((er + vr, ei + vi), (er - vr, ei - vi))):
                for z, value in enumerate(pair):
                    at, lanes = pl.ds(z * 128, 128), pl.ds(t * 128, 128)
                    h4[q, at, lanes], l4[q, at, lanes] = split(value)

    def rows_back():
        for q in range(2):
            m4[q] = left(mats.at[q, 0], h4[q], l4[q])

    def update():
        out = [[[None] * 2 for _ in range(2)] for _ in range(2)]
        for t in range(2):
            lanes = pl.ds(128 * t, 128)
            er, ei = m4[0, pl.ds(0, 128), lanes], m4[0, pl.ds(128, 128), lanes]
            vr, vi = m4[1, pl.ds(0, 128), lanes], m4[1, pl.ds(128, 128), lanes]
            for h, (xr, xi) in enumerate(((er + vr, ei + vi), (er - vr, ei - vi))):
                rows = pl.ds(h * 128, 128)
                cr, ci = xr - wave[0, rows, lanes], xi - wave[1, rows, lanes]
                if live is not None:
                    cr, ci = cr * live, ci * live
                a, b = patch[0, rows, lanes], patch[1, rows, lanes]
                pterm[0, t, rows, :] += a * cr + b * ci
                pterm[1, t, rows, :] += a * ci - b * cr
                pr, pi = ill[0, rows, lanes], ill[1, rows, lanes]
                out[h][0][t] = pr * cr + pi * ci
                out[h][1][t] = pr * ci - pi * cr
        for h in range(2):
            for z in range(2):
                place(z, h, out[h][z])

    return (cut, rows_forward, between_forward, columns_forward, project,
            columns_back, between_back, rows_back, update)


def places(offs):
    return lambda s: offs[0, s], lambda s: offs[1, s]


def together(*windows):
    for steps in zip(*windows):
        for step in steps:
            step()


def deposit(grad, row, col, z, h, values):
    tile = col // 128
    shift = col % 128
    low = lax.broadcasted_iota(jnp.int32, (128, 128), 1) < shift
    first, second = (pltpu.roll(v, shift, 1) for v in values)
    rows = pl.ds(row + h * 128, 128)
    grad[z, tile, rows, :] += jnp.where(low, 0.0, first)
    grad[z, tile + 1, rows, :] += jnp.where(low, first, second)
    grad[z, tile + 2, rows, :] += jnp.where(low, second, 0.0)


def window_kernel(offs, count, ext, ill, mats, moduli, near, near_term, grad, pterm, todo, done, *bufs):
    n = count[0]
    row_of, col_of = places(offs)

    @pl.loop(0, 96)
    def _(i):
        rows = pl.ds(pl.multiple_of(8 * i, 8), 8)
        for p in range(2):
            for t in range(6):
                grad[p, t, rows, :] = jnp.zeros((8, 128), F32)

    pterm[...] = near_term[...]

    def sort(s, counts):
        left_over, taken = counts
        r = row_of(s)
        inside = jnp.logical_and(jnp.logical_and(r >= 128, r <= 384), s < n)
        inside = jnp.logical_and(inside, taken < NEAR)
        todo[left_over] = s
        done[taken] = s
        return (left_over + jnp.logical_and(s < n, jnp.logical_not(inside)).astype(jnp.int32),
                taken + inside.astype(jnp.int32))

    left_over, taken = lax.fori_loop(0, 16, sort, (jnp.int32(0), jnp.int32(0)))

    @pl.loop(0, taken)
    def _(i):
        s = done[i]
        for h in range(2):
            for z in range(2):
                deposit(grad, row_of(s), col_of(s), z, h, [near[i, z, t, pl.ds(h * 128, 128), :] for t in range(2)])

    @pl.loop(0, (left_over + 1) // 2)
    def _(k):
        windows = []
        for i in range(2):
            s = todo[jnp.minimum(2 * k + i, left_over - 1)]
            row, col = row_of(s), col_of(s)
            live = None if i == 0 else jnp.where(2 * k + i < left_over, 1.0, 0.0).astype(F32)

            def place(z, h, values, row=row, col=col):
                deposit(grad, row, col, z, h, values)

            windows.append(stages(s, row, col, live, ext, ill, mats, moduli, pterm, place,
                                  bufs[BUFFERS * i:BUFFERS * (i + 1)]))
        together(*windows)


def windows(offs, count, ext, ill, mats, moduli, near, near_term):
    V = pl.BlockSpec(memory_space=pltpu.VMEM)
    S = pl.BlockSpec(memory_space=pltpu.SMEM)
    return pl.pallas_call(
        window_kernel,
        out_shape=(jax.ShapeDtypeStruct((2, 6, 768, 128), F32), jax.ShapeDtypeStruct((2, 2, 256, 128), F32)),
        in_specs=[S, S, V, V, V, V, V, V], out_specs=(V, V),
        scratch_shapes=[pltpu.SMEM((16,), jnp.int32), pltpu.SMEM((16,), jnp.int32)] + buffers() * 2,
        compiler_params=pltpu.CompilerParams(vmem_limit_bytes=28 * 2**20),
    )(offs, count, ext, ill, mats, moduli, near, near_term)


def remote(src, dst, send_sem, recv_sem, device):
    return pltpu.make_async_remote_copy(
        src_ref=src, dst_ref=dst, send_sem=send_sem, recv_sem=recv_sem,
        device_id=device, device_id_type=MESH,
    )


def greet(devices):
    barrier = pltpu.get_barrier_semaphore()
    expected = 0
    for condition, device in devices:
        if condition is None:
            pl.semaphore_signal(barrier, inc=1, device_id=device, device_id_type=MESH)
            expected = expected + 1
        else:
            @pl.when(condition)
            def _(device=device):
                pl.semaphore_signal(barrier, inc=1, device_id=device, device_id_type=MESH)
            expected = expected + condition.astype(jnp.int32)
    return barrier, expected


def neighbours():
    a = lax.axis_index("ty")
    b = lax.axis_index("tx")
    has = {"up": a > 0, "down": a < 15, "left": b > 0, "right": b < 15}
    ids = {"up": (jnp.maximum(a - 1, 0), b), "down": (jnp.minimum(a + 1, 15), b),
           "left": (a, jnp.maximum(b - 1, 0)), "right": (a, jnp.minimum(b + 1, 15))}
    return a, b, has, ids


OPPOSITE = {"up": "down", "down": "up", "left": "right", "right": "left"}


def halo_kernel(offs, count, tile, meas, ill, mats, ext, moduli, near, near_term,
                mid, mbuf, meas_sem, own_sem, mid_sem, row_send, row_recv, col_send, col_recv, cor_send, cor_recv, *bufs):
    a, b, has, ids = neighbours()
    barrier, expected = greet([(has[k], ids[k]) for k in ids])
    own = [pltpu.make_async_copy(tile.at[:, :, pl.ds(128 * t, 128)], mid.at[:, 1 + t], own_sem.at[t]) for t in range(4)]
    for copy in own:
        copy.start()

    def fetch(s, t):
        return pltpu.make_async_copy(meas.at[s, :, pl.ds(128 * t, 128)], mbuf.at[s, t], meas_sem.at[s, t])

    @pl.loop(0, 16)
    def _(s):
        for t in range(2):
            fetch(s, t).start()

    pl.semaphore_wait(barrier, expected)
    rows, cols, corners = {}, {}, {}
    for i, way in enumerate(("down", "up")):
        src_row, dst_row = (384, 0) if way == "down" else (0, 640)
        for t in (0, 3, 1, 2):
            rows[way, t] = remote(
                tile.at[:, pl.ds(src_row, 128), pl.ds(128 * t, 128)],
                ext.at[:, 1 + t, pl.ds(dst_row, 128), :],
                row_send.at[i, t], row_recv.at[i, t], ids[way])
    for i, way in enumerate(("right", "left")):
        src_t, dst_t = (3, 0) if way == "right" else (0, 5)
        cols[way] = remote(
            tile.at[:, :, pl.ds(128 * src_t, 128)], mid.at[:, dst_t],
            col_send.at[i], col_recv.at[i], ids[way])
        for j, row in enumerate((0, 640)):
            corners[way, j] = remote(
                ext.at[:, 1 + src_t, pl.ds(row, 128), :], ext.at[:, dst_t, pl.ds(row, 128), :],
                cor_send.at[i, j], cor_recv.at[i, j], ids[way])
    outer = jnp.logical_or((b // 2) % 4 == 0, (b // 2) % 4 == 3)

    def start_rows(mine):
        for t in (0, 3, 1, 2):
            for way in ("down", "up"):
                pl.when(jnp.logical_and(has[way], mine))(rows[way, t].start)

    for way in ("right", "left"):
        pl.when(has[way])(cols[way].start)
    start_rows(jnp.logical_not(outer))
    near_term[...] = jnp.zeros_like(near_term)
    for side in ("right", "left"):
        pl.when(has[side])(cols[side].wait_send)
        pl.when(has[OPPOSITE[side]])(cols[side].wait_recv)
    start_rows(outer)
    for copy in own:
        copy.wait()
    centre = pltpu.make_async_copy(mid, ext.at[:, :, pl.ds(128, 512), :], mid_sem)
    centre.start()
    to = lax.broadcasted_iota(jnp.int32, (256, 256), 1)
    source = 2 * (to % 128) + to // 128
    perm = jnp.where(lax.broadcasted_iota(jnp.int32, (256, 256), 0) == source, 1.0, 0.0).astype(BF)

    @pl.loop(0, 16)
    def _(s):
        for t in range(2):
            fetch(s, t).wait()
        for q in range(2):
            picked = jnp.concatenate([mbuf[s, t, pl.ds(q, 128, stride=2), :] for t in range(2)], axis=1)
            high, low = split(picked)
            moduli[s, pl.ds(128 * q, 128), :] = dot(high, perm) + dot(low, perm)

    n = count[0]
    row_of, col_of = places(offs)
    inside, rank, total = [], [], jnp.int32(0)
    for s in range(16):
        r = row_of(s)
        ok = jnp.logical_and(jnp.logical_and(r >= 128, r <= 384), s < n).astype(jnp.int32)
        inside.append(ok)
        rank.append(total)
        total = total + ok

    @pl.loop(0, NEAR // 2)
    def _(k):
        @pl.when(k == 2)
        def _():
            for j, way in enumerate(("down", "up")):
                @pl.when(has[OPPOSITE[way]])
                def _(way=way):
                    rows[way, 0].wait_recv()
                    rows[way, 3].wait_recv()
                for side in ("right", "left"):
                    pl.when(jnp.logical_and(has[side], has[OPPOSITE[way]]))(corners[side, j].start)

        taken = []
        for i in range(2):
            at = 2 * k + i
            slot = jnp.int32(0)
            for s in range(1, 16):
                slot = slot + s * inside[s] * (rank[s] == at).astype(jnp.int32)
            row = jnp.clip(row_of(slot) - 128, 0, 256)
            live = (at < total).astype(F32)

            def place(z, h, values, at=at):
                for t in range(2):
                    near[at, z, t, pl.ds(h * 128, 128), :] = values[t]

            taken.append(stages(slot, row, col_of(slot), live, mid, ill, mats, moduli, near_term, place,
                                bufs[BUFFERS * i:BUFFERS * (i + 1)]))
        together(*taken)

    for way in ("down", "up"):
        for t in (1, 2):
            pl.when(has[OPPOSITE[way]])(rows[way, t].wait_recv)
        for t in range(4):
            pl.when(has[way])(rows[way, t].wait_send)
    for side in ("right", "left"):
        for j, way in enumerate(("down", "up")):
            pl.when(jnp.logical_and(has[OPPOSITE[side]], has[OPPOSITE[way]]))(corners[side, j].wait_recv)
            pl.when(jnp.logical_and(has[side], has[OPPOSITE[way]]))(corners[side, j].wait_send)
    centre.wait()


def halo(offs, count, tile, meas, ill, mats):
    D = pltpu.SemaphoreType.DMA
    A = pl.BlockSpec(memory_space=pl.ANY)
    V = pl.BlockSpec(memory_space=pltpu.VMEM)
    S = pl.BlockSpec(memory_space=pltpu.SMEM)
    return pl.pallas_call(
        halo_kernel,
        out_shape=(jax.ShapeDtypeStruct((2, 6, 768, 128), F32), jax.ShapeDtypeStruct((16, 256, 256), F32),
                   jax.ShapeDtypeStruct((NEAR, 2, 2, 256, 128), F32), jax.ShapeDtypeStruct((2, 2, 256, 128), F32)),
        in_specs=[S, S, A, A, V, V], out_specs=(V, V, V, V),
        scratch_shapes=[pltpu.VMEM((2, 6, 512, 128), F32), pltpu.VMEM((16, 2, 256, 128), F32), D((16, 2)),
                        D((4,)), D, D((2, 4)), D((2, 4)), D((2,)), D((2,)), D((2, 2)), D((2, 2))] + buffers() * 2,
        compiler_params=pltpu.CompilerParams(collective_id=1, has_side_effects=True, vmem_limit_bytes=26 * 2**20),
    )(offs, count, tile, meas, ill, mats)


def partners(b):
    core = b % 2
    x = (b // 2) % 4
    zlo = b // 8
    return core, x, zlo


def finish_kernel(spec, ill, grad, pterm, newspec, newill,
                  rxc, rxm, rz, edge, rcore, rx, sumc, part, rc, total,
                  core_s, core_r, xs, xr, cs, cr, ms, mr, zs, zr,
                  us, ur, ds, dr, es, er, fs, fr):
    a, b, has, ids = neighbours()
    core, x, zlo = partners(b)
    low = x * 2 + core
    unit = zlo * 16 + a

    def member(d):
        u = (unit + d) % 32
        return (u % 16, (u // 16) * 8 + low)

    mates = [(a, zlo * 8 + ((x + d) % 4) * 2 + core) for d in (1, 2, 3)]
    other = (a, zlo * 8 + x * 2 + (1 - core))
    barrier, expected = greet([(None, m) for m in mates] + [(None, other)]
                              + [(jnp.logical_and(core == 0, has["left"]), ids["left"]),
                                 (jnp.logical_and(core == 1, has["right"]), ids["right"])])

    @pl.loop(1, 32)
    def _(d):
        pl.semaphore_signal(barrier, inc=1, device_id=member(d), device_id_type=MESH)

    power = jnp.sum(ill[0] * ill[0] + ill[1] * ill[1]) * (1.0 / 65536) + 1e-05
    inv = 1.0 / power
    pl.semaphore_wait(barrier, expected + 31)
    first = remote(pterm.at[1 - core], rcore, core_s, core_r, other)
    corner, middle, vert = {}, {}, {}
    for i, side in enumerate(("right", "left")):
        src_t = 5 if side == "right" else 0
        for j, row in enumerate((0, 640)):
            corner[side, j] = remote(grad.at[:, src_t, pl.ds(row, 128), :], rxc.at[i, j],
                                     cs.at[i, j], cr.at[i, j], ids[side])
        middle[side] = remote(grad.at[:, src_t, pl.ds(128, 512), :], rxm.at[i], ms.at[i], mr.at[i], ids[side])
    for j, way in enumerate(("up", "down")):
        row = 0 if way == "up" else 640
        for t in range(4):
            src = edge.at[j, t // 3] if t in (0, 3) else grad.at[:, 1 + t, pl.ds(row, 128), :]
            vert[way, t] = remote(src, rz.at[j, :, t], zs.at[j, t], zr.at[j, t], ids[way])

    outer = jnp.logical_or(x == 0, x == 3)
    inner = jnp.logical_not(outer)
    crossing = {"right": b == 7, "left": b == 8}

    def send_vert(t, mine):
        for way in ("up", "down"):
            pl.when(jnp.logical_and(has[way], mine))(vert[way, t].start)

    def add_vert(t):
        for j, (way, row) in enumerate((("up", 384), ("down", 0))):
            @pl.when(has[OPPOSITE[way]])
            def _(j=j, way=way, row=row):
                vert[way, t].wait_recv()
                newspec[:, row:row + 128, 128 * t:128 * t + 128] += inv * rz[j, :, t]

    first.start()
    for side in ("right", "left"):
        pl.when(crossing[side])(middle[side].start)
    send_vert(1, inner)
    first.wait_recv()
    sumc[...] = pterm[core] + rcore[...]
    xsend = [remote(sumc.at[(x + d) % 4], rx.at[d - 1], xs.at[d - 1], xr.at[d - 1], mates[d - 1]) for d in (1, 2, 3)]
    for copy in xsend:
        copy.start()
    for side in ("right", "left"):
        for j in range(2):
            pl.when(has[side])(corner[side, j].start)
    for copy in xsend:
        copy.wait_recv()
    part[...] = sumc[x] + rx[0] + rx[1] + rx[2]

    @pl.loop(1, 32)
    def _(d):
        device = member(d)
        remote(part.at[device[0]], rc.at[d - 1], us, ur, device).start()

    send_vert(1, outer)
    send_vert(2, inner)
    for side in ("right", "left"):
        pl.when(jnp.logical_and(has[side], jnp.logical_not(crossing[side])))(middle[side].start)

    @pl.loop(0, 16)
    def _(i):
        rows = pl.ds(pl.multiple_of(32 * i, 32), 32)
        more = pl.ds(pl.multiple_of(32 * i + 128, 32), 32)
        for p in range(2):
            for t in range(4):
                lanes = pl.ds(128 * t, 128)
                newspec[p, rows, lanes] = spec[p, rows, lanes] + inv * grad[p, 1 + t, more, :]

    for j, row in enumerate((0, 640)):
        for k, (t, side) in enumerate(((1, "right"), (4, "left"))):
            edge[j, k] = grad[:, t, row:row + 128, :]
            @pl.when(has[OPPOSITE[side]])
            def _(j=j, k=k, side=side):
                corner[side, j].wait_recv()
                edge[j, k] += rxc[k, j]
    whole = remote(rc, rc, us, ur, other)
    whole.wait_recv()
    acc = part[a]
    for i in range(31):
        acc = acc + rc[i]
    total[core, x, a] = acc

    @pl.loop(1, 16)
    def _(d):
        remote(total.at[core, x, a], total.at[core, x, a], ds, dr, ((a + d) % 16, b)).start()

    send_vert(2, outer)
    send_vert(0, has["up"] | has["down"])
    send_vert(3, has["up"] | has["down"])
    for k, (side, t) in enumerate((("right", 0), ("left", 3))):
        @pl.when(has[OPPOSITE[side]])
        def _(k=k, side=side, t=t):
            middle[side].wait_recv()
            newspec[:, :, 128 * t:128 * t + 128] += inv * rxm[k]
    some = remote(rc.at[pl.ds(0, 15)], rc.at[pl.ds(0, 15)], ds, dr, other)
    some.wait_recv()
    gather = [remote(total.at[core, x], total.at[core, x], es.at[d - 1], er.at[d - 1], mates[d - 1]) for d in (1, 2, 3)]
    for copy in gather:
        copy.start()
    add_vert(1)
    add_vert(2)
    for copy in gather:
        copy.wait_recv()
    last = remote(total.at[core], total.at[core], fs, fr, other)
    last.start()
    last.wait()
    for p in range(2):
        for s in range(4):
            rows, lanes = pl.ds((s % 2) * 128, 128), pl.ds((s // 2) * 128, 128)
            newill[p, rows, lanes] = ill[p, rows, lanes] + total[p, s].reshape(128, 128) * (1.0 / 64)
    add_vert(0)
    add_vert(3)
    first.wait_send()
    for copy in xsend + gather:
        copy.wait_send()
    whole.wait_send()
    some.wait_send()
    for side in ("right", "left"):
        for j in range(2):
            pl.when(has[side])(corner[side, j].wait_send)
        pl.when(has[side])(middle[side].wait_send)
    for way in ("up", "down"):
        for t in range(4):
            pl.when(has[way])(vert[way, t].wait_send)


def finish(spec, ill, grad, pterm):
    D = pltpu.SemaphoreType.DMA
    V = pl.BlockSpec(memory_space=pltpu.VMEM)
    return pl.pallas_call(
        finish_kernel,
        out_shape=(jax.ShapeDtypeStruct((2, 512, 512), F32), jax.ShapeDtypeStruct((2, 256, 256), F32)),
        in_specs=[V, V, V, V], out_specs=(V, V),
        scratch_shapes=[
            pltpu.VMEM((2, 2, 2, 128, 128), F32), pltpu.VMEM((2, 2, 512, 128), F32),
            pltpu.VMEM((2, 2, 4, 128, 128), F32), pltpu.VMEM((2, 2, 2, 128, 128), F32),
            pltpu.VMEM((4, 16, 8, 128), F32), pltpu.VMEM((3, 16, 8, 128), F32), pltpu.VMEM((4, 16, 8, 128), F32),
            pltpu.VMEM((16, 8, 128), F32), pltpu.VMEM((31, 8, 128), F32), pltpu.VMEM((2, 4, 16, 8, 128), F32),
            D, D, D((3,)), D((3,)), D((2, 2)), D((2, 2)), D((2,)), D((2,)), D((2, 4)), D((2, 4)),
            D, D, D, D, D((3,)), D((3,)), D, D,
        ],
        compiler_params=pltpu.CompilerParams(collective_id=2, has_side_effects=True, vmem_limit_bytes=32 * 2**20),
    )(spec, ill, grad, pterm)


def shards(specimen, illumination, scan_offsets, slot_counts, measured):
    anchor = jnp.stack([lax.axis_index("ty") * 512, lax.axis_index("tx") * 512]) - 128
    local = scan_offsets[0, 0] - anchor[:, None]
    count = slot_counts[0]
    mats = jnp.asarray(consts())
    ext, moduli, near, near_term = halo(local, count, specimen, measured[0, 0], illumination, mats)
    grad, probe_term = windows(local, count, ext, illumination, mats, moduli, near, near_term)
    return finish(specimen, illumination, grad, probe_term.reshape(2, 4, 16, 8, 128))


def solution(mesh):
    in_specs = (
        P(None, "ty", "tx"),
        P(),
        P("ty", "tx", None, None),
        P("ty", "tx"),
        P("ty", "tx", None, None, None),
    )
    out_specs = (P(None, "ty", "tx"), P())
    return jax.shard_map(shards, mesh=mesh, in_specs=in_specs, out_specs=out_specs, check_vma=False)
```

```python
import math
import numpy as np
import jax, jax.numpy as jnp
from jax import lax
from jax.experimental import pallas as pl
from jax.experimental.pallas import tpu as pltpu
from jax.sharding import PartitionSpec as P
import ml_dtypes

F32 = jnp.float32
BF = jnp.bfloat16
MESH = pl.DeviceIdType.MESH
NEAR = 10


def consts():
    n = np.arange(128)
    out = []
    for odd in (0, 1):
        angle = 2 * np.pi * (np.outer(n, 2 * n + odd) % 256) / 256
        real, imag = np.cos(angle) / 16, -np.sin(angle) / 16
        block = np.block([[real, imag], [-imag, real]])
        for m in (block, block.T):
            m = m.astype(np.float32)
            high = m.astype(ml_dtypes.bfloat16)
            low = (m - high.astype(np.float32)).astype(ml_dtypes.bfloat16)
            out.append(np.stack([high, low]))
    mats = np.stack(out).reshape(2, 2, 2, 256, 256)
    return mats


def split(x):
    high = x.astype(BF)
    return high, (x - high.astype(F32)).astype(BF)


def dot(a, b):
    return jnp.dot(a, b, preferred_element_type=F32)


def left(mats, high, low):
    x = dot(jnp.concatenate([mats[0], mats[1]], axis=0), high)
    return x[:256] + x[256:] + dot(mats[0], low)


def right(high, low, mats):
    x = dot(jnp.concatenate([high, low], axis=0), mats[0])
    return x[:256] + x[256:] + dot(high, mats[1])


BUFFERS = 14


def buffers():
    whole = pltpu.VMEM((2, 256, 256), F32)
    half = pltpu.VMEM((2, 256, 256), BF)
    return [whole, whole] + [half, half, whole] * 4


def stages(slot, row, col, live, source, ill, mats, moduli, pterm, place, bufs):
    patch, wave, h1, l1, m1, h2, l2, m2, h3, l3, m3, h4, l4, m4 = bufs
    tile = col // 128
    shift = col % 128
    back = (128 - shift) % 128
    lane = lax.broadcasted_iota(jnp.int32, (128, 128), 1)

    def cut():
        halves = []
        for h in range(2):
            rows = pl.ds(h * 128, 128)
            x = [[pltpu.roll(source[p, tile + t, pl.ds(row + h * 128, 128), :], back, 1) for t in range(3)]
                 for p in range(2)]
            picked = [[jnp.where(lane < 128 - shift, x[p][t], x[p][t + 1]) for t in range(2)] for p in range(2)]
            waves = []
            for t in range(2):
                lanes = pl.ds(128 * t, 128)
                pr, pi = ill[0, rows, lanes], ill[1, rows, lanes]
                a, b = picked[0][t], picked[1][t]
                patch[0, rows, lanes] = a
                patch[1, rows, lanes] = b
                wr, wi = pr * a - pi * b, pr * b + pi * a
                wave[0, rows, lanes] = wr
                wave[1, rows, lanes] = wi
                waves.append((wr, wi))
            halves.append(waves)
        for t in range(2):
            lanes = pl.ds(128 * t, 128)
            (ar, ai), (br, bi) = halves[0][t], halves[1][t]
            for q, pair in enumerate(((ar + br, ai + bi), (ar - br, ai - bi))):
                for z, value in enumerate(pair):
                    rows = pl.ds(z * 128, 128)
                    h1[q, rows, lanes], l1[q, rows, lanes] = split(value)

    def rows_forward():
        for q in range(2):
            m1[q] = left(mats.at[q, 1], h1[q], l1[q])

    def between_forward():
        for q in range(2):
            ar, br = m1[q, pl.ds(0, 128), pl.ds(0, 128)], m1[q, pl.ds(0, 128), pl.ds(128, 128)]
            ai, bi = m1[q, pl.ds(128, 128), pl.ds(0, 128)], m1[q, pl.ds(128, 128), pl.ds(128, 128)]
            rows = pl.ds(q * 128, 128)
            for e, pair in enumerate(((ar + br, ai + bi), (ar - br, ai - bi))):
                for z, value in enumerate(pair):
                    lanes = pl.ds(z * 128, 128)
                    h2[e, rows, lanes], l2[e, rows, lanes] = split(value)

    def columns_forward():
        for e in range(2):
            m2[e] = right(h2[e], l2[e], mats.at[e, 0])

    def project():
        for q in range(2):
            for e in range(2):
                rows = pl.ds(q * 128, 128)
                fr, fi = m2[e, rows, pl.ds(0, 128)], m2[e, rows, pl.ds(128, 128)]
                f = moduli[slot, rows, pl.ds(e * 128, 128)] * lax.rsqrt(jnp.maximum(fr * fr + fi * fi, 0.25))
                for z, value in enumerate((fr * f, fi * f)):
                    lanes = pl.ds(z * 128, 128)
                    h3[e, rows, lanes], l3[e, rows, lanes] = split(value)

    def columns_back():
        for e in range(2):
            m3[e] = right(h3[e], l3[e], mats.at[e, 1])

    def between_back():
        for q in range(2):
            rows = pl.ds(q * 128, 128)
            er, ei = m3[0, rows, pl.ds(0, 128)], m3[0, rows, pl.ds(128, 128)]
            vr, vi = m3[1, rows, pl.ds(0, 128)], m3[1, rows, pl.ds(128, 128)]
            for t, pair in enumerate(((er + vr, ei + vi), (er - vr, ei - vi))):
                for z, value in enumerate(pair):
                    at, lanes = pl.ds(z * 128, 128), pl.ds(t * 128, 128)
                    h4[q, at, lanes], l4[q, at, lanes] = split(value)

    def rows_back():
        for q in range(2):
            m4[q] = left(mats.at[q, 0], h4[q], l4[q])

    def update():
        out = [[[None] * 2 for _ in range(2)] for _ in range(2)]
        for t in range(2):
            lanes = pl.ds(128 * t, 128)
            er, ei = m4[0, pl.ds(0, 128), lanes], m4[0, pl.ds(128, 128), lanes]
            vr, vi = m4[1, pl.ds(0, 128), lanes], m4[1, pl.ds(128, 128), lanes]
            for h, (xr, xi) in enumerate(((er + vr, ei + vi), (er - vr, ei - vi))):
                rows = pl.ds(h * 128, 128)
                cr, ci = xr - wave[0, rows, lanes], xi - wave[1, rows, lanes]
                if live is not None:
                    cr, ci = cr * live, ci * live
                a, b = patch[0, rows, lanes], patch[1, rows, lanes]
                pterm[0, t, rows, :] += a * cr + b * ci
                pterm[1, t, rows, :] += a * ci - b * cr
                pr, pi = ill[0, rows, lanes], ill[1, rows, lanes]
                out[h][0][t] = pr * cr + pi * ci
                out[h][1][t] = pr * ci - pi * cr
        for h in range(2):
            for z in range(2):
                place(z, h, out[h][z])

    return (cut, rows_forward, between_forward, columns_forward, project,
            columns_back, between_back, rows_back, update)


def places(offs):
    return lambda s: offs[0, s], lambda s: offs[1, s]


def together(*windows):
    for steps in zip(*windows):
        for step in steps:
            step()


def deposit(grad, row, col, z, h, values):
    tile = col // 128
    shift = col % 128
    low = lax.broadcasted_iota(jnp.int32, (128, 128), 1) < shift
    first, second = (pltpu.roll(v, shift, 1) for v in values)
    rows = pl.ds(row + h * 128, 128)
    grad[z, tile, rows, :] += jnp.where(low, 0.0, first)
    grad[z, tile + 1, rows, :] += jnp.where(low, first, second)
    grad[z, tile + 2, rows, :] += jnp.where(low, second, 0.0)


def window_kernel(offs, count, ext, ill, mats, moduli, near, near_term, grad, pterm, todo, done, *bufs):
    n = count[0]
    row_of, col_of = places(offs)

    @pl.loop(0, 96)
    def _(i):
        rows = pl.ds(pl.multiple_of(8 * i, 8), 8)
        for p in range(2):
            for t in range(6):
                grad[p, t, rows, :] = jnp.zeros((8, 128), F32)

    pterm[...] = near_term[...]

    def sort(s, counts):
        left_over, taken = counts
        r = row_of(s)
        inside = jnp.logical_and(jnp.logical_and(r >= 128, r <= 384), s < n)
        inside = jnp.logical_and(inside, taken < NEAR)
        todo[left_over] = s
        done[taken] = s
        return (left_over + jnp.logical_and(s < n, jnp.logical_not(inside)).astype(jnp.int32),
                taken + inside.astype(jnp.int32))

    left_over, taken = lax.fori_loop(0, 16, sort, (jnp.int32(0), jnp.int32(0)))

    @pl.loop(0, taken)
    def _(i):
        s = done[i]
        for h in range(2):
            for z in range(2):
                deposit(grad, row_of(s), col_of(s), z, h, [near[i, z, t, pl.ds(h * 128, 128), :] for t in range(2)])

    @pl.loop(0, (left_over + 1) // 2)
    def _(k):
        windows = []
        for i in range(2):
            s = todo[jnp.minimum(2 * k + i, left_over - 1)]
            row, col = row_of(s), col_of(s)
            live = None if i == 0 else jnp.where(2 * k + i < left_over, 1.0, 0.0).astype(F32)

            def place(z, h, values, row=row, col=col):
                deposit(grad, row, col, z, h, values)

            windows.append(stages(s, row, col, live, ext, ill, mats, moduli, pterm, place,
                                  bufs[BUFFERS * i:BUFFERS * (i + 1)]))
        together(*windows)


def windows(offs, count, ext, ill, mats, moduli, near, near_term):
    V = pl.BlockSpec(memory_space=pltpu.VMEM)
    S = pl.BlockSpec(memory_space=pltpu.SMEM)
    return pl.pallas_call(
        window_kernel,
        out_shape=(jax.ShapeDtypeStruct((2, 6, 768, 128), F32), jax.ShapeDtypeStruct((2, 2, 256, 128), F32)),
        in_specs=[S, S, V, V, V, V, V, V], out_specs=(V, V),
        scratch_shapes=[pltpu.SMEM((16,), jnp.int32), pltpu.SMEM((16,), jnp.int32)] + buffers() * 2,
        compiler_params=pltpu.CompilerParams(vmem_limit_bytes=28 * 2**20),
    )(offs, count, ext, ill, mats, moduli, near, near_term)


def remote(src, dst, send_sem, recv_sem, device):
    return pltpu.make_async_remote_copy(
        src_ref=src, dst_ref=dst, send_sem=send_sem, recv_sem=recv_sem,
        device_id=device, device_id_type=MESH,
    )


def greet(devices):
    barrier = pltpu.get_barrier_semaphore()
    expected = 0
    for condition, device in devices:
        if condition is None:
            pl.semaphore_signal(barrier, inc=1, device_id=device, device_id_type=MESH)
            expected = expected + 1
        else:
            @pl.when(condition)
            def _(device=device):
                pl.semaphore_signal(barrier, inc=1, device_id=device, device_id_type=MESH)
            expected = expected + condition.astype(jnp.int32)
    return barrier, expected


def neighbours():
    a = lax.axis_index("ty")
    b = lax.axis_index("tx")
    has = {"up": a > 0, "down": a < 15, "left": b > 0, "right": b < 15}
    ids = {"up": (jnp.maximum(a - 1, 0), b), "down": (jnp.minimum(a + 1, 15), b),
           "left": (a, jnp.maximum(b - 1, 0)), "right": (a, jnp.minimum(b + 1, 15))}
    return a, b, has, ids


OPPOSITE = {"up": "down", "down": "up", "left": "right", "right": "left"}


def halo_kernel(offs, count, tile, meas, ill, mats, ext, moduli, near, near_term,
                mid, mbuf, meas_sem, own_sem, mid_sem, row_send, row_recv, col_send, col_recv, cor_send, cor_recv, *bufs):
    a, b, has, ids = neighbours()
    barrier, expected = greet([(has[k], ids[k]) for k in ids])
    own = [pltpu.make_async_copy(tile.at[:, :, pl.ds(128 * t, 128)], mid.at[:, 1 + t], own_sem.at[t]) for t in range(4)]
    for copy in own:
        copy.start()

    def fetch(s, t):
        return pltpu.make_async_copy(meas.at[s, :, pl.ds(128 * t, 128)], mbuf.at[s, t], meas_sem.at[s, t])

    @pl.loop(0, 16)
    def _(s):
        for t in range(2):
            fetch(s, t).start()

    pl.semaphore_wait(barrier, expected)
    rows, cols, corners = {}, {}, {}
    for i, way in enumerate(("down", "up")):
        src_row, dst_row = (384, 0) if way == "down" else (0, 640)
        for t in (0, 3, 1, 2):
            rows[way, t] = remote(
                tile.at[:, pl.ds(src_row, 128), pl.ds(128 * t, 128)],
                ext.at[:, 1 + t, pl.ds(dst_row, 128), :],
                row_send.at[i, t], row_recv.at[i, t], ids[way])
    for i, way in enumerate(("right", "left")):
        src_t, dst_t = (3, 0) if way == "right" else (0, 5)
        cols[way] = remote(
            tile.at[:, :, pl.ds(128 * src_t, 128)], mid.at[:, dst_t],
            col_send.at[i], col_recv.at[i], ids[way])
        for j, row in enumerate((0, 640)):
            corners[way, j] = remote(
                ext.at[:, 1 + src_t, pl.ds(row, 128), :], ext.at[:, dst_t, pl.ds(row, 128), :],
                cor_send.at[i, j], cor_recv.at[i, j], ids[way])
    outer = jnp.logical_or((b // 2) % 4 == 0, (b // 2) % 4 == 3)

    inner = jnp.logical_not(outer)

    def start_rows(mine, tiles):
        for t in tiles:
            for way in ("down", "up"):
                pl.when(jnp.logical_and(has[way], mine))(rows[way, t].start)

    for way in ("right", "left"):
        pl.when(has[way])(cols[way].start)
    start_rows(inner, (0, 3))
    near_term[...] = jnp.zeros_like(near_term)
    for side in ("right", "left"):
        pl.when(has[side])(cols[side].wait_send)
        pl.when(has[OPPOSITE[side]])(cols[side].wait_recv)
    start_rows(outer, (0, 3))
    for copy in own:
        copy.wait()
    centre = pltpu.make_async_copy(mid, ext.at[:, :, pl.ds(128, 512), :], mid_sem)
    centre.start()
    to = lax.broadcasted_iota(jnp.int32, (256, 256), 1)
    source = 2 * (to % 128) + to // 128
    perm = jnp.where(lax.broadcasted_iota(jnp.int32, (256, 256), 0) == source, 1.0, 0.0).astype(BF)

    @pl.loop(0, 16)
    def _(s):
        for t in range(2):
            fetch(s, t).wait()
        for q in range(2):
            picked = jnp.concatenate([mbuf[s, t, pl.ds(q, 128, stride=2), :] for t in range(2)], axis=1)
            high, low = split(picked)
            moduli[s, pl.ds(128 * q, 128), :] = dot(high, perm) + dot(low, perm)

    n = count[0]
    row_of, col_of = places(offs)
    inside, rank, total = [], [], jnp.int32(0)
    for s in range(16):
        r = row_of(s)
        ok = jnp.logical_and(jnp.logical_and(r >= 128, r <= 384), s < n).astype(jnp.int32)
        inside.append(ok)
        rank.append(total)
        total = total + ok

    @pl.loop(0, NEAR // 2)
    def _(k):
        def sent_edges(mine):
            for way in ("down", "up"):
                for t in (0, 3):
                    pl.when(jnp.logical_and(has[way], mine))(rows[way, t].wait_send)

        @pl.when(k == 1)
        def _():
            sent_edges(inner)
            start_rows(inner, (1, 2))

        @pl.when(k == 2)
        def _():
            sent_edges(outer)
            for j, way in enumerate(("down", "up")):
                @pl.when(has[OPPOSITE[way]])
                def _(way=way):
                    rows[way, 0].wait_recv()
                    rows[way, 3].wait_recv()
                for side in ("right", "left"):
                    pl.when(jnp.logical_and(has[side], has[OPPOSITE[way]]))(corners[side, j].start)
            start_rows(outer, (1, 2))

        taken = []
        for i in range(2):
            at = 2 * k + i
            slot = jnp.int32(0)
            for s in range(1, 16):
                slot = slot + s * inside[s] * (rank[s] == at).astype(jnp.int32)
            row = jnp.clip(row_of(slot) - 128, 0, 256)
            live = (at < total).astype(F32)

            def place(z, h, values, at=at):
                for t in range(2):
                    near[at, z, t, pl.ds(h * 128, 128), :] = values[t]

            taken.append(stages(slot, row, col_of(slot), live, mid, ill, mats, moduli, near_term, place,
                                bufs[BUFFERS * i:BUFFERS * (i + 1)]))
        together(*taken)

    for way in ("down", "up"):
        for t in (1, 2):
            pl.when(has[OPPOSITE[way]])(rows[way, t].wait_recv)
            pl.when(has[way])(rows[way, t].wait_send)
    for side in ("right", "left"):
        for j, way in enumerate(("down", "up")):
            pl.when(jnp.logical_and(has[OPPOSITE[side]], has[OPPOSITE[way]]))(corners[side, j].wait_recv)
            pl.when(jnp.logical_and(has[side], has[OPPOSITE[way]]))(corners[side, j].wait_send)
    centre.wait()


def halo(offs, count, tile, meas, ill, mats):
    D = pltpu.SemaphoreType.DMA
    A = pl.BlockSpec(memory_space=pl.ANY)
    V = pl.BlockSpec(memory_space=pltpu.VMEM)
    S = pl.BlockSpec(memory_space=pltpu.SMEM)
    return pl.pallas_call(
        halo_kernel,
        out_shape=(jax.ShapeDtypeStruct((2, 6, 768, 128), F32), jax.ShapeDtypeStruct((16, 256, 256), F32),
                   jax.ShapeDtypeStruct((NEAR, 2, 2, 256, 128), F32), jax.ShapeDtypeStruct((2, 2, 256, 128), F32)),
        in_specs=[S, S, A, A, V, V], out_specs=(V, V, V, V),
        scratch_shapes=[pltpu.VMEM((2, 6, 512, 128), F32), pltpu.VMEM((16, 2, 256, 128), F32), D((16, 2)),
                        D((4,)), D, D((2, 4)), D((2, 4)), D((2,)), D((2,)), D((2, 2)), D((2, 2))] + buffers() * 2,
        compiler_params=pltpu.CompilerParams(collective_id=1, has_side_effects=True, vmem_limit_bytes=26 * 2**20),
    )(offs, count, tile, meas, ill, mats)


def partners(b):
    core = b % 2
    x = (b // 2) % 4
    zlo = b // 8
    return core, x, zlo


def finish_kernel(spec, ill, grad, pterm, newspec, newill,
                  rxc, rxm, rz, edge, rcore, rx, sumc, part, rc, total,
                  core_s, core_r, xs, xr, cs, cr, ms, mr, zs, zr,
                  us, ur, ds, dr, es, er, fs, fr):
    a, b, has, ids = neighbours()
    core, x, zlo = partners(b)
    low = x * 2 + core
    unit = zlo * 16 + a

    def member(d):
        u = (unit + d) % 32
        return (u % 16, (u // 16) * 8 + low)

    mates = [(a, zlo * 8 + ((x + d) % 4) * 2 + core) for d in (1, 2, 3)]
    other = (a, zlo * 8 + x * 2 + (1 - core))
    barrier, expected = greet([(None, m) for m in mates] + [(None, other)]
                              + [(jnp.logical_and(core == 0, has["left"]), ids["left"]),
                                 (jnp.logical_and(core == 1, has["right"]), ids["right"])])

    @pl.loop(1, 32)
    def _(d):
        pl.semaphore_signal(barrier, inc=1, device_id=member(d), device_id_type=MESH)

    power = jnp.sum(ill[0] * ill[0] + ill[1] * ill[1]) * (1.0 / 65536) + 1e-05
    inv = 1.0 / power
    pl.semaphore_wait(barrier, expected + 31)
    first = remote(pterm.at[1 - core], rcore, core_s, core_r, other)
    corner, middle, vert = {}, {}, {}
    for i, side in enumerate(("right", "left")):
        src_t = 5 if side == "right" else 0
        for j, row in enumerate((0, 640)):
            corner[side, j] = remote(grad.at[:, src_t, pl.ds(row, 128), :], rxc.at[i, j],
                                     cs.at[i, j], cr.at[i, j], ids[side])
        middle[side] = remote(grad.at[:, src_t, pl.ds(128, 512), :], rxm.at[i], ms.at[i], mr.at[i], ids[side])
    for j, way in enumerate(("up", "down")):
        row = 0 if way == "up" else 640
        for t in range(4):
            src = edge.at[j, t // 3] if t in (0, 3) else grad.at[:, 1 + t, pl.ds(row, 128), :]
            vert[way, t] = remote(src, rz.at[j, :, t], zs.at[j, t], zr.at[j, t], ids[way])

    outer = jnp.logical_or(x == 0, x == 3)
    inner = jnp.logical_not(outer)
    crossing = {"right": b == 7, "left": b == 8}

    def send_vert(t, mine):
        for way in ("up", "down"):
            pl.when(jnp.logical_and(has[way], mine))(vert[way, t].start)

    def add_vert(t):
        for j, (way, row) in enumerate((("up", 384), ("down", 0))):
            @pl.when(has[OPPOSITE[way]])
            def _(j=j, way=way, row=row):
                vert[way, t].wait_recv()
                newspec[:, row:row + 128, 128 * t:128 * t + 128] += inv * rz[j, :, t]

    first.start()
    for side in ("right", "left"):
        pl.when(crossing[side])(middle[side].start)
    send_vert(1, inner)
    first.wait_recv()
    sumc[...] = pterm[core] + rcore[...]
    xsend = [remote(sumc.at[(x + d) % 4], rx.at[d - 1], xs.at[d - 1], xr.at[d - 1], mates[d - 1]) for d in (1, 2, 3)]
    for copy in xsend:
        copy.start()
    for side in ("right", "left"):
        for j in range(2):
            pl.when(has[side])(corner[side, j].start)
    for copy in xsend:
        copy.wait_recv()
    part[...] = sumc[x] + rx[0] + rx[1] + rx[2]

    @pl.loop(1, 32)
    def _(d):
        device = member(d)
        remote(part.at[device[0]], rc.at[d - 1], us, ur, device).start()

    send_vert(1, outer)
    send_vert(2, inner)
    for side in ("right", "left"):
        pl.when(jnp.logical_and(has[side], jnp.logical_not(crossing[side])))(middle[side].start)

    @pl.loop(0, 16)
    def _(i):
        rows = pl.ds(pl.multiple_of(32 * i, 32), 32)
        more = pl.ds(pl.multiple_of(32 * i + 128, 32), 32)
        for p in range(2):
            for t in range(4):
                lanes = pl.ds(128 * t, 128)
                newspec[p, rows, lanes] = spec[p, rows, lanes] + inv * grad[p, 1 + t, more, :]

    for j, row in enumerate((0, 640)):
        for k, (t, side) in enumerate(((1, "right"), (4, "left"))):
            edge[j, k] = grad[:, t, row:row + 128, :]
            @pl.when(has[OPPOSITE[side]])
            def _(j=j, k=k, side=side):
                corner[side, j].wait_recv()
                edge[j, k] += rxc[k, j]
    whole = remote(rc, rc, us, ur, other)
    whole.wait_recv()
    acc = part[a]
    for i in range(31):
        acc = acc + rc[i]
    total[core, x, a] = acc

    @pl.loop(1, 16)
    def _(d):
        remote(total.at[core, x, a], total.at[core, x, a], ds, dr, ((a + d) % 16, b)).start()

    send_vert(2, outer)
    send_vert(0, has["up"] | has["down"])
    send_vert(3, has["up"] | has["down"])
    for k, (side, t) in enumerate((("right", 0), ("left", 3))):
        @pl.when(has[OPPOSITE[side]])
        def _(k=k, side=side, t=t):
            middle[side].wait_recv()
            newspec[:, :, 128 * t:128 * t + 128] += inv * rxm[k]
    some = remote(rc.at[pl.ds(0, 15)], rc.at[pl.ds(0, 15)], ds, dr, other)
    some.wait_recv()
    gather = [remote(total.at[core, x], total.at[core, x], es.at[d - 1], er.at[d - 1], mates[d - 1]) for d in (1, 2, 3)]
    for copy in gather:
        copy.start()
    add_vert(1)
    add_vert(2)
    for copy in gather:
        copy.wait_recv()
    last = remote(total.at[core], total.at[core], fs, fr, other)
    last.start()
    last.wait()
    for p in range(2):
        for s in range(4):
            rows, lanes = pl.ds((s % 2) * 128, 128), pl.ds((s // 2) * 128, 128)
            newill[p, rows, lanes] = ill[p, rows, lanes] + total[p, s].reshape(128, 128) * (1.0 / 64)
    add_vert(0)
    add_vert(3)
    first.wait_send()
    for copy in xsend + gather:
        copy.wait_send()
    whole.wait_send()
    some.wait_send()
    for side in ("right", "left"):
        for j in range(2):
            pl.when(has[side])(corner[side, j].wait_send)
        pl.when(has[side])(middle[side].wait_send)
    for way in ("up", "down"):
        for t in range(4):
            pl.when(has[way])(vert[way, t].wait_send)


def finish(spec, ill, grad, pterm):
    D = pltpu.SemaphoreType.DMA
    V = pl.BlockSpec(memory_space=pltpu.VMEM)
    return pl.pallas_call(
        finish_kernel,
        out_shape=(jax.ShapeDtypeStruct((2, 512, 512), F32), jax.ShapeDtypeStruct((2, 256, 256), F32)),
        in_specs=[V, V, V, V], out_specs=(V, V),
        scratch_shapes=[
            pltpu.VMEM((2, 2, 2, 128, 128), F32), pltpu.VMEM((2, 2, 512, 128), F32),
            pltpu.VMEM((2, 2, 4, 128, 128), F32), pltpu.VMEM((2, 2, 2, 128, 128), F32),
            pltpu.VMEM((4, 16, 8, 128), F32), pltpu.VMEM((3, 16, 8, 128), F32), pltpu.VMEM((4, 16, 8, 128), F32),
            pltpu.VMEM((16, 8, 128), F32), pltpu.VMEM((31, 8, 128), F32), pltpu.VMEM((2, 4, 16, 8, 128), F32),
            D, D, D((3,)), D((3,)), D((2, 2)), D((2, 2)), D((2,)), D((2,)), D((2, 4)), D((2, 4)),
            D, D, D, D, D((3,)), D((3,)), D, D,
        ],
        compiler_params=pltpu.CompilerParams(collective_id=2, has_side_effects=True, vmem_limit_bytes=32 * 2**20),
    )(spec, ill, grad, pterm)


def shards(specimen, illumination, scan_offsets, slot_counts, measured):
    anchor = jnp.stack([lax.axis_index("ty") * 512, lax.axis_index("tx") * 512]) - 128
    local = scan_offsets[0, 0] - anchor[:, None]
    count = slot_counts[0]
    mats = jnp.asarray(consts())
    ext, moduli, near, near_term = halo(local, count, specimen, measured[0, 0], illumination, mats)
    grad, probe_term = windows(local, count, ext, illumination, mats, moduli, near, near_term)
    return finish(specimen, illumination, grad, probe_term.reshape(2, 4, 16, 8, 128))


def solution(mesh):
    in_specs = (
        P(None, "ty", "tx"),
        P(),
        P("ty", "tx", None, None),
        P("ty", "tx"),
        P("ty", "tx", None, None, None),
    )
    out_specs = (P(None, "ty", "tx"), P())
    return jax.shard_map(shards, mesh=mesh, in_specs=in_specs, out_specs=out_specs, check_vma=False)
```

```python
import math
import numpy as np
import jax, jax.numpy as jnp
from jax import lax
from jax.experimental import pallas as pl
from jax.experimental.pallas import tpu as pltpu
from jax.sharding import PartitionSpec as P
import ml_dtypes

F32 = jnp.float32
BF = jnp.bfloat16
MESH = pl.DeviceIdType.MESH
NEAR = 10


def consts():
    n = np.arange(128)
    out = []
    for odd in (0, 1):
        angle = 2 * np.pi * (np.outer(n, 2 * n + odd) % 256) / 256
        real, imag = np.cos(angle) / 16, -np.sin(angle) / 16
        block = np.block([[real, imag], [-imag, real]])
        for m in (block, block.T):
            m = m.astype(np.float32)
            high = m.astype(ml_dtypes.bfloat16)
            low = (m - high.astype(np.float32)).astype(ml_dtypes.bfloat16)
            out.append(np.stack([high, low]))
    mats = np.stack(out).reshape(2, 2, 2, 256, 256)
    return mats


def split(x):
    high = x.astype(BF)
    return high, (x - high.astype(F32)).astype(BF)


def dot(a, b):
    return jnp.dot(a, b, preferred_element_type=F32)


def left(mats, high, low):
    x = dot(jnp.concatenate([mats[0], mats[1]], axis=0), high)
    return x[:256] + x[256:] + dot(mats[0], low)


def right(high, low, mats):
    x = dot(jnp.concatenate([high, low], axis=0), mats[0])
    return x[:256] + x[256:] + dot(high, mats[1])


BUFFERS = 14


def buffers():
    whole = pltpu.VMEM((2, 256, 256), F32)
    half = pltpu.VMEM((2, 256, 256), BF)
    return [whole, whole] + [half, half, whole] * 4


def stages(slot, row, col, live, source, ill, mats, moduli, pterm, place, bufs):
    patch, wave, h1, l1, m1, h2, l2, m2, h3, l3, m3, h4, l4, m4 = bufs
    tile = col // 128
    shift = col % 128
    back = (128 - shift) % 128
    lane = lax.broadcasted_iota(jnp.int32, (128, 128), 1)

    def cut():
        halves = []
        for h in range(2):
            rows = pl.ds(h * 128, 128)
            x = [[pltpu.roll(source[p, tile + t, pl.ds(row + h * 128, 128), :], back, 1) for t in range(3)]
                 for p in range(2)]
            picked = [[jnp.where(lane < 128 - shift, x[p][t], x[p][t + 1]) for t in range(2)] for p in range(2)]
            waves = []
            for t in range(2):
                lanes = pl.ds(128 * t, 128)
                pr, pi = ill[0, rows, lanes], ill[1, rows, lanes]
                a, b = picked[0][t], picked[1][t]
                patch[0, rows, lanes] = a
                patch[1, rows, lanes] = b
                wr, wi = pr * a - pi * b, pr * b + pi * a
                wave[0, rows, lanes] = wr
                wave[1, rows, lanes] = wi
                waves.append((wr, wi))
            halves.append(waves)
        for t in range(2):
            lanes = pl.ds(128 * t, 128)
            (ar, ai), (br, bi) = halves[0][t], halves[1][t]
            for q, pair in enumerate(((ar + br, ai + bi), (ar - br, ai - bi))):
                for z, value in enumerate(pair):
                    rows = pl.ds(z * 128, 128)
                    h1[q, rows, lanes], l1[q, rows, lanes] = split(value)

    def rows_forward():
        for q in range(2):
            m1[q] = left(mats.at[q, 1], h1[q], l1[q])

    def between_forward():
        for q in range(2):
            ar, br = m1[q, pl.ds(0, 128), pl.ds(0, 128)], m1[q, pl.ds(0, 128), pl.ds(128, 128)]
            ai, bi = m1[q, pl.ds(128, 128), pl.ds(0, 128)], m1[q, pl.ds(128, 128), pl.ds(128, 128)]
            rows = pl.ds(q * 128, 128)
            for e, pair in enumerate(((ar + br, ai + bi), (ar - br, ai - bi))):
                for z, value in enumerate(pair):
                    lanes = pl.ds(z * 128, 128)
                    h2[e, rows, lanes], l2[e, rows, lanes] = split(value)

    def columns_forward():
        for e in range(2):
            m2[e] = right(h2[e], l2[e], mats.at[e, 0])

    def project():
        for q in range(2):
            for e in range(2):
                rows = pl.ds(q * 128, 128)
                fr, fi = m2[e, rows, pl.ds(0, 128)], m2[e, rows, pl.ds(128, 128)]
                f = moduli[slot, rows, pl.ds(e * 128, 128)] * lax.rsqrt(jnp.maximum(fr * fr + fi * fi, 0.25))
                for z, value in enumerate((fr * f, fi * f)):
                    lanes = pl.ds(z * 128, 128)
                    h3[e, rows, lanes], l3[e, rows, lanes] = split(value)

    def columns_back():
        for e in range(2):
            m3[e] = right(h3[e], l3[e], mats.at[e, 1])

    def between_back():
        for q in range(2):
            rows = pl.ds(q * 128, 128)
            er, ei = m3[0, rows, pl.ds(0, 128)], m3[0, rows, pl.ds(128, 128)]
            vr, vi = m3[1, rows, pl.ds(0, 128)], m3[1, rows, pl.ds(128, 128)]
            for t, pair in enumerate(((er + vr, ei + vi), (er - vr, ei - vi))):
                for z, value in enumerate(pair):
                    at, lanes = pl.ds(z * 128, 128), pl.ds(t * 128, 128)
                    h4[q, at, lanes], l4[q, at, lanes] = split(value)

    def rows_back():
        for q in range(2):
            m4[q] = left(mats.at[q, 0], h4[q], l4[q])

    def update():
        out = [[[None] * 2 for _ in range(2)] for _ in range(2)]
        for t in range(2):
            lanes = pl.ds(128 * t, 128)
            er, ei = m4[0, pl.ds(0, 128), lanes], m4[0, pl.ds(128, 128), lanes]
            vr, vi = m4[1, pl.ds(0, 128), lanes], m4[1, pl.ds(128, 128), lanes]
            for h, (xr, xi) in enumerate(((er + vr, ei + vi), (er - vr, ei - vi))):
                rows = pl.ds(h * 128, 128)
                cr, ci = xr - wave[0, rows, lanes], xi - wave[1, rows, lanes]
                if live is not None:
                    cr, ci = cr * live, ci * live
                a, b = patch[0, rows, lanes], patch[1, rows, lanes]
                pterm[0, t, rows, :] += a * cr + b * ci
                pterm[1, t, rows, :] += a * ci - b * cr
                pr, pi = ill[0, rows, lanes], ill[1, rows, lanes]
                out[h][0][t] = pr * cr + pi * ci
                out[h][1][t] = pr * ci - pi * cr
        for h in range(2):
            for z in range(2):
                place(z, h, out[h][z])

    return (cut, rows_forward, between_forward, columns_forward, project,
            columns_back, between_back, rows_back, update)


def places(offs):
    return lambda s: offs[0, s], lambda s: offs[1, s]


def together(*windows):
    for steps in zip(*windows):
        for step in steps:
            step()


def deposit(grad, row, col, z, h, values):
    tile = col // 128
    shift = col % 128
    low = lax.broadcasted_iota(jnp.int32, (128, 128), 1) < shift
    first, second = (pltpu.roll(v, shift, 1) for v in values)
    rows = pl.ds(row + h * 128, 128)
    grad[z, tile, rows, :] += jnp.where(low, 0.0, first)
    grad[z, tile + 1, rows, :] += jnp.where(low, first, second)
    grad[z, tile + 2, rows, :] += jnp.where(low, second, 0.0)


def window_kernel(offs, count, ext, ill, mats, moduli, near, near_term, grad, pterm, todo, done, *bufs):
    n = count[0]
    row_of, col_of = places(offs)

    @pl.loop(0, 96)
    def _(i):
        rows = pl.ds(pl.multiple_of(8 * i, 8), 8)
        for p in range(2):
            for t in range(6):
                grad[p, t, rows, :] = jnp.zeros((8, 128), F32)

    pterm[...] = near_term[...]

    def sort(s, counts):
        left_over, taken = counts
        r = row_of(s)
        inside = jnp.logical_and(jnp.logical_and(r >= 128, r <= 384), s < n)
        inside = jnp.logical_and(inside, taken < NEAR)
        todo[left_over] = s
        done[taken] = s
        return (left_over + jnp.logical_and(s < n, jnp.logical_not(inside)).astype(jnp.int32),
                taken + inside.astype(jnp.int32))

    left_over, taken = lax.fori_loop(0, 16, sort, (jnp.int32(0), jnp.int32(0)))

    @pl.loop(0, taken)
    def _(i):
        s = done[i]
        for h in range(2):
            for z in range(2):
                deposit(grad, row_of(s), col_of(s), z, h, [near[i, z, t, pl.ds(h * 128, 128), :] for t in range(2)])

    @pl.loop(0, (left_over + 1) // 2)
    def _(k):
        windows = []
        for i in range(2):
            s = todo[jnp.minimum(2 * k + i, left_over - 1)]
            row, col = row_of(s), col_of(s)
            live = None if i == 0 else jnp.where(2 * k + i < left_over, 1.0, 0.0).astype(F32)

            def place(z, h, values, row=row, col=col):
                deposit(grad, row, col, z, h, values)

            windows.append(stages(s, row, col, live, ext, ill, mats, moduli, pterm, place,
                                  bufs[BUFFERS * i:BUFFERS * (i + 1)]))
        together(*windows)


def windows(offs, count, ext, ill, mats, moduli, near, near_term):
    V = pl.BlockSpec(memory_space=pltpu.VMEM)
    S = pl.BlockSpec(memory_space=pltpu.SMEM)
    return pl.pallas_call(
        window_kernel,
        out_shape=(jax.ShapeDtypeStruct((2, 6, 768, 128), F32), jax.ShapeDtypeStruct((2, 2, 256, 128), F32)),
        in_specs=[S, S, V, V, V, V, V, V], out_specs=(V, V),
        scratch_shapes=[pltpu.SMEM((16,), jnp.int32), pltpu.SMEM((16,), jnp.int32)] + buffers() * 2,
        compiler_params=pltpu.CompilerParams(vmem_limit_bytes=28 * 2**20),
    )(offs, count, ext, ill, mats, moduli, near, near_term)


def remote(src, dst, send_sem, recv_sem, device):
    return pltpu.make_async_remote_copy(
        src_ref=src, dst_ref=dst, send_sem=send_sem, recv_sem=recv_sem,
        device_id=device, device_id_type=MESH,
    )


def greet(devices):
    barrier = pltpu.get_barrier_semaphore()
    expected = 0
    for condition, device in devices:
        if condition is None:
            pl.semaphore_signal(barrier, inc=1, device_id=device, device_id_type=MESH)
            expected = expected + 1
        else:
            @pl.when(condition)
            def _(device=device):
                pl.semaphore_signal(barrier, inc=1, device_id=device, device_id_type=MESH)
            expected = expected + condition.astype(jnp.int32)
    return barrier, expected


def neighbours():
    a = lax.axis_index("ty")
    b = lax.axis_index("tx")
    has = {"up": a > 0, "down": a < 15, "left": b > 0, "right": b < 15}
    ids = {"up": (jnp.maximum(a - 1, 0), b), "down": (jnp.minimum(a + 1, 15), b),
           "left": (a, jnp.maximum(b - 1, 0)), "right": (a, jnp.minimum(b + 1, 15))}
    return a, b, has, ids


OPPOSITE = {"up": "down", "down": "up", "left": "right", "right": "left"}


def halo_kernel(offs, count, tile, meas, ill, mats, ext, moduli, near, near_term,
                mid, mbuf, meas_sem, own_sem, mid_sem, row_send, row_recv, col_send, col_recv, cor_send, cor_recv, *bufs):
    a, b, has, ids = neighbours()
    barrier, expected = greet([(has[k], ids[k]) for k in ids])
    own = [pltpu.make_async_copy(tile.at[:, :, pl.ds(128 * t, 128)], mid.at[:, 1 + t], own_sem.at[t]) for t in range(4)]
    for copy in own:
        copy.start()

    def fetch(s, t):
        return pltpu.make_async_copy(meas.at[s, :, pl.ds(128 * t, 128)], mbuf.at[s, t], meas_sem.at[s, t])

    @pl.loop(0, 16)
    def _(s):
        for t in range(2):
            fetch(s, t).start()

    pl.semaphore_wait(barrier, expected)
    rows, cols, corners = {}, {}, {}
    for i, way in enumerate(("down", "up")):
        src_row, dst_row = (384, 0) if way == "down" else (0, 640)
        for t in (0, 3, 1, 2):
            rows[way, t] = remote(
                tile.at[:, pl.ds(src_row, 128), pl.ds(128 * t, 128)],
                ext.at[:, 1 + t, pl.ds(dst_row, 128), :],
                row_send.at[i, t], row_recv.at[i, t], ids[way])
    for i, way in enumerate(("right", "left")):
        src_t, dst_t = (3, 0) if way == "right" else (0, 5)
        cols[way] = remote(
            tile.at[:, :, pl.ds(128 * src_t, 128)], mid.at[:, dst_t],
            col_send.at[i], col_recv.at[i], ids[way])
        for j, row in enumerate((0, 640)):
            corners[way, j] = remote(
                ext.at[:, 1 + src_t, pl.ds(row, 128), :], ext.at[:, dst_t, pl.ds(row, 128), :],
                cor_send.at[i, j], cor_recv.at[i, j], ids[way])
    outer = jnp.logical_or((b // 2) % 4 == 0, (b // 2) % 4 == 3)

    inner = jnp.logical_not(outer)

    def start_rows(mine, tiles):
        for t in tiles:
            for way in ("down", "up"):
                pl.when(jnp.logical_and(has[way], mine))(rows[way, t].start)

    for way in ("right", "left"):
        pl.when(has[way])(cols[way].start)
    start_rows(inner, (0, 3))
    near_term[...] = jnp.zeros_like(near_term)
    for side in ("right", "left"):
        pl.when(has[side])(cols[side].wait_send)
        pl.when(has[OPPOSITE[side]])(cols[side].wait_recv)
    start_rows(outer, (0, 3))
    for copy in own:
        copy.wait()
    centre = pltpu.make_async_copy(mid, ext.at[:, :, pl.ds(128, 512), :], mid_sem)
    centre.start()
    to = lax.broadcasted_iota(jnp.int32, (256, 256), 1)
    source = 2 * (to % 128) + to // 128
    perm = jnp.where(lax.broadcasted_iota(jnp.int32, (256, 256), 0) == source, 1.0, 0.0).astype(BF)

    @pl.loop(0, 16)
    def _(s):
        for t in range(2):
            fetch(s, t).wait()
        for q in range(2):
            picked = jnp.concatenate([mbuf[s, t, pl.ds(q, 128, stride=2), :] for t in range(2)], axis=1)
            high, low = split(picked)
            moduli[s, pl.ds(128 * q, 128), :] = dot(high, perm) + dot(low, perm)

    n = count[0]
    row_of, col_of = places(offs)
    inside, rank, total = [], [], jnp.int32(0)
    for s in range(16):
        r = row_of(s)
        ok = jnp.logical_and(jnp.logical_and(r >= 128, r <= 384), s < n).astype(jnp.int32)
        inside.append(ok)
        rank.append(total)
        total = total + ok

    @pl.loop(0, NEAR // 2)
    def _(k):
        def sent_edges(mine):
            for way in ("down", "up"):
                for t in (0, 3):
                    pl.when(jnp.logical_and(has[way], mine))(rows[way, t].wait_send)

        @pl.when(k == 1)
        def _():
            sent_edges(inner)
            start_rows(inner, (1, 2))

        @pl.when(k == 2)
        def _():
            sent_edges(outer)
            for j, way in enumerate(("down", "up")):
                @pl.when(has[OPPOSITE[way]])
                def _(way=way):
                    rows[way, 0].wait_recv()
                    rows[way, 3].wait_recv()
                for side in ("right", "left"):
                    pl.when(jnp.logical_and(has[side], has[OPPOSITE[way]]))(corners[side, j].start)

        @pl.when(k == 3)
        def _():
            start_rows(outer, (1, 2))

        taken = []
        for i in range(2):
            at = 2 * k + i
            slot = jnp.int32(0)
            for s in range(1, 16):
                slot = slot + s * inside[s] * (rank[s] == at).astype(jnp.int32)
            row = jnp.clip(row_of(slot) - 128, 0, 256)
            live = (at < total).astype(F32)

            def place(z, h, values, at=at):
                for t in range(2):
                    near[at, z, t, pl.ds(h * 128, 128), :] = values[t]

            taken.append(stages(slot, row, col_of(slot), live, mid, ill, mats, moduli, near_term, place,
                                bufs[BUFFERS * i:BUFFERS * (i + 1)]))
        together(*taken)

    for way in ("down", "up"):
        for t in (1, 2):
            pl.when(has[OPPOSITE[way]])(rows[way, t].wait_recv)
            pl.when(has[way])(rows[way, t].wait_send)
    for side in ("right", "left"):
        for j, way in enumerate(("down", "up")):
            pl.when(jnp.logical_and(has[OPPOSITE[side]], has[OPPOSITE[way]]))(corners[side, j].wait_recv)
            pl.when(jnp.logical_and(has[side], has[OPPOSITE[way]]))(corners[side, j].wait_send)
    centre.wait()


def halo(offs, count, tile, meas, ill, mats):
    D = pltpu.SemaphoreType.DMA
    A = pl.BlockSpec(memory_space=pl.ANY)
    V = pl.BlockSpec(memory_space=pltpu.VMEM)
    S = pl.BlockSpec(memory_space=pltpu.SMEM)
    return pl.pallas_call(
        halo_kernel,
        out_shape=(jax.ShapeDtypeStruct((2, 6, 768, 128), F32), jax.ShapeDtypeStruct((16, 256, 256), F32),
                   jax.ShapeDtypeStruct((NEAR, 2, 2, 256, 128), F32), jax.ShapeDtypeStruct((2, 2, 256, 128), F32)),
        in_specs=[S, S, A, A, V, V], out_specs=(V, V, V, V),
        scratch_shapes=[pltpu.VMEM((2, 6, 512, 128), F32), pltpu.VMEM((16, 2, 256, 128), F32), D((16, 2)),
                        D((4,)), D, D((2, 4)), D((2, 4)), D((2,)), D((2,)), D((2, 2)), D((2, 2))] + buffers() * 2,
        cost_estimate=pl.CostEstimate(flops=2 * 10**10, bytes_accessed=2 * 10**7, transcendentals=0),
        compiler_params=pltpu.CompilerParams(collective_id=1, has_side_effects=True, vmem_limit_bytes=26 * 2**20),
    )(offs, count, tile, meas, ill, mats)


def partners(b):
    core = b % 2
    x = (b // 2) % 4
    zlo = b // 8
    return core, x, zlo


def finish_kernel(spec, ill, grad, pterm, newspec, newill,
                  rxc, rxm, rz, edge, rcore, rx, sumc, part, rc, total,
                  core_s, core_r, xs, xr, cs, cr, ms, mr, zs, zr,
                  us, ur, ds, dr, es, er, fs, fr):
    a, b, has, ids = neighbours()
    core, x, zlo = partners(b)
    low = x * 2 + core
    unit = zlo * 16 + a

    def member(d):
        u = (unit + d) % 32
        return (u % 16, (u // 16) * 8 + low)

    mates = [(a, zlo * 8 + ((x + d) % 4) * 2 + core) for d in (1, 2, 3)]
    other = (a, zlo * 8 + x * 2 + (1 - core))
    barrier, expected = greet([(None, m) for m in mates] + [(None, other)]
                              + [(jnp.logical_and(core == 0, has["left"]), ids["left"]),
                                 (jnp.logical_and(core == 1, has["right"]), ids["right"])])

    @pl.loop(1, 32)
    def _(d):
        pl.semaphore_signal(barrier, inc=1, device_id=member(d), device_id_type=MESH)

    power = jnp.sum(ill[0] * ill[0] + ill[1] * ill[1]) * (1.0 / 65536) + 1e-05
    inv = 1.0 / power
    pl.semaphore_wait(barrier, expected + 31)
    first = remote(pterm.at[1 - core], rcore, core_s, core_r, other)
    corner, middle, vert = {}, {}, {}
    for i, side in enumerate(("right", "left")):
        src_t = 5 if side == "right" else 0
        for j, row in enumerate((0, 640)):
            corner[side, j] = remote(grad.at[:, src_t, pl.ds(row, 128), :], rxc.at[i, j],
                                     cs.at[i, j], cr.at[i, j], ids[side])
        middle[side] = remote(grad.at[:, src_t, pl.ds(128, 512), :], rxm.at[i], ms.at[i], mr.at[i], ids[side])
    for j, way in enumerate(("up", "down")):
        row = 0 if way == "up" else 640
        for t in range(4):
            src = edge.at[j, t // 3] if t in (0, 3) else grad.at[:, 1 + t, pl.ds(row, 128), :]
            vert[way, t] = remote(src, rz.at[j, :, t], zs.at[j, t], zr.at[j, t], ids[way])

    outer = jnp.logical_or(x == 0, x == 3)
    inner = jnp.logical_not(outer)
    crossing = {"right": b == 7, "left": b == 8}

    def send_vert(t, mine):
        for way in ("up", "down"):
            pl.when(jnp.logical_and(has[way], mine))(vert[way, t].start)

    def add_vert(t):
        for j, (way, row) in enumerate((("up", 384), ("down", 0))):
            @pl.when(has[OPPOSITE[way]])
            def _(j=j, way=way, row=row):
                vert[way, t].wait_recv()
                newspec[:, row:row + 128, 128 * t:128 * t + 128] += inv * rz[j, :, t]

    first.start()
    for side in ("right", "left"):
        pl.when(crossing[side])(middle[side].start)
    send_vert(1, inner)
    first.wait_recv()
    sumc[...] = pterm[core] + rcore[...]
    xsend = [remote(sumc.at[(x + d) % 4], rx.at[d - 1], xs.at[d - 1], xr.at[d - 1], mates[d - 1]) for d in (1, 2, 3)]
    for copy in xsend:
        copy.start()
    for side in ("right", "left"):
        for j in range(2):
            pl.when(has[side])(corner[side, j].start)
    for copy in xsend:
        copy.wait_recv()
    part[...] = sumc[x] + rx[0] + rx[1] + rx[2]

    @pl.loop(1, 32)
    def _(d):
        device = member(d)
        remote(part.at[device[0]], rc.at[d - 1], us, ur, device).start()

    send_vert(1, outer)
    send_vert(2, inner)
    for side in ("right", "left"):
        pl.when(jnp.logical_and(has[side], jnp.logical_not(crossing[side])))(middle[side].start)

    @pl.loop(0, 16)
    def _(i):
        rows = pl.ds(pl.multiple_of(32 * i, 32), 32)
        more = pl.ds(pl.multiple_of(32 * i + 128, 32), 32)
        for p in range(2):
            for t in range(4):
                lanes = pl.ds(128 * t, 128)
                newspec[p, rows, lanes] = spec[p, rows, lanes] + inv * grad[p, 1 + t, more, :]

    for j, row in enumerate((0, 640)):
        for k, (t, side) in enumerate(((1, "right"), (4, "left"))):
            edge[j, k] = grad[:, t, row:row + 128, :]
            @pl.when(has[OPPOSITE[side]])
            def _(j=j, k=k, side=side):
                corner[side, j].wait_recv()
                edge[j, k] += rxc[k, j]
    whole = remote(rc, rc, us, ur, other)
    whole.wait_recv()
    acc = part[a]
    for i in range(31):
        acc = acc + rc[i]
    total[core, x, a] = acc

    @pl.loop(1, 16)
    def _(d):
        remote(total.at[core, x, a], total.at[core, x, a], ds, dr, ((a + d) % 16, b)).start()

    send_vert(2, outer)
    send_vert(0, has["up"] | has["down"])
    send_vert(3, has["up"] | has["down"])
    for k, (side, t) in enumerate((("right", 0), ("left", 3))):
        @pl.when(has[OPPOSITE[side]])
        def _(k=k, side=side, t=t):
            middle[side].wait_recv()
            newspec[:, :, 128 * t:128 * t + 128] += inv * rxm[k]
    some = remote(rc.at[pl.ds(0, 15)], rc.at[pl.ds(0, 15)], ds, dr, other)
    some.wait_recv()
    gather = [remote(total.at[core, x], total.at[core, x], es.at[d - 1], er.at[d - 1], mates[d - 1]) for d in (1, 2, 3)]
    for copy in gather:
        copy.start()
    add_vert(1)
    add_vert(2)
    for copy in gather:
        copy.wait_recv()
    last = remote(total.at[core], total.at[core], fs, fr, other)
    last.start()
    last.wait()
    for p in range(2):
        for s in range(4):
            rows, lanes = pl.ds((s % 2) * 128, 128), pl.ds((s // 2) * 128, 128)
            newill[p, rows, lanes] = ill[p, rows, lanes] + total[p, s].reshape(128, 128) * (1.0 / 64)
    add_vert(0)
    add_vert(3)
    first.wait_send()
    for copy in xsend + gather:
        copy.wait_send()
    whole.wait_send()
    some.wait_send()
    for side in ("right", "left"):
        for j in range(2):
            pl.when(has[side])(corner[side, j].wait_send)
        pl.when(has[side])(middle[side].wait_send)
    for way in ("up", "down"):
        for t in range(4):
            pl.when(has[way])(vert[way, t].wait_send)


def finish(spec, ill, grad, pterm):
    D = pltpu.SemaphoreType.DMA
    V = pl.BlockSpec(memory_space=pltpu.VMEM)
    return pl.pallas_call(
        finish_kernel,
        out_shape=(jax.ShapeDtypeStruct((2, 512, 512), F32), jax.ShapeDtypeStruct((2, 256, 256), F32)),
        in_specs=[V, V, V, V], out_specs=(V, V),
        scratch_shapes=[
            pltpu.VMEM((2, 2, 2, 128, 128), F32), pltpu.VMEM((2, 2, 512, 128), F32),
            pltpu.VMEM((2, 2, 4, 128, 128), F32), pltpu.VMEM((2, 2, 2, 128, 128), F32),
            pltpu.VMEM((4, 16, 8, 128), F32), pltpu.VMEM((3, 16, 8, 128), F32), pltpu.VMEM((4, 16, 8, 128), F32),
            pltpu.VMEM((16, 8, 128), F32), pltpu.VMEM((31, 8, 128), F32), pltpu.VMEM((2, 4, 16, 8, 128), F32),
            D, D, D((3,)), D((3,)), D((2, 2)), D((2, 2)), D((2,)), D((2,)), D((2, 4)), D((2, 4)),
            D, D, D, D, D((3,)), D((3,)), D, D,
        ],
        compiler_params=pltpu.CompilerParams(collective_id=2, has_side_effects=True, vmem_limit_bytes=32 * 2**20),
    )(spec, ill, grad, pterm)


def shards(specimen, illumination, scan_offsets, slot_counts, measured):
    anchor = jnp.stack([lax.axis_index("ty") * 512, lax.axis_index("tx") * 512]) - 128
    local = scan_offsets[0, 0] - anchor[:, None]
    count = slot_counts[0]
    mats = jnp.asarray(consts())
    ext, moduli, near, near_term = halo(local, count, specimen, measured[0, 0], illumination, mats)
    grad, probe_term = windows(local, count, ext, illumination, mats, moduli, near, near_term)
    return finish(specimen, illumination, grad, probe_term.reshape(2, 4, 16, 8, 128))


def solution(mesh):
    in_specs = (
        P(None, "ty", "tx"),
        P(),
        P("ty", "tx", None, None),
        P("ty", "tx"),
        P("ty", "tx", None, None, None),
    )
    out_specs = (P(None, "ty", "tx"), P())
    return jax.shard_map(shards, mesh=mesh, in_specs=in_specs, out_specs=out_specs, check_vma=False)
```

```python
import math
import numpy as np
import jax, jax.numpy as jnp
from jax import lax
from jax.experimental import pallas as pl
from jax.experimental.pallas import tpu as pltpu
from jax.sharding import PartitionSpec as P
import ml_dtypes

F32 = jnp.float32
BF = jnp.bfloat16
MESH = pl.DeviceIdType.MESH
NEAR = 10


def consts():
    n = np.arange(128)
    out = []
    for odd in (0, 1):
        angle = 2 * np.pi * (np.outer(n, 2 * n + odd) % 256) / 256
        real, imag = np.cos(angle) / 16, -np.sin(angle) / 16
        block = np.block([[real, imag], [-imag, real]])
        for m in (block, block.T):
            m = m.astype(np.float32)
            high = m.astype(ml_dtypes.bfloat16)
            low = (m - high.astype(np.float32)).astype(ml_dtypes.bfloat16)
            out.append(np.stack([high, low]))
    mats = np.stack(out).reshape(2, 2, 2, 256, 256)
    return mats


def split(x):
    high = x.astype(BF)
    return high, (x - high.astype(F32)).astype(BF)


def dot(a, b):
    return jnp.dot(a, b, preferred_element_type=F32)


def left(mats, high, low):
    x = dot(jnp.concatenate([mats[0], mats[1]], axis=0), high)
    return x[:256] + x[256:] + dot(mats[0], low)


def right(high, low, mats):
    x = dot(jnp.concatenate([high, low], axis=0), mats[0])
    return x[:256] + x[256:] + dot(high, mats[1])


BUFFERS = 14


def buffers():
    whole = pltpu.VMEM((2, 256, 256), F32)
    half = pltpu.VMEM((2, 256, 256), BF)
    return [whole, whole] + [half, half, whole] * 4


def stages(slot, row, col, live, source, ill, mats, moduli, pterm, place, bufs):
    patch, wave, h1, l1, m1, h2, l2, m2, h3, l3, m3, h4, l4, m4 = bufs
    tile = col // 128
    shift = col % 128
    back = (128 - shift) % 128
    lane = lax.broadcasted_iota(jnp.int32, (128, 128), 1)

    def cut():
        halves = []
        for h in range(2):
            rows = pl.ds(h * 128, 128)
            x = [[pltpu.roll(source[p, tile + t, pl.ds(row + h * 128, 128), :], back, 1) for t in range(3)]
                 for p in range(2)]
            picked = [[jnp.where(lane < 128 - shift, x[p][t], x[p][t + 1]) for t in range(2)] for p in range(2)]
            waves = []
            for t in range(2):
                lanes = pl.ds(128 * t, 128)
                pr, pi = ill[0, rows, lanes], ill[1, rows, lanes]
                a, b = picked[0][t], picked[1][t]
                patch[0, rows, lanes] = a
                patch[1, rows, lanes] = b
                wr, wi = pr * a - pi * b, pr * b + pi * a
                wave[0, rows, lanes] = wr
                wave[1, rows, lanes] = wi
                waves.append((wr, wi))
            halves.append(waves)
        for t in range(2):
            lanes = pl.ds(128 * t, 128)
            (ar, ai), (br, bi) = halves[0][t], halves[1][t]
            for q, pair in enumerate(((ar + br, ai + bi), (ar - br, ai - bi))):
                for z, value in enumerate(pair):
                    rows = pl.ds(z * 128, 128)
                    h1[q, rows, lanes], l1[q, rows, lanes] = split(value)

    def rows_forward():
        for q in range(2):
            m1[q] = left(mats.at[q, 1], h1[q], l1[q])

    def between_forward():
        for q in range(2):
            ar, br = m1[q, pl.ds(0, 128), pl.ds(0, 128)], m1[q, pl.ds(0, 128), pl.ds(128, 128)]
            ai, bi = m1[q, pl.ds(128, 128), pl.ds(0, 128)], m1[q, pl.ds(128, 128), pl.ds(128, 128)]
            rows = pl.ds(q * 128, 128)
            for e, pair in enumerate(((ar + br, ai + bi), (ar - br, ai - bi))):
                for z, value in enumerate(pair):
                    lanes = pl.ds(z * 128, 128)
                    h2[e, rows, lanes], l2[e, rows, lanes] = split(value)

    def columns_forward():
        for e in range(2):
            m2[e] = right(h2[e], l2[e], mats.at[e, 0])

    def project():
        for q in range(2):
            for e in range(2):
                rows = pl.ds(q * 128, 128)
                fr, fi = m2[e, rows, pl.ds(0, 128)], m2[e, rows, pl.ds(128, 128)]
                f = moduli[slot, rows, pl.ds(e * 128, 128)] * lax.rsqrt(jnp.maximum(fr * fr + fi * fi, 0.25))
                for z, value in enumerate((fr * f, fi * f)):
                    lanes = pl.ds(z * 128, 128)
                    h3[e, rows, lanes], l3[e, rows, lanes] = split(value)

    def columns_back():
        for e in range(2):
            m3[e] = right(h3[e], l3[e], mats.at[e, 1])

    def between_back():
        for q in range(2):
            rows = pl.ds(q * 128, 128)
            er, ei = m3[0, rows, pl.ds(0, 128)], m3[0, rows, pl.ds(128, 128)]
            vr, vi = m3[1, rows, pl.ds(0, 128)], m3[1, rows, pl.ds(128, 128)]
            for t, pair in enumerate(((er + vr, ei + vi), (er - vr, ei - vi))):
                for z, value in enumerate(pair):
                    at, lanes = pl.ds(z * 128, 128), pl.ds(t * 128, 128)
                    h4[q, at, lanes], l4[q, at, lanes] = split(value)

    def rows_back():
        for q in range(2):
            m4[q] = left(mats.at[q, 0], h4[q], l4[q])

    def update():
        out = [[[None] * 2 for _ in range(2)] for _ in range(2)]
        for t in range(2):
            lanes = pl.ds(128 * t, 128)
            er, ei = m4[0, pl.ds(0, 128), lanes], m4[0, pl.ds(128, 128), lanes]
            vr, vi = m4[1, pl.ds(0, 128), lanes], m4[1, pl.ds(128, 128), lanes]
            for h, (xr, xi) in enumerate(((er + vr, ei + vi), (er - vr, ei - vi))):
                rows = pl.ds(h * 128, 128)
                cr, ci = xr - wave[0, rows, lanes], xi - wave[1, rows, lanes]
                if live is not None:
                    cr, ci = cr * live, ci * live
                a, b = patch[0, rows, lanes], patch[1, rows, lanes]
                pterm[0, t, rows, :] += a * cr + b * ci
                pterm[1, t, rows, :] += a * ci - b * cr
                pr, pi = ill[0, rows, lanes], ill[1, rows, lanes]
                out[h][0][t] = pr * cr + pi * ci
                out[h][1][t] = pr * ci - pi * cr
        for h in range(2):
            for z in range(2):
                place(z, h, out[h][z])

    return (cut, rows_forward, between_forward, columns_forward, project,
            columns_back, between_back, rows_back, update)


def places(offs):
    return lambda s: offs[0, s], lambda s: offs[1, s]


def together(*windows):
    for steps in zip(*windows):
        for step in steps:
            step()


def deposit(grad, row, col, z, h, values):
    tile = col // 128
    shift = col % 128
    low = lax.broadcasted_iota(jnp.int32, (128, 128), 1) < shift
    first, second = (pltpu.roll(v, shift, 1) for v in values)
    rows = pl.ds(row + h * 128, 128)
    grad[z, tile, rows, :] += jnp.where(low, 0.0, first)
    grad[z, tile + 1, rows, :] += jnp.where(low, first, second)
    grad[z, tile + 2, rows, :] += jnp.where(low, second, 0.0)


def window_kernel(offs, count, ext, ill, mats, moduli, near, near_term, grad, pterm, todo, done, *bufs):
    n = count[0]
    row_of, col_of = places(offs)

    @pl.loop(0, 96)
    def _(i):
        rows = pl.ds(pl.multiple_of(8 * i, 8), 8)
        for p in range(2):
            for t in range(6):
                grad[p, t, rows, :] = jnp.zeros((8, 128), F32)

    pterm[...] = near_term[...]

    def sort(s, counts):
        left_over, taken = counts
        r = row_of(s)
        inside = jnp.logical_and(jnp.logical_and(r >= 128, r <= 384), s < n)
        inside = jnp.logical_and(inside, taken < NEAR)
        todo[left_over] = s
        done[taken] = s
        return (left_over + jnp.logical_and(s < n, jnp.logical_not(inside)).astype(jnp.int32),
                taken + inside.astype(jnp.int32))

    left_over, taken = lax.fori_loop(0, 16, sort, (jnp.int32(0), jnp.int32(0)))

    @pl.loop(0, taken)
    def _(i):
        s = done[i]
        for h in range(2):
            for z in range(2):
                deposit(grad, row_of(s), col_of(s), z, h, [near[i, z, t, pl.ds(h * 128, 128), :] for t in range(2)])

    @pl.loop(0, (left_over + 1) // 2)
    def _(k):
        windows = []
        for i in range(2):
            s = todo[jnp.minimum(2 * k + i, left_over - 1)]
            row, col = row_of(s), col_of(s)
            live = None if i == 0 else jnp.where(2 * k + i < left_over, 1.0, 0.0).astype(F32)

            def place(z, h, values, row=row, col=col):
                deposit(grad, row, col, z, h, values)

            windows.append(stages(s, row, col, live, ext, ill, mats, moduli, pterm, place,
                                  bufs[BUFFERS * i:BUFFERS * (i + 1)]))
        together(*windows)


def windows(offs, count, ext, ill, mats, moduli, near, near_term):
    V = pl.BlockSpec(memory_space=pltpu.VMEM)
    S = pl.BlockSpec(memory_space=pltpu.SMEM)
    return pl.pallas_call(
        window_kernel,
        out_shape=(jax.ShapeDtypeStruct((2, 6, 768, 128), F32), jax.ShapeDtypeStruct((2, 2, 256, 128), F32)),
        in_specs=[S, S, V, V, V, V, V, V], out_specs=(V, V),
        scratch_shapes=[pltpu.SMEM((16,), jnp.int32), pltpu.SMEM((16,), jnp.int32)] + buffers() * 2,
        compiler_params=pltpu.CompilerParams(vmem_limit_bytes=28 * 2**20),
    )(offs, count, ext, ill, mats, moduli, near, near_term)


def remote(src, dst, send_sem, recv_sem, device):
    return pltpu.make_async_remote_copy(
        src_ref=src, dst_ref=dst, send_sem=send_sem, recv_sem=recv_sem,
        device_id=device, device_id_type=MESH,
    )


def greet(devices):
    barrier = pltpu.get_barrier_semaphore()
    expected = 0
    for condition, device in devices:
        if condition is None:
            pl.semaphore_signal(barrier, inc=1, device_id=device, device_id_type=MESH)
            expected = expected + 1
        else:
            @pl.when(condition)
            def _(device=device):
                pl.semaphore_signal(barrier, inc=1, device_id=device, device_id_type=MESH)
            expected = expected + condition.astype(jnp.int32)
    return barrier, expected


def neighbours():
    a = lax.axis_index("ty")
    b = lax.axis_index("tx")
    has = {"up": a > 0, "down": a < 15, "left": b > 0, "right": b < 15}
    ids = {"up": (jnp.maximum(a - 1, 0), b), "down": (jnp.minimum(a + 1, 15), b),
           "left": (a, jnp.maximum(b - 1, 0)), "right": (a, jnp.minimum(b + 1, 15))}
    return a, b, has, ids


OPPOSITE = {"up": "down", "down": "up", "left": "right", "right": "left"}


def halo_kernel(offs, count, tile, meas, ill, mats, ext, moduli, near, near_term,
                mid, mbuf, meas_sem, own_sem, mid_sem, row_send, row_recv, col_send, col_recv, cor_send, cor_recv, *bufs):
    a, b, has, ids = neighbours()
    barrier, expected = greet([(has[k], ids[k]) for k in ids])
    own = [pltpu.make_async_copy(tile.at[:, :, pl.ds(128 * t, 128)], mid.at[:, 1 + t], own_sem.at[t]) for t in range(4)]
    for copy in own:
        copy.start()

    def fetch(s, t):
        return pltpu.make_async_copy(meas.at[s, :, pl.ds(128 * t, 128)], mbuf.at[s, t], meas_sem.at[s, t])

    @pl.loop(0, 16)
    def _(s):
        for t in range(2):
            fetch(s, t).start()

    pl.semaphore_wait(barrier, expected)
    rows, cols, corners = {}, {}, {}
    for i, way in enumerate(("down", "up")):
        src_row, dst_row = (384, 0) if way == "down" else (0, 640)
        for t in (0, 3, 1, 2):
            rows[way, t] = remote(
                tile.at[:, pl.ds(src_row, 128), pl.ds(128 * t, 128)],
                ext.at[:, 1 + t, pl.ds(dst_row, 128), :],
                row_send.at[i, t], row_recv.at[i, t], ids[way])
    for i, way in enumerate(("right", "left")):
        src_t, dst_t = (3, 0) if way == "right" else (0, 5)
        cols[way] = remote(
            tile.at[:, :, pl.ds(128 * src_t, 128)], mid.at[:, dst_t],
            col_send.at[i], col_recv.at[i], ids[way])
        for j, row in enumerate((0, 640)):
            corners[way, j] = remote(
                ext.at[:, 1 + src_t, pl.ds(row, 128), :], ext.at[:, dst_t, pl.ds(row, 128), :],
                cor_send.at[i, j], cor_recv.at[i, j], ids[way])
    outer = jnp.logical_or((b // 2) % 4 == 0, (b // 2) % 4 == 3)

    inner = jnp.logical_not(outer)

    def start_rows(mine, tiles):
        for t in tiles:
            for way in ("down", "up"):
                pl.when(jnp.logical_and(has[way], mine))(rows[way, t].start)

    for way in ("right", "left"):
        pl.when(has[way])(cols[way].start)
    start_rows(inner, (0, 3))
    near_term[...] = jnp.zeros_like(near_term)
    crossing = {"right": b == 7, "left": b == 8}

    def settle(late):
        for side in ("right", "left"):
            sends, lands = crossing[side], crossing[OPPOSITE[side]]
            if not late:
                sends, lands = jnp.logical_not(sends), jnp.logical_not(lands)
            pl.when(jnp.logical_and(has[side], sends))(cols[side].wait_send)
            pl.when(jnp.logical_and(has[OPPOSITE[side]], lands))(cols[side].wait_recv)

    settle(False)
    start_rows(outer, (0, 3))
    to = lax.broadcasted_iota(jnp.int32, (256, 256), 1)
    source = 2 * (to % 128) + to // 128
    perm = jnp.where(lax.broadcasted_iota(jnp.int32, (256, 256), 0) == source, 1.0, 0.0).astype(BF)

    @pl.loop(0, 16)
    def _(s):
        for t in range(2):
            fetch(s, t).wait()
        for q in range(2):
            picked = jnp.concatenate([mbuf[s, t, pl.ds(q, 128, stride=2), :] for t in range(2)], axis=1)
            high, low = split(picked)
            moduli[s, pl.ds(128 * q, 128), :] = dot(high, perm) + dot(low, perm)

    settle(True)
    for copy in own:
        copy.wait()
    centre = pltpu.make_async_copy(mid, ext.at[:, :, pl.ds(128, 512), :], mid_sem)
    centre.start()
    n = count[0]
    row_of, col_of = places(offs)
    inside, rank, total = [], [], jnp.int32(0)
    for s in range(16):
        r = row_of(s)
        ok = jnp.logical_and(jnp.logical_and(r >= 128, r <= 384), s < n).astype(jnp.int32)
        inside.append(ok)
        rank.append(total)
        total = total + ok

    @pl.loop(0, NEAR // 2)
    def _(k):
        def sent_edges(mine):
            for way in ("down", "up"):
                for t in (0, 3):
                    pl.when(jnp.logical_and(has[way], mine))(rows[way, t].wait_send)

        @pl.when(k == 1)
        def _():
            sent_edges(inner)
            start_rows(inner, (1, 2))

        @pl.when(k == 2)
        def _():
            sent_edges(outer)
            for j, way in enumerate(("down", "up")):
                @pl.when(has[OPPOSITE[way]])
                def _(way=way):
                    rows[way, 0].wait_recv()
                    rows[way, 3].wait_recv()
                for side in ("right", "left"):
                    pl.when(jnp.logical_and(has[side], has[OPPOSITE[way]]))(corners[side, j].start)

        @pl.when(k == 3)
        def _():
            start_rows(outer, (1, 2))

        taken = []
        for i in range(2):
            at = 2 * k + i
            slot = jnp.int32(0)
            for s in range(1, 16):
                slot = slot + s * inside[s] * (rank[s] == at).astype(jnp.int32)
            row = jnp.clip(row_of(slot) - 128, 0, 256)
            live = (at < total).astype(F32)

            def place(z, h, values, at=at):
                for t in range(2):
                    near[at, z, t, pl.ds(h * 128, 128), :] = values[t]

            taken.append(stages(slot, row, col_of(slot), live, mid, ill, mats, moduli, near_term, place,
                                bufs[BUFFERS * i:BUFFERS * (i + 1)]))
        together(*taken)

    for way in ("down", "up"):
        for t in (1, 2):
            pl.when(has[OPPOSITE[way]])(rows[way, t].wait_recv)
            pl.when(has[way])(rows[way, t].wait_send)
    for side in ("right", "left"):
        for j, way in enumerate(("down", "up")):
            pl.when(jnp.logical_and(has[OPPOSITE[side]], has[OPPOSITE[way]]))(corners[side, j].wait_recv)
            pl.when(jnp.logical_and(has[side], has[OPPOSITE[way]]))(corners[side, j].wait_send)
    centre.wait()


def halo(offs, count, tile, meas, ill, mats):
    D = pltpu.SemaphoreType.DMA
    A = pl.BlockSpec(memory_space=pl.ANY)
    V = pl.BlockSpec(memory_space=pltpu.VMEM)
    S = pl.BlockSpec(memory_space=pltpu.SMEM)
    return pl.pallas_call(
        halo_kernel,
        out_shape=(jax.ShapeDtypeStruct((2, 6, 768, 128), F32), jax.ShapeDtypeStruct((16, 256, 256), F32),
                   jax.ShapeDtypeStruct((NEAR, 2, 2, 256, 128), F32), jax.ShapeDtypeStruct((2, 2, 256, 128), F32)),
        in_specs=[S, S, A, A, V, V], out_specs=(V, V, V, V),
        scratch_shapes=[pltpu.VMEM((2, 6, 512, 128), F32), pltpu.VMEM((16, 2, 256, 128), F32), D((16, 2)),
                        D((4,)), D, D((2, 4)), D((2, 4)), D((2,)), D((2,)), D((2, 2)), D((2, 2))] + buffers() * 2,
        cost_estimate=pl.CostEstimate(flops=2 * 10**10, bytes_accessed=2 * 10**7, transcendentals=0),
        compiler_params=pltpu.CompilerParams(collective_id=1, has_side_effects=True, vmem_limit_bytes=26 * 2**20),
    )(offs, count, tile, meas, ill, mats)


def partners(b):
    core = b % 2
    x = (b // 2) % 4
    zlo = b // 8
    return core, x, zlo


def finish_kernel(spec, ill, grad, pterm, newspec, newill,
                  rxc, rxm, rz, edge, rcore, rx, sumc, part, rc, total,
                  core_s, core_r, xs, xr, cs, cr, ms, mr, zs, zr,
                  us, ur, ds, dr, es, er, fs, fr):
    a, b, has, ids = neighbours()
    core, x, zlo = partners(b)
    low = x * 2 + core
    unit = zlo * 16 + a

    def member(d):
        u = (unit + d) % 32
        return (u % 16, (u // 16) * 8 + low)

    mates = [(a, zlo * 8 + ((x + d) % 4) * 2 + core) for d in (1, 2, 3)]
    other = (a, zlo * 8 + x * 2 + (1 - core))
    barrier, expected = greet([(None, m) for m in mates] + [(None, other)]
                              + [(jnp.logical_and(core == 0, has["left"]), ids["left"]),
                                 (jnp.logical_and(core == 1, has["right"]), ids["right"])])

    @pl.loop(1, 32)
    def _(d):
        pl.semaphore_signal(barrier, inc=1, device_id=member(d), device_id_type=MESH)

    power = jnp.sum(ill[0] * ill[0] + ill[1] * ill[1]) * (1.0 / 65536) + 1e-05
    inv = 1.0 / power
    pl.semaphore_wait(barrier, expected + 31)
    first = remote(pterm.at[1 - core], rcore, core_s, core_r, other)
    corner, middle, vert = {}, {}, {}
    for i, side in enumerate(("right", "left")):
        src_t = 5 if side == "right" else 0
        for j, row in enumerate((0, 640)):
            corner[side, j] = remote(grad.at[:, src_t, pl.ds(row, 128), :], rxc.at[i, j],
                                     cs.at[i, j], cr.at[i, j], ids[side])
        middle[side] = remote(grad.at[:, src_t, pl.ds(128, 512), :], rxm.at[i], ms.at[i], mr.at[i], ids[side])
    for j, way in enumerate(("up", "down")):
        row = 0 if way == "up" else 640
        for t in range(4):
            src = edge.at[j, t // 3] if t in (0, 3) else grad.at[:, 1 + t, pl.ds(row, 128), :]
            vert[way, t] = remote(src, rz.at[j, :, t], zs.at[j, t], zr.at[j, t], ids[way])

    outer = jnp.logical_or(x == 0, x == 3)
    inner = jnp.logical_not(outer)
    crossing = {"right": b == 7, "left": b == 8}

    def send_vert(t, mine):
        for way in ("up", "down"):
            pl.when(jnp.logical_and(has[way], mine))(vert[way, t].start)

    def add_vert(t):
        for j, (way, row) in enumerate((("up", 384), ("down", 0))):
            @pl.when(has[OPPOSITE[way]])
            def _(j=j, way=way, row=row):
                vert[way, t].wait_recv()
                newspec[:, row:row + 128, 128 * t:128 * t + 128] += inv * rz[j, :, t]

    first.start()
    for side in ("right", "left"):
        pl.when(crossing[side])(middle[side].start)
    send_vert(1, inner)
    first.wait_recv()
    sumc[...] = pterm[core] + rcore[...]
    xsend = [remote(sumc.at[(x + d) % 4], rx.at[d - 1], xs.at[d - 1], xr.at[d - 1], mates[d - 1]) for d in (1, 2, 3)]
    for copy in xsend:
        copy.start()
    for side in ("right", "left"):
        for j in range(2):
            pl.when(has[side])(corner[side, j].start)
    for copy in xsend:
        copy.wait_recv()
    part[...] = sumc[x] + rx[0] + rx[1] + rx[2]

    @pl.loop(1, 32)
    def _(d):
        device = member(d)
        remote(part.at[device[0]], rc.at[d - 1], us, ur, device).start()

    send_vert(1, outer)
    send_vert(2, inner)
    for side in ("right", "left"):
        pl.when(jnp.logical_and(has[side], jnp.logical_not(crossing[side])))(middle[side].start)

    @pl.loop(0, 16)
    def _(i):
        rows = pl.ds(pl.multiple_of(32 * i, 32), 32)
        more = pl.ds(pl.multiple_of(32 * i + 128, 32), 32)
        for p in range(2):
            for t in range(4):
                lanes = pl.ds(128 * t, 128)
                newspec[p, rows, lanes] = spec[p, rows, lanes] + inv * grad[p, 1 + t, more, :]

    for j, row in enumerate((0, 640)):
        for k, (t, side) in enumerate(((1, "right"), (4, "left"))):
            edge[j, k] = grad[:, t, row:row + 128, :]
            @pl.when(has[OPPOSITE[side]])
            def _(j=j, k=k, side=side):
                corner[side, j].wait_recv()
                edge[j, k] += rxc[k, j]
    whole = remote(rc, rc, us, ur, other)
    whole.wait_recv()
    acc = part[a]
    for i in range(31):
        acc = acc + rc[i]
    total[core, x, a] = acc

    @pl.loop(1, 16)
    def _(d):
        remote(total.at[core, x, a], total.at[core, x, a], ds, dr, ((a + d) % 16, b)).start()

    send_vert(2, outer)
    send_vert(0, has["up"] | has["down"])
    send_vert(3, has["up"] | has["down"])
    for k, (side, t) in enumerate((("right", 0), ("left", 3))):
        @pl.when(has[OPPOSITE[side]])
        def _(k=k, side=side, t=t):
            middle[side].wait_recv()
            newspec[:, :, 128 * t:128 * t + 128] += inv * rxm[k]
    some = remote(rc.at[pl.ds(0, 15)], rc.at[pl.ds(0, 15)], ds, dr, other)
    some.wait_recv()
    gather = [remote(total.at[core, x], total.at[core, x], es.at[d - 1], er.at[d - 1], mates[d - 1]) for d in (1, 2, 3)]
    for copy in gather:
        copy.start()
    add_vert(1)
    add_vert(2)
    for copy in gather:
        copy.wait_recv()
    last = remote(total.at[core], total.at[core], fs, fr, other)
    last.start()
    last.wait()
    for p in range(2):
        for s in range(4):
            rows, lanes = pl.ds((s % 2) * 128, 128), pl.ds((s // 2) * 128, 128)
            newill[p, rows, lanes] = ill[p, rows, lanes] + total[p, s].reshape(128, 128) * (1.0 / 64)
    add_vert(0)
    add_vert(3)
    first.wait_send()
    for copy in xsend + gather:
        copy.wait_send()
    whole.wait_send()
    some.wait_send()
    for side in ("right", "left"):
        for j in range(2):
            pl.when(has[side])(corner[side, j].wait_send)
        pl.when(has[side])(middle[side].wait_send)
    for way in ("up", "down"):
        for t in range(4):
            pl.when(has[way])(vert[way, t].wait_send)


def finish(spec, ill, grad, pterm):
    D = pltpu.SemaphoreType.DMA
    V = pl.BlockSpec(memory_space=pltpu.VMEM)
    return pl.pallas_call(
        finish_kernel,
        out_shape=(jax.ShapeDtypeStruct((2, 512, 512), F32), jax.ShapeDtypeStruct((2, 256, 256), F32)),
        in_specs=[V, V, V, V], out_specs=(V, V),
        scratch_shapes=[
            pltpu.VMEM((2, 2, 2, 128, 128), F32), pltpu.VMEM((2, 2, 512, 128), F32),
            pltpu.VMEM((2, 2, 4, 128, 128), F32), pltpu.VMEM((2, 2, 2, 128, 128), F32),
            pltpu.VMEM((4, 16, 8, 128), F32), pltpu.VMEM((3, 16, 8, 128), F32), pltpu.VMEM((4, 16, 8, 128), F32),
            pltpu.VMEM((16, 8, 128), F32), pltpu.VMEM((31, 8, 128), F32), pltpu.VMEM((2, 4, 16, 8, 128), F32),
            D, D, D((3,)), D((3,)), D((2, 2)), D((2, 2)), D((2,)), D((2,)), D((2, 4)), D((2, 4)),
            D, D, D, D, D((3,)), D((3,)), D, D,
        ],
        compiler_params=pltpu.CompilerParams(collective_id=2, has_side_effects=True, vmem_limit_bytes=32 * 2**20),
    )(spec, ill, grad, pterm)


def shards(specimen, illumination, scan_offsets, slot_counts, measured):
    anchor = jnp.stack([lax.axis_index("ty") * 512, lax.axis_index("tx") * 512]) - 128
    local = scan_offsets[0, 0] - anchor[:, None]
    count = slot_counts[0]
    mats = jnp.asarray(consts())
    ext, moduli, near, near_term = halo(local, count, specimen, measured[0, 0], illumination, mats)
    grad, probe_term = windows(local, count, ext, illumination, mats, moduli, near, near_term)
    return finish(specimen, illumination, grad, probe_term.reshape(2, 4, 16, 8, 128))


def solution(mesh):
    in_specs = (
        P(None, "ty", "tx"),
        P(),
        P("ty", "tx", None, None),
        P("ty", "tx"),
        P("ty", "tx", None, None, None),
    )
    out_specs = (P(None, "ty", "tx"), P())
    return jax.shard_map(shards, mesh=mesh, in_specs=in_specs, out_specs=out_specs, check_vma=False)
```

```python
import math
import numpy as np
import jax, jax.numpy as jnp
from jax import lax
from jax.experimental import pallas as pl
from jax.experimental.pallas import tpu as pltpu
from jax.sharding import PartitionSpec as P
import ml_dtypes

F32 = jnp.float32
BF = jnp.bfloat16
MESH = pl.DeviceIdType.MESH
NEAR = 8


def consts():
    n = np.arange(128)
    out = []
    for odd in (0, 1):
        angle = 2 * np.pi * (np.outer(n, 2 * n + odd) % 256) / 256
        real, imag = np.cos(angle) / 16, -np.sin(angle) / 16
        block = np.block([[real, imag], [-imag, real]])
        for m in (block, block.T):
            m = m.astype(np.float32)
            high = m.astype(ml_dtypes.bfloat16)
            low = (m - high.astype(np.float32)).astype(ml_dtypes.bfloat16)
            out.append(np.stack([high, low]))
    mats = np.stack(out).reshape(2, 2, 2, 256, 256)
    return mats


def split(x):
    high = x.astype(BF)
    return high, (x - high.astype(F32)).astype(BF)


def dot(a, b):
    return jnp.dot(a, b, preferred_element_type=F32)


def left(mats, high, low):
    x = dot(jnp.concatenate([mats[0], mats[1]], axis=0), high)
    return x[:256] + x[256:] + dot(mats[0], low)


def right(high, low, mats):
    x = dot(jnp.concatenate([high, low], axis=0), mats[0])
    return x[:256] + x[256:] + dot(high, mats[1])


BUFFERS = 14


def buffers():
    whole = pltpu.VMEM((2, 256, 256), F32)
    half = pltpu.VMEM((2, 256, 256), BF)
    return [whole, whole] + [half, half, whole] * 4


def stages(slot, row, col, live, source, ill, mats, moduli, pterm, place, bufs):
    patch, wave, h1, l1, m1, h2, l2, m2, h3, l3, m3, h4, l4, m4 = bufs
    tile = col // 128
    shift = col % 128
    back = (128 - shift) % 128
    lane = lax.broadcasted_iota(jnp.int32, (128, 128), 1)

    def cut():
        halves = []
        for h in range(2):
            rows = pl.ds(h * 128, 128)
            x = [[pltpu.roll(source[p, tile + t, pl.ds(row + h * 128, 128), :], back, 1) for t in range(3)]
                 for p in range(2)]
            picked = [[jnp.where(lane < 128 - shift, x[p][t], x[p][t + 1]) for t in range(2)] for p in range(2)]
            waves = []
            for t in range(2):
                lanes = pl.ds(128 * t, 128)
                pr, pi = ill[0, rows, lanes], ill[1, rows, lanes]
                a, b = picked[0][t], picked[1][t]
                patch[0, rows, lanes] = a
                patch[1, rows, lanes] = b
                wr, wi = pr * a - pi * b, pr * b + pi * a
                wave[0, rows, lanes] = wr
                wave[1, rows, lanes] = wi
                waves.append((wr, wi))
            halves.append(waves)
        for t in range(2):
            lanes = pl.ds(128 * t, 128)
            (ar, ai), (br, bi) = halves[0][t], halves[1][t]
            for q, pair in enumerate(((ar + br, ai + bi), (ar - br, ai - bi))):
                for z, value in enumerate(pair):
                    rows = pl.ds(z * 128, 128)
                    h1[q, rows, lanes], l1[q, rows, lanes] = split(value)

    def rows_forward():
        for q in range(2):
            m1[q] = left(mats.at[q, 1], h1[q], l1[q])

    def between_forward():
        for q in range(2):
            ar, br = m1[q, pl.ds(0, 128), pl.ds(0, 128)], m1[q, pl.ds(0, 128), pl.ds(128, 128)]
            ai, bi = m1[q, pl.ds(128, 128), pl.ds(0, 128)], m1[q, pl.ds(128, 128), pl.ds(128, 128)]
            rows = pl.ds(q * 128, 128)
            for e, pair in enumerate(((ar + br, ai + bi), (ar - br, ai - bi))):
                for z, value in enumerate(pair):
                    lanes = pl.ds(z * 128, 128)
                    h2[e, rows, lanes], l2[e, rows, lanes] = split(value)

    def columns_forward():
        for e in range(2):
            m2[e] = right(h2[e], l2[e], mats.at[e, 0])

    def project():
        for q in range(2):
            for e in range(2):
                rows = pl.ds(q * 128, 128)
                fr, fi = m2[e, rows, pl.ds(0, 128)], m2[e, rows, pl.ds(128, 128)]
                f = moduli[slot, rows, pl.ds(e * 128, 128)] * lax.rsqrt(jnp.maximum(fr * fr + fi * fi, 0.25))
                for z, value in enumerate((fr * f, fi * f)):
                    lanes = pl.ds(z * 128, 128)
                    h3[e, rows, lanes], l3[e, rows, lanes] = split(value)

    def columns_back():
        for e in range(2):
            m3[e] = right(h3[e], l3[e], mats.at[e, 1])

    def between_back():
        for q in range(2):
            rows = pl.ds(q * 128, 128)
            er, ei = m3[0, rows, pl.ds(0, 128)], m3[0, rows, pl.ds(128, 128)]
            vr, vi = m3[1, rows, pl.ds(0, 128)], m3[1, rows, pl.ds(128, 128)]
            for t, pair in enumerate(((er + vr, ei + vi), (er - vr, ei - vi))):
                for z, value in enumerate(pair):
                    at, lanes = pl.ds(z * 128, 128), pl.ds(t * 128, 128)
                    h4[q, at, lanes], l4[q, at, lanes] = split(value)

    def rows_back():
        for q in range(2):
            m4[q] = left(mats.at[q, 0], h4[q], l4[q])

    def update():
        out = [[[None] * 2 for _ in range(2)] for _ in range(2)]
        for t in range(2):
            lanes = pl.ds(128 * t, 128)
            er, ei = m4[0, pl.ds(0, 128), lanes], m4[0, pl.ds(128, 128), lanes]
            vr, vi = m4[1, pl.ds(0, 128), lanes], m4[1, pl.ds(128, 128), lanes]
            for h, (xr, xi) in enumerate(((er + vr, ei + vi), (er - vr, ei - vi))):
                rows = pl.ds(h * 128, 128)
                cr, ci = xr - wave[0, rows, lanes], xi - wave[1, rows, lanes]
                if live is not None:
                    cr, ci = cr * live, ci * live
                a, b = patch[0, rows, lanes], patch[1, rows, lanes]
                pterm[0, t, rows, :] += a * cr + b * ci
                pterm[1, t, rows, :] += a * ci - b * cr
                pr, pi = ill[0, rows, lanes], ill[1, rows, lanes]
                out[h][0][t] = pr * cr + pi * ci
                out[h][1][t] = pr * ci - pi * cr
        for h in range(2):
            for z in range(2):
                place(z, h, out[h][z])

    return (cut, rows_forward, between_forward, columns_forward, project,
            columns_back, between_back, rows_back, update)


def places(offs):
    return lambda s: offs[0, s], lambda s: offs[1, s]


def together(*windows):
    for steps in zip(*windows):
        for step in steps:
            step()


def deposit(grad, row, col, z, h, values):
    tile = col // 128
    shift = col % 128
    low = lax.broadcasted_iota(jnp.int32, (128, 128), 1) < shift
    first, second = (pltpu.roll(v, shift, 1) for v in values)
    rows = pl.ds(row + h * 128, 128)
    grad[z, tile, rows, :] += jnp.where(low, 0.0, first)
    grad[z, tile + 1, rows, :] += jnp.where(low, first, second)
    grad[z, tile + 2, rows, :] += jnp.where(low, second, 0.0)


def window_kernel(offs, count, ext, ill, mats, moduli, near, near_term, grad, pterm, todo, done, *bufs):
    n = count[0]
    row_of, col_of = places(offs)

    @pl.loop(0, 96)
    def _(i):
        rows = pl.ds(pl.multiple_of(8 * i, 8), 8)
        for p in range(2):
            for t in range(6):
                grad[p, t, rows, :] = jnp.zeros((8, 128), F32)

    pterm[...] = near_term[...]

    def sort(s, counts):
        left_over, taken = counts
        r = row_of(s)
        inside = jnp.logical_and(jnp.logical_and(r >= 128, r <= 384), s < n)
        inside = jnp.logical_and(inside, taken < NEAR)
        todo[left_over] = s
        done[taken] = s
        return (left_over + jnp.logical_and(s < n, jnp.logical_not(inside)).astype(jnp.int32),
                taken + inside.astype(jnp.int32))

    left_over, taken = lax.fori_loop(0, 16, sort, (jnp.int32(0), jnp.int32(0)))

    @pl.loop(0, taken)
    def _(i):
        s = done[i]
        for h in range(2):
            for z in range(2):
                deposit(grad, row_of(s), col_of(s), z, h, [near[i, z, t, pl.ds(h * 128, 128), :] for t in range(2)])

    @pl.loop(0, (left_over + 1) // 2)
    def _(k):
        windows = []
        for i in range(2):
            s = todo[jnp.minimum(2 * k + i, left_over - 1)]
            row, col = row_of(s), col_of(s)
            live = None if i == 0 else jnp.where(2 * k + i < left_over, 1.0, 0.0).astype(F32)

            def place(z, h, values, row=row, col=col):
                deposit(grad, row, col, z, h, values)

            windows.append(stages(s, row, col, live, ext, ill, mats, moduli, pterm, place,
                                  bufs[BUFFERS * i:BUFFERS * (i + 1)]))
        together(*windows)


def windows(offs, count, ext, ill, mats, moduli, near, near_term):
    V = pl.BlockSpec(memory_space=pltpu.VMEM)
    S = pl.BlockSpec(memory_space=pltpu.SMEM)
    return pl.pallas_call(
        window_kernel,
        out_shape=(jax.ShapeDtypeStruct((2, 6, 768, 128), F32), jax.ShapeDtypeStruct((2, 2, 256, 128), F32)),
        in_specs=[S, S, V, V, V, V, V, V], out_specs=(V, V),
        scratch_shapes=[pltpu.SMEM((16,), jnp.int32), pltpu.SMEM((16,), jnp.int32)] + buffers() * 2,
        compiler_params=pltpu.CompilerParams(vmem_limit_bytes=28 * 2**20),
    )(offs, count, ext, ill, mats, moduli, near, near_term)


def remote(src, dst, send_sem, recv_sem, device):
    return pltpu.make_async_remote_copy(
        src_ref=src, dst_ref=dst, send_sem=send_sem, recv_sem=recv_sem,
        device_id=device, device_id_type=MESH,
    )


def greet(devices):
    barrier = pltpu.get_barrier_semaphore()
    expected = 0
    for condition, device in devices:
        if condition is None:
            pl.semaphore_signal(barrier, inc=1, device_id=device, device_id_type=MESH)
            expected = expected + 1
        else:
            @pl.when(condition)
            def _(device=device):
                pl.semaphore_signal(barrier, inc=1, device_id=device, device_id_type=MESH)
            expected = expected + condition.astype(jnp.int32)
    return barrier, expected


def neighbours():
    a = lax.axis_index("ty")
    b = lax.axis_index("tx")
    has = {"up": a > 0, "down": a < 15, "left": b > 0, "right": b < 15}
    ids = {"up": (jnp.maximum(a - 1, 0), b), "down": (jnp.minimum(a + 1, 15), b),
           "left": (a, jnp.maximum(b - 1, 0)), "right": (a, jnp.minimum(b + 1, 15))}
    return a, b, has, ids


OPPOSITE = {"up": "down", "down": "up", "left": "right", "right": "left"}


def halo_kernel(offs, count, tile, meas, ill, mats, ext, moduli, near, near_term,
                mid, mbuf, meas_sem, own_sem, mid_sem, row_send, row_recv, col_send, col_recv, cor_send, cor_recv, *bufs):
    a, b, has, ids = neighbours()
    barrier, expected = greet([(has[k], ids[k]) for k in ids])
    own = [pltpu.make_async_copy(tile.at[:, :, pl.ds(128 * t, 128)], mid.at[:, 1 + t], own_sem.at[t]) for t in range(4)]
    for copy in own:
        copy.start()

    def fetch(s, t):
        return pltpu.make_async_copy(meas.at[s, :, pl.ds(128 * t, 128)], mbuf.at[s, t], meas_sem.at[s, t])

    @pl.loop(0, 16)
    def _(s):
        for t in range(2):
            fetch(s, t).start()

    pl.semaphore_wait(barrier, expected)
    rows, cols, corners = {}, {}, {}
    for i, way in enumerate(("down", "up")):
        src_row, dst_row = (384, 0) if way == "down" else (0, 640)
        for t in (0, 3, 1, 2):
            rows[way, t] = remote(
                tile.at[:, pl.ds(src_row, 128), pl.ds(128 * t, 128)],
                ext.at[:, 1 + t, pl.ds(dst_row, 128), :],
                row_send.at[i, t], row_recv.at[i, t], ids[way])
    for i, way in enumerate(("right", "left")):
        src_t, dst_t = (3, 0) if way == "right" else (0, 5)
        cols[way] = remote(
            tile.at[:, :, pl.ds(128 * src_t, 128)], mid.at[:, dst_t],
            col_send.at[i], col_recv.at[i], ids[way])
        for j, row in enumerate((0, 640)):
            corners[way, j] = remote(
                ext.at[:, 1 + src_t, pl.ds(row, 128), :], ext.at[:, dst_t, pl.ds(row, 128), :],
                cor_send.at[i, j], cor_recv.at[i, j], ids[way])
    outer = jnp.logical_or((b // 2) % 4 == 0, (b // 2) % 4 == 3)

    inner = jnp.logical_not(outer)

    def start_rows(mine, tiles):
        for t in tiles:
            for way in ("down", "up"):
                pl.when(jnp.logical_and(has[way], mine))(rows[way, t].start)

    for way in ("right", "left"):
        pl.when(has[way])(cols[way].start)
    start_rows(inner, (0, 3))
    near_term[...] = jnp.zeros_like(near_term)
    crossing = {"right": b == 7, "left": b == 8}

    def settle(late):
        for side in ("right", "left"):
            sends, lands = crossing[side], crossing[OPPOSITE[side]]
            if not late:
                sends, lands = jnp.logical_not(sends), jnp.logical_not(lands)
            pl.when(jnp.logical_and(has[side], sends))(cols[side].wait_send)
            pl.when(jnp.logical_and(has[OPPOSITE[side]], lands))(cols[side].wait_recv)

    settle(False)
    start_rows(outer, (0, 3))
    to = lax.broadcasted_iota(jnp.int32, (256, 256), 1)
    source = 2 * (to % 128) + to // 128
    perm = jnp.where(lax.broadcasted_iota(jnp.int32, (256, 256), 0) == source, 1.0, 0.0).astype(BF)

    @pl.loop(0, 16)
    def _(s):
        for t in range(2):
            fetch(s, t).wait()
        for q in range(2):
            picked = jnp.concatenate([mbuf[s, t, pl.ds(q, 128, stride=2), :] for t in range(2)], axis=1)
            high, low = split(picked)
            moduli[s, pl.ds(128 * q, 128), :] = dot(high, perm) + dot(low, perm)

    settle(True)
    for copy in own:
        copy.wait()
    centre = pltpu.make_async_copy(mid, ext.at[:, :, pl.ds(128, 512), :], mid_sem)
    centre.start()
    n = count[0]
    row_of, col_of = places(offs)
    inside, rank, total = [], [], jnp.int32(0)
    for s in range(16):
        r = row_of(s)
        ok = jnp.logical_and(jnp.logical_and(r >= 128, r <= 384), s < n).astype(jnp.int32)
        inside.append(ok)
        rank.append(total)
        total = total + ok

    @pl.loop(0, NEAR // 2)
    def _(k):
        def sent_edges(mine):
            for way in ("down", "up"):
                for t in (0, 3):
                    pl.when(jnp.logical_and(has[way], mine))(rows[way, t].wait_send)

        @pl.when(k == 1)
        def _():
            sent_edges(inner)
            start_rows(inner, (1, 2))

        @pl.when(k == 2)
        def _():
            sent_edges(outer)
            for j, way in enumerate(("down", "up")):
                @pl.when(has[OPPOSITE[way]])
                def _(way=way):
                    rows[way, 0].wait_recv()
                    rows[way, 3].wait_recv()
                for side in ("right", "left"):
                    pl.when(jnp.logical_and(has[side], has[OPPOSITE[way]]))(corners[side, j].start)

        @pl.when(k == 3)
        def _():
            start_rows(outer, (1, 2))

        taken = []
        for i in range(2):
            at = 2 * k + i
            slot = jnp.int32(0)
            for s in range(1, 16):
                slot = slot + s * inside[s] * (rank[s] == at).astype(jnp.int32)
            row = jnp.clip(row_of(slot) - 128, 0, 256)
            live = (at < total).astype(F32)

            def place(z, h, values, at=at):
                for t in range(2):
                    near[at, z, t, pl.ds(h * 128, 128), :] = values[t]

            taken.append(stages(slot, row, col_of(slot), live, mid, ill, mats, moduli, near_term, place,
                                bufs[BUFFERS * i:BUFFERS * (i + 1)]))
        together(*taken)

    for way in ("down", "up"):
        for t in (1, 2):
            pl.when(has[OPPOSITE[way]])(rows[way, t].wait_recv)
            pl.when(has[way])(rows[way, t].wait_send)
    for side in ("right", "left"):
        for j, way in enumerate(("down", "up")):
            pl.when(jnp.logical_and(has[OPPOSITE[side]], has[OPPOSITE[way]]))(corners[side, j].wait_recv)
            pl.when(jnp.logical_and(has[side], has[OPPOSITE[way]]))(corners[side, j].wait_send)
    centre.wait()


def halo(offs, count, tile, meas, ill, mats):
    D = pltpu.SemaphoreType.DMA
    A = pl.BlockSpec(memory_space=pl.ANY)
    V = pl.BlockSpec(memory_space=pltpu.VMEM)
    S = pl.BlockSpec(memory_space=pltpu.SMEM)
    return pl.pallas_call(
        halo_kernel,
        out_shape=(jax.ShapeDtypeStruct((2, 6, 768, 128), F32), jax.ShapeDtypeStruct((16, 256, 256), F32),
                   jax.ShapeDtypeStruct((NEAR, 2, 2, 256, 128), F32), jax.ShapeDtypeStruct((2, 2, 256, 128), F32)),
        in_specs=[S, S, A, A, V, V], out_specs=(V, V, V, V),
        scratch_shapes=[pltpu.VMEM((2, 6, 512, 128), F32), pltpu.VMEM((16, 2, 256, 128), F32), D((16, 2)),
                        D((4,)), D, D((2, 4)), D((2, 4)), D((2,)), D((2,)), D((2, 2)), D((2, 2))] + buffers() * 2,
        cost_estimate=pl.CostEstimate(flops=2 * 10**10, bytes_accessed=2 * 10**7, transcendentals=0),
        compiler_params=pltpu.CompilerParams(collective_id=1, has_side_effects=True, vmem_limit_bytes=26 * 2**20),
    )(offs, count, tile, meas, ill, mats)


def partners(b):
    core = b % 2
    x = (b // 2) % 4
    zlo = b // 8
    return core, x, zlo


def finish_kernel(spec, ill, grad, pterm, newspec, newill,
                  rxc, rxm, rz, edge, rcore, rx, sumc, part, rc, total,
                  core_s, core_r, xs, xr, cs, cr, ms, mr, zs, zr,
                  us, ur, ds, dr, es, er, fs, fr):
    a, b, has, ids = neighbours()
    core, x, zlo = partners(b)
    low = x * 2 + core
    unit = zlo * 16 + a

    def member(d):
        u = (unit + d) % 32
        return (u % 16, (u // 16) * 8 + low)

    mates = [(a, zlo * 8 + ((x + d) % 4) * 2 + core) for d in (1, 2, 3)]
    other = (a, zlo * 8 + x * 2 + (1 - core))
    barrier, expected = greet([(None, m) for m in mates] + [(None, other)]
                              + [(jnp.logical_and(core == 0, has["left"]), ids["left"]),
                                 (jnp.logical_and(core == 1, has["right"]), ids["right"])])

    @pl.loop(1, 32)
    def _(d):
        pl.semaphore_signal(barrier, inc=1, device_id=member(d), device_id_type=MESH)

    power = jnp.sum(ill[0] * ill[0] + ill[1] * ill[1]) * (1.0 / 65536) + 1e-05
    inv = 1.0 / power
    pl.semaphore_wait(barrier, expected + 31)
    first = remote(pterm.at[1 - core], rcore, core_s, core_r, other)
    corner, middle, vert = {}, {}, {}
    for i, side in enumerate(("right", "left")):
        src_t = 5 if side == "right" else 0
        for j, row in enumerate((0, 640)):
            corner[side, j] = remote(grad.at[:, src_t, pl.ds(row, 128), :], rxc.at[i, j],
                                     cs.at[i, j], cr.at[i, j], ids[side])
        middle[side] = remote(grad.at[:, src_t, pl.ds(128, 512), :], rxm.at[i], ms.at[i], mr.at[i], ids[side])
    for j, way in enumerate(("up", "down")):
        row = 0 if way == "up" else 640
        for t in range(4):
            src = edge.at[j, t // 3] if t in (0, 3) else grad.at[:, 1 + t, pl.ds(row, 128), :]
            vert[way, t] = remote(src, rz.at[j, :, t], zs.at[j, t], zr.at[j, t], ids[way])

    outer = jnp.logical_or(x == 0, x == 3)
    inner = jnp.logical_not(outer)
    crossing = {"right": b == 7, "left": b == 8}

    def send_vert(t, mine):
        for way in ("up", "down"):
            pl.when(jnp.logical_and(has[way], mine))(vert[way, t].start)

    def add_vert(t):
        for j, (way, row) in enumerate((("up", 384), ("down", 0))):
            @pl.when(has[OPPOSITE[way]])
            def _(j=j, way=way, row=row):
                vert[way, t].wait_recv()
                newspec[:, row:row + 128, 128 * t:128 * t + 128] += inv * rz[j, :, t]

    first.start()
    for side in ("right", "left"):
        pl.when(crossing[side])(middle[side].start)
    send_vert(1, inner)
    first.wait_recv()
    sumc[...] = pterm[core] + rcore[...]
    xsend = [remote(sumc.at[(x + d) % 4], rx.at[d - 1], xs.at[d - 1], xr.at[d - 1], mates[d - 1]) for d in (1, 2, 3)]
    for copy in xsend:
        copy.start()
    for side in ("right", "left"):
        for j in range(2):
            pl.when(has[side])(corner[side, j].start)
    for copy in xsend:
        copy.wait_recv()
    part[...] = sumc[x] + rx[0] + rx[1] + rx[2]

    @pl.loop(1, 32)
    def _(d):
        device = member(d)
        remote(part.at[device[0]], rc.at[d - 1], us, ur, device).start()

    send_vert(1, outer)
    send_vert(2, inner)
    for side in ("right", "left"):
        pl.when(jnp.logical_and(has[side], jnp.logical_not(crossing[side])))(middle[side].start)

    @pl.loop(0, 16)
    def _(i):
        rows = pl.ds(pl.multiple_of(32 * i, 32), 32)
        more = pl.ds(pl.multiple_of(32 * i + 128, 32), 32)
        for p in range(2):
            for t in range(4):
                lanes = pl.ds(128 * t, 128)
                newspec[p, rows, lanes] = spec[p, rows, lanes] + inv * grad[p, 1 + t, more, :]

    for j, row in enumerate((0, 640)):
        for k, (t, side) in enumerate(((1, "right"), (4, "left"))):
            edge[j, k] = grad[:, t, row:row + 128, :]
            @pl.when(has[OPPOSITE[side]])
            def _(j=j, k=k, side=side):
                corner[side, j].wait_recv()
                edge[j, k] += rxc[k, j]
    whole = remote(rc, rc, us, ur, other)
    whole.wait_recv()
    acc = part[a]
    for i in range(31):
        acc = acc + rc[i]
    total[core, x, a] = acc

    @pl.loop(1, 16)
    def _(d):
        remote(total.at[core, x, a], total.at[core, x, a], ds, dr, ((a + d) % 16, b)).start()

    send_vert(2, outer)
    send_vert(0, has["up"] | has["down"])
    send_vert(3, has["up"] | has["down"])
    for k, (side, t) in enumerate((("right", 0), ("left", 3))):
        @pl.when(has[OPPOSITE[side]])
        def _(k=k, side=side, t=t):
            middle[side].wait_recv()
            newspec[:, :, 128 * t:128 * t + 128] += inv * rxm[k]
    some = remote(rc.at[pl.ds(0, 15)], rc.at[pl.ds(0, 15)], ds, dr, other)
    some.wait_recv()
    gather = [remote(total.at[core, x], total.at[core, x], es.at[d - 1], er.at[d - 1], mates[d - 1]) for d in (1, 2, 3)]
    for copy in gather:
        copy.start()
    add_vert(1)
    add_vert(2)
    for copy in gather:
        copy.wait_recv()
    last = remote(total.at[core], total.at[core], fs, fr, other)
    last.start()
    last.wait()
    for p in range(2):
        for s in range(4):
            rows, lanes = pl.ds((s % 2) * 128, 128), pl.ds((s // 2) * 128, 128)
            newill[p, rows, lanes] = ill[p, rows, lanes] + total[p, s].reshape(128, 128) * (1.0 / 64)
    add_vert(0)
    add_vert(3)
    first.wait_send()
    for copy in xsend + gather:
        copy.wait_send()
    whole.wait_send()
    some.wait_send()
    for side in ("right", "left"):
        for j in range(2):
            pl.when(has[side])(corner[side, j].wait_send)
        pl.when(has[side])(middle[side].wait_send)
    for way in ("up", "down"):
        for t in range(4):
            pl.when(has[way])(vert[way, t].wait_send)


def finish(spec, ill, grad, pterm):
    D = pltpu.SemaphoreType.DMA
    V = pl.BlockSpec(memory_space=pltpu.VMEM)
    return pl.pallas_call(
        finish_kernel,
        out_shape=(jax.ShapeDtypeStruct((2, 512, 512), F32), jax.ShapeDtypeStruct((2, 256, 256), F32)),
        in_specs=[V, V, V, V], out_specs=(V, V),
        scratch_shapes=[
            pltpu.VMEM((2, 2, 2, 128, 128), F32), pltpu.VMEM((2, 2, 512, 128), F32),
            pltpu.VMEM((2, 2, 4, 128, 128), F32), pltpu.VMEM((2, 2, 2, 128, 128), F32),
            pltpu.VMEM((4, 16, 8, 128), F32), pltpu.VMEM((3, 16, 8, 128), F32), pltpu.VMEM((4, 16, 8, 128), F32),
            pltpu.VMEM((16, 8, 128), F32), pltpu.VMEM((31, 8, 128), F32), pltpu.VMEM((2, 4, 16, 8, 128), F32),
            D, D, D((3,)), D((3,)), D((2, 2)), D((2, 2)), D((2,)), D((2,)), D((2, 4)), D((2, 4)),
            D, D, D, D, D((3,)), D((3,)), D, D,
        ],
        compiler_params=pltpu.CompilerParams(collective_id=2, has_side_effects=True, vmem_limit_bytes=32 * 2**20),
    )(spec, ill, grad, pterm)


def shards(specimen, illumination, scan_offsets, slot_counts, measured):
    anchor = jnp.stack([lax.axis_index("ty") * 512, lax.axis_index("tx") * 512]) - 128
    local = scan_offsets[0, 0] - anchor[:, None]
    count = slot_counts[0]
    mats = jnp.asarray(consts())
    ext, moduli, near, near_term = halo(local, count, specimen, measured[0, 0], illumination, mats)
    grad, probe_term = windows(local, count, ext, illumination, mats, moduli, near, near_term)
    return finish(specimen, illumination, grad, probe_term.reshape(2, 4, 16, 8, 128))


def solution(mesh):
    in_specs = (
        P(None, "ty", "tx"),
        P(),
        P("ty", "tx", None, None),
        P("ty", "tx"),
        P("ty", "tx", None, None, None),
    )
    out_specs = (P(None, "ty", "tx"), P())
    return jax.shard_map(shards, mesh=mesh, in_specs=in_specs, out_specs=out_specs, check_vma=False)
```
